256 devices in a mesh: rep: 32 (over z, y_lo, core), fsdp: 8 (over y_hi, x).
Axes of the slice: x: 4, y: 4 (y_hi: 2, y_lo: 2; y = y_hi * 2 + y_lo), z: 8, core: 2. Of those that a mesh axis runs over, the one named last changes fastest.
Arguments:
- tokens: bfloat16 [32768, 1536], P(('rep', 'fsdp')), may hold values from -6 to 6
- segment_ids: int32 [32768], P('rep'), may hold values from 0 to 3, as said below
- routes: int32 [32768, 6], P(('rep', 'fsdp')), may hold values from 0 to 7, all different within a row
- gain_attn: bfloat16 [1536], P('fsdp'), may hold values from 0.099609375 to 1.8984375
- w_query: bfloat16 [1536, 1536], P('fsdp'), may hold values from -0.3125 to 0.3125
- w_key: bfloat16 [1536, 512], P('fsdp'), may hold values from -0.15625 to 0.15625
- w_value: bfloat16 [1536, 512], P('fsdp'), may hold values from -0.15625 to 0.15625
- w_out: bfloat16 [1536, 1536], P('fsdp'), may hold values from -0.625 to 0.625
- gain_ffn: bfloat16 [1536], P('fsdp'), may hold values from 0.099609375 to 1.8984375
- w_router: bfloat16 [1536, 8], P('fsdp'), may hold values from -0.078125 to 0.078125
- w_shared_in: bfloat16 [1536, 2048], P('fsdp'), may hold values from -0.15625 to 0.15625
- w_shared_out: bfloat16 [1024, 1536], P('fsdp'), may hold values from -0.375 to 0.375
- w_expert_in: bfloat16 [1536, 8, 1024], P('fsdp'), may hold values from -0.15625 to 0.15625
- w_expert_out: bfloat16 [8, 512, 1536], P(None, 'fsdp'), may hold values from -1 to 1
- cotangent: bfloat16 [32768, 1536], P(('rep', 'fsdp')), may hold values from -6 to 6
Outputs:
- result: bfloat16 [32768, 1536], P(('rep', 'fsdp'))
- grad_input: bfloat16 [32768, 1536], P(('rep', 'fsdp'))
- grad_gain_attn: float32 [1536], P('fsdp')
- grad_query: float32 [1536, 1536], P('fsdp')
- grad_key: float32 [1536, 512], P('fsdp')
- grad_value: float32 [1536, 512], P('fsdp')
- grad_out: float32 [1536, 1536], P('fsdp')
- grad_gain_ffn: float32 [1536], P('fsdp')
- grad_router: float32 [1536, 8], P('fsdp')
- grad_shared_in: float32 [1536, 2048], P('fsdp')
- grad_shared_out: float32 [1024, 1536], P('fsdp')
- grad_expert_in: float32 [1536, 8, 1024], P('fsdp')
- grad_expert_out: float32 [8, 512, 1536], P(None, 'fsdp')
The draws below stay inside these ranges and needn't reach their ends.
Inputs may be any that keep to these rules, and one draw needn't show every extreme that they name: `segment_ids`: within each sequence of 1024 tokens, documents 1, 2, 3 follow one another and padding 0 closes the sequence; document 2 begins on the sequence's first device and ends on its last. `routes`: 6 different experts for each token.
All inputs are finite; a program needn't handle non-finite values.
Results may differ from the reference program's by a relative error of at most 0.03.
Values may be sent and summed in bfloat16 or wider, within the bound.
No kernel may reach another device: no remote copies, remote signals or barrier semaphores. Data moves between devices by JAX's collectives and lax.ppermute only.
A program may use at most 256 MiB of HBM per device.

```python
import jax
import jax.numpy as jnp
from jax import lax

D = 1536
HEADS = 12
KV_HEADS = 4
HEAD = 128
FE = 512
FS = 1024
TOP = 6
EXPERTS = 8
TOK_DEV = 128
SEQ = 1024
TOKENS = 32768


def draw_segment_ids(key, part):
    groups = TOKENS // SEQ
    first_key, second_key, third_key = jax.random.split(key, 3)
    upper = max(2, TOK_DEV // 2)
    head_len = jax.random.randint(first_key, (groups, 1), 1, upper)
    pad_len = jax.random.randint(second_key, (groups, 1), 1, upper)
    tail_len = jax.random.randint(third_key, (groups, 1), 1, upper)
    pos = jnp.arange(SEQ, dtype=jnp.int32)[None, :]
    ident = jnp.where(pos < head_len, 1, jnp.where(pos < SEQ - pad_len - tail_len, 2, jnp.where(pos < SEQ - pad_len, 3, 0)))
    return ident.astype(jnp.int32).reshape(TOKENS)


def level_of(stream_key, dims, pieces, low, top_value):
    factor_of, own = 1.0, jax.random.fold_in(stream_key, 6)
    for position, blocks in pieces:
        draws = jnp.exp(jax.random.uniform(jax.random.fold_in(own, position), (blocks,), jnp.float32, low / len(pieces), top_value / len(pieces)))
        factor_of = factor_of * jnp.repeat(draws, dims[position] // blocks).reshape([-1 if axis == position else 1 for axis in range(len(dims))])
    return factor_of


def choose_distinct(own_key, rows, amount, top, lift):
    sequence = jax.random.permutation(jax.random.fold_in(own_key, 1), amount)
    boost = sequence
    for power in range(3):
        boost = boost * boost // amount
    boost = boost * lift // amount
    tickets = jax.random.randint(jax.random.fold_in(own_key, 2), (rows, amount), 0, 4096) + boost
    fixed_rows = jax.random.permutation(jax.random.fold_in(own_key, 3), rows)[jnp.arange(amount) % rows]
    tickets = jnp.where(jnp.arange(rows)[:, None] == fixed_rows[None, :], 1 << 14, tickets)
    merit = tickets * amount + jnp.arange(amount)
    return lax.top_k(merit.astype(jnp.int32), top)[1].astype(jnp.int32)


def bell_draw(rng, extent, scale, bound, cuts=(), kind=jnp.bfloat16):
    entries = scale * jax.random.normal(rng, extent, jnp.float32)
    if cuts:
        entries = entries * level_of(rng, extent, cuts, -0.22, 0.18)
    return jnp.clip(entries, -bound, bound).astype(kind)


def setup_inputs(seed: int = 0) -> dict:
    key_of = jax.random.split(jax.random.key(seed), 16)
    return {
        "tokens": bell_draw(key_of[0], (TOKENS, D), 1.0, 6.0, ((0, 256),)),
        "segment_ids": draw_segment_ids(jax.random.fold_in(key_of[15], 71), 0),
        "routes": choose_distinct(key_of[2], TOKENS, EXPERTS, TOP, 6144),
        "gain_attn": jnp.clip(1.0 + 0.18 * jax.random.normal(key_of[3], (D,), jnp.float32), 0.099609375, 1.8984375).astype(jnp.bfloat16),
        "w_query": bell_draw(key_of[4], (D, HEADS * HEAD), (D // 4) ** -0.5, 0.3125, ((0, 8),)),
        "w_key": bell_draw(key_of[5], (D, KV_HEADS * HEAD), D ** -0.5, 0.15625, ((0, 8),)),
        "w_value": bell_draw(key_of[6], (D, KV_HEADS * HEAD), D ** -0.5, 0.15625, ((0, 8),)),
        "w_out": bell_draw(key_of[7], (HEADS * HEAD, D), (HEADS * HEAD // 16) ** -0.5, 0.625, ((0, 8),)),
        "gain_ffn": jnp.clip(1.0 + 0.18 * jax.random.normal(key_of[8], (D,), jnp.float32), 0.099609375, 1.8984375).astype(jnp.bfloat16),
        "w_router": bell_draw(key_of[9], (D, EXPERTS), (4 * D) ** -0.5, 0.078125, ((0, 8),)),
        "w_shared_in": bell_draw(key_of[10], (D, 2 * FS), D ** -0.5, 0.15625, ((0, 8),)),
        "w_shared_out": bell_draw(key_of[11], (FS, D), (FS // 4) ** -0.5, 0.375, ((0, 8),)),
        "w_expert_in": bell_draw(key_of[12], (D, EXPERTS, 2 * FE), D ** -0.5, 0.15625, ((0, 8),)),
        "w_expert_out": bell_draw(key_of[13], (EXPERTS, FE, D), (FE // 16) ** -0.5, 1.0, ((1, 8),)),
        "cotangent": bell_draw(key_of[14], (TOKENS, D), 1.0, 6.0, ((0, 256),)),
    }


@jax.custom_vjp
def low(v):
    return lax.optimization_barrier(v.astype(jnp.bfloat16)).astype(jnp.float32)

@jax.custom_vjp
def low_back(v):
    return v

def low_keep(v):
    return (low(v), None)

def low_pass(kept, grad):
    return (grad,)

def back_keep(v):
    return (v, None)

def back_low(kept, grad):
    return (low(grad),)
low.defvjp(low_keep, low_pass)
low_back.defvjp(back_keep, back_low)

def highest_dot(left, right):
    return jnp.dot(left, right, precision=lax.Precision.HIGHEST)

def normalize(values):
    return values * lax.rsqrt(lax.optimization_barrier(jnp.mean(values * values, axis=-1, keepdims=True)) + 1e-05)

def attend(query, keys, values, seg):
    pos = jnp.arange(SEQ, dtype=jnp.int32)
    allowed = (pos[:, None] == pos[None, :]) | (pos[None, :] < pos[:, None]) & (seg[:, None] == seg[None, :]) & (seg[None, :] != 0)
    query_heads = query.reshape(SEQ, KV_HEADS, HEADS // KV_HEADS, HEAD)
    key_heads = keys.reshape(SEQ, KV_HEADS, HEAD)
    value_heads = values.reshape(SEQ, KV_HEADS, HEAD)
    scores = jnp.einsum('tkgd,skd->kgts', query_heads, key_heads, precision=lax.Precision.HIGHEST) * (1.0 / jnp.sqrt(jnp.float32(HEAD)))
    scores = low_back(scores)
    scores = jnp.where(allowed[None, None], scores, -1e+30)
    top_score = lax.optimization_barrier(jnp.max(scores, axis=-1, keepdims=True))
    expo = jnp.exp(scores - top_score)
    probs = low(expo / lax.optimization_barrier(jnp.sum(expo, axis=-1, keepdims=True)))
    mixed = jnp.einsum('kgts,skd->tkgd', probs, value_heads, precision=lax.Precision.HIGHEST)
    return mixed.reshape(SEQ, HEADS * HEAD)

def layer(params, inputs, seg, route_rows):
    gain_one, w_query, w_key, w_value, w_out, gain_two, w_router, w_shared_in, w_shared_out, w_expert_in, w_expert_out = params
    normed_one = low(normalize(inputs) * gain_one)
    query = low(low_back(highest_dot(normed_one, w_query)))
    keys = low(low_back(highest_dot(normed_one, w_key)))
    values = low(low_back(highest_dot(normed_one, w_value)))
    attended = low(low_back(jax.checkpoint(attend)(query, keys, values, seg)))
    hidden = inputs + low_back(highest_dot(attended, w_out))
    normed_two = low(normalize(hidden) * gain_two)
    logits = low_back(highest_dot(normed_two, w_router))
    chosen = lax.optimization_barrier(jnp.sum((route_rows[:, :, None] == jnp.arange(EXPERTS, dtype=jnp.int32)[None, None, :]).astype(jnp.float32), axis=1))
    weighted = chosen * jnp.exp(logits)
    gates = weighted / lax.optimization_barrier(jnp.sum(weighted, axis=-1, keepdims=True))
    expert_pre = low_back(jnp.einsum('td,def->tef', normed_two, w_expert_in, precision=lax.Precision.HIGHEST))
    gate_part = expert_pre[:, :, :FE]
    up_part = expert_pre[:, :, FE:]
    mixed = low(gates[:, :, None] * (gate_part * jax.nn.sigmoid(gate_part) * up_part))
    routed = jnp.einsum('tef,efd->td', mixed, w_expert_out, precision=lax.Precision.HIGHEST)
    shared_pre = low_back(highest_dot(normed_two, w_shared_in))
    shared_gate = shared_pre[:, :FS]
    shared_act = low(shared_gate * jax.nn.sigmoid(shared_gate) * shared_pre[:, FS:])
    return hidden + routed + highest_dot(shared_act, w_shared_out)

def reference(tokens, segment_ids, routes, gain_attn, w_query, w_key, w_value, w_out, gain_ffn, w_router, w_shared_in, w_shared_out, w_expert_in, w_expert_out, cotangent):
    params = tuple((item.astype(jnp.float32) for item in (gain_attn, w_query, w_key, w_value, w_out, gain_ffn, w_router, w_shared_in, w_shared_out, w_expert_in, w_expert_out)))
    groups = TOKENS // SEQ
    inputs = tokens.astype(jnp.float32).reshape(groups, SEQ, D)
    seg_rows = segment_ids.reshape(groups, SEQ)
    route_rows = routes.reshape(groups, SEQ, TOP)
    grads_in = cotangent.astype(jnp.float32).reshape(groups, SEQ, D)

    def step(acc, item):
        seq_in, seq_seg, seq_route, seq_grad = item
        outputs, pull = jax.vjp(lambda weights, values: layer(weights, values, seq_seg, seq_route), params, seq_in)
        weight_grads, input_grad = pull(seq_grad)
        acc = jax.tree.map(lambda total, part: total + part, acc, weight_grads)
        return (acc, (outputs.astype(jnp.bfloat16), input_grad.astype(jnp.bfloat16)))
    zeros = jax.tree.map(jnp.zeros_like, params)
    acc, (outputs, input_grads) = lax.scan(step, zeros, (inputs, seg_rows, route_rows, grads_in))
    return (outputs.reshape(TOKENS, D), input_grads.reshape(TOKENS, D), acc[0], acc[1], acc[2], acc[3], acc[4], acc[5], acc[6], acc[7], acc[8], acc[9], acc[10])
```

```python
import math

import jax
import jax.numpy as jnp
from jax import lax
from jax.sharding import Mesh, PartitionSpec as P

HEADS = 12
KV_HEADS = 4
HEAD = 128
GROUP = HEADS // KV_HEADS
D = 1536
FE = 512
FS = 1024
EXPERTS = 8
EPS = 1e-05
SCALE = 1.0 / math.sqrt(HEAD)

AXES = ("z", "ylo", "core", "yhi", "x")
SIZES = (8, 2, 2, 2, 4)
REP = ("z", "ylo", "core")
FSDP = ("yhi", "x")
PLANE = ("ylo", "yhi", "x")
BF = jnp.bfloat16
F32 = jnp.float32


def dot(left, right):
    return jnp.dot(left, right, preferred_element_type=F32)


def dot_rows(left, right):
    return lax.dot_general(left, right, (((1,), (1,)), ((), ())), preferred_element_type=F32)


def dot_cols(left, right):
    return lax.dot_general(left, right, (((0,), (0,)), ((), ())), preferred_element_type=F32)


def exchange(blocks, axes):
    return lax.all_to_all(blocks, axes, 0, 0, tiled=True)


def spread_x(rows):
    got = exchange(jnp.broadcast_to(rows[None], (4, *rows.shape)), "x")
    return got.reshape(4 * rows.shape[0], *rows.shape[1:])


def collect_x(rows):
    got = exchange(rows.reshape(4, rows.shape[0] // 4, *rows.shape[1:]), "x")
    return jnp.sum(got.astype(F32), axis=0)


def swap_core(rows):
    return lax.ppermute(rows, "core", [(0, 1), (1, 0)])


def pair_of_float(values):
    high = values.astype(BF)
    return high, (values - high.astype(F32)).astype(BF)


def normalize(values):
    factor = lax.rsqrt(jnp.mean(values * values, axis=-1, keepdims=True) + EPS)
    return values * factor, factor


def norm_back(grad_normed, unit, factor, gain):
    scaled = grad_normed * gain
    inner = jnp.mean(scaled * unit, axis=-1, keepdims=True)
    return factor * (scaled - unit * inner)


def silu_slope(values, sig):
    return sig * (1.0 + values * (1.0 - sig))


def shards(
    tokens,
    segment_ids,
    routes,
    gain_attn,
    w_query,
    w_key,
    w_value,
    w_out,
    gain_ffn,
    w_router,
    w_shared_in,
    w_shared_out,
    w_expert_in,
    w_expert_out,
    cotangent,
):
    core, half, place = (lax.axis_index(a) for a in ("core", "yhi", "x"))
    rows = tokens.shape[0]
    own = w_query.shape[0]

    slots = jnp.concatenate(
        [
            w_query.reshape(own, 4, GROUP * HEAD),
            w_key.reshape(own, 4, HEAD),
            w_value.reshape(own, 4, HEAD),
        ],
        axis=2,
    ).transpose(1, 0, 2)
    small = jnp.concatenate([gain_attn, gain_ffn, w_router.T.reshape(-1)]).reshape(3, 640)
    small = jnp.pad(small, ((0, 13), (0, 0)))
    slots = jnp.concatenate([slots, jnp.broadcast_to(small[None], (4, 16, 640))], axis=1)
    got = exchange(jnp.concatenate([slots, slots], axis=0), FSDP)
    w_qkv = got[:, :own].reshape(D, 640)
    small = got[:, own : own + 3].reshape(8, 1920)
    gain_one = small[:, :192].reshape(1, D).astype(F32)
    gain_two = small[:, 192:384].reshape(1, D).astype(F32)
    router = small[:, 384:].reshape(8, EXPERTS, 192).transpose(1, 0, 2).reshape(EXPERTS, D)

    all_tokens = spread_x(tokens)

    out_a = lax.ppermute(w_out, FSDP, [(b, (b % 2) * 4 + b // 2) for b in range(8)])
    out_b = lax.ppermute(w_out, FSDP, [(b, (1 - b % 2) * 4 + b // 2) for b in range(8)])
    w_o = jnp.concatenate(
        [jnp.where(half == 0, out_a, out_b), jnp.where(half == 0, out_b, out_a)], axis=0
    )

    of_core = lax.dynamic_index_in_dim(w_expert_in.reshape(own, 2, 4, 2 * FE), core, 1, False)
    of_shared = lax.dynamic_index_in_dim(w_shared_in.reshape(own, 2, 2, 4, 128), core, 2, False)
    of_shared = of_shared.transpose(2, 0, 1, 3).reshape(4, own, 256)
    slots = jnp.concatenate([of_core.transpose(1, 0, 2), of_shared], axis=2)
    w_in = exchange(jnp.concatenate([slots, slots], axis=0), FSDP).reshape(D, 1280)
    slots = lax.dynamic_index_in_dim(w_expert_out.reshape(2, 4, 64, D), core, 0, False)
    w_down = exchange(jnp.concatenate([slots, slots], axis=0), FSDP).reshape(FE, D)
    other = lax.ppermute(w_shared_out, ("core", "yhi"), [(0, 1), (3, 2)])
    w_down = jnp.concatenate([w_down, jnp.where(core == half, w_shared_out, other)], axis=0)

    grad_own = spread_x(cotangent)
    grad_all = jnp.concatenate([grad_own, swap_core(grad_own)], axis=0)

    inputs = tokens.astype(F32)
    unit_one, factor_one = normalize(all_tokens.astype(F32))
    normed_one = (unit_one * gain_one).astype(BF)
    qkv = dot(normed_one, w_qkv).astype(BF)
    kv_own = qkv[:, GROUP * HEAD :]
    kv_other = lax.ppermute(kv_own, "yhi", [(0, 1)])
    kv = jnp.concatenate([kv_own, kv_other], axis=0)
    keys, values = kv[:, :HEAD], kv[:, HEAD:]
    queries = qkv[:, : GROUP * HEAD].reshape(512, GROUP, HEAD).transpose(1, 0, 2)
    seg_own = lax.dynamic_slice_in_dim(segment_ids, half * 512, 512)
    seg_other = segment_ids[:512]
    pos = jnp.arange(512, dtype=jnp.int32)
    allowed_own = (pos[:, None] == pos[None, :]) | (pos[None, :] < pos[:, None]) & (
        seg_own[:, None] == seg_own[None, :]
    ) & (seg_own[None, :] != 0)
    allowed_other = (
        (seg_own[:, None] == seg_other[None, :]) & (seg_other[None, :] != 0) & (half == 1)
    )
    allowed = jnp.concatenate([allowed_own, allowed_other], axis=1)

    def scores_of():
        raw = jnp.einsum("gtd,sd->gts", queries, keys, preferred_element_type=F32) * SCALE
        return jnp.where(allowed[None], raw, -1e30)

    scores = scores_of()
    top_score = jnp.max(scores, axis=-1, keepdims=True)
    expo = jnp.exp(scores - top_score)
    total = jnp.sum(expo, axis=-1, keepdims=True)
    log_total = top_score + jnp.log(total)
    probs = (expo / total).astype(BF)
    attended = jnp.einsum("gts,sd->tgd", probs, values, preferred_element_type=F32)
    attended = attended.reshape(512, GROUP * HEAD).astype(BF)
    hidden = inputs + collect_x(dot(attended, w_o).astype(BF))

    unit_two, factor_two = normalize(hidden)
    normed_two = (unit_two * gain_two).astype(BF)
    logits = dot_rows(normed_two, router)
    chosen = jnp.sum(
        (routes[:, :, None] == jnp.arange(EXPERTS, dtype=jnp.int32)[None, None, :]).astype(F32),
        axis=1,
    )
    weighted = chosen * jnp.exp(logits)
    gates = weighted / jnp.sum(weighted, axis=-1, keepdims=True)
    packed = jnp.concatenate(
        [normed_two, *pair_of_float(gates), jnp.zeros((rows, 112), BF)], axis=1
    )
    packed = spread_x(packed)
    packed = jnp.concatenate([packed, swap_core(packed)], axis=0)
    normed_all = packed[:, :D]
    expert = core * 4 + place
    mine = (jnp.arange(EXPERTS, dtype=jnp.int32) == expert).astype(F32)[None]
    gates_all = packed[:, D : D + 8].astype(F32) + packed[:, D + 8 : D + 16].astype(F32)
    gate = jnp.sum(gates_all * mine, axis=1, keepdims=True)

    pre = dot(normed_all, w_in)
    gate_part, up_part = pre[:, :FE], pre[:, FE : 2 * FE]
    shared_gate, shared_up = pre[:, 2 * FE : 2 * FE + 128], pre[:, 2 * FE + 128 :]
    gate_sig = jax.nn.sigmoid(gate_part)
    activ = gate_part * gate_sig * up_part
    shared_sig = jax.nn.sigmoid(shared_gate)
    mixed = jnp.concatenate(
        [(gate * activ).astype(BF), (shared_gate * shared_sig * shared_up).astype(BF)], axis=1
    )
    back = dot_rows(grad_all, w_down)
    grad_mixed, grad_shared = back[:, :FE], back[:, FE:]
    grad_gate = jnp.sum(grad_mixed * activ, axis=1, keepdims=True)
    grad_activ = grad_mixed * gate
    grad_pre = jnp.concatenate(
        [
            (grad_activ * up_part * silu_slope(gate_part, gate_sig)).astype(BF),
            (grad_activ * gate_part * gate_sig).astype(BF),
            (grad_shared * shared_up * silu_slope(shared_gate, shared_sig)).astype(BF),
            (grad_shared * shared_gate * shared_sig).astype(BF),
        ],
        axis=1,
    )
    back_part = dot_rows(grad_pre, w_in).astype(BF)
    back_part = jnp.concatenate(
        [back_part, *pair_of_float(grad_gate * mine), jnp.zeros((1024, 112), BF)], axis=1
    )
    back_part = back_part[:512].astype(F32) + swap_core(back_part[512:]).astype(F32)
    back_sum = collect_x(back_part.astype(BF))

    result_part = dot(mixed, w_down).astype(BF)
    result_part = result_part[:512].astype(F32) + swap_core(result_part[512:]).astype(F32)
    result = (hidden + collect_x(result_part.astype(BF))).astype(BF)

    grad_in = dot_cols(normed_all, grad_pre).astype(BF)
    grad_down = dot_cols(mixed, grad_all).astype(BF)

    main = jnp.concatenate(
        [
            grad_in.reshape(8, 192, 10, 128).transpose(0, 2, 1, 3).reshape(8, 1920, 128),
            grad_down[:FE].reshape(8, 64, 12, 128).transpose(0, 2, 1, 3).reshape(8, 768, 128),
        ],
        axis=1,
    )
    main = main.reshape(8, 8, 2, 168, 128).transpose(1, 2, 0, 3, 4).reshape(8, 2, 1344, 128)
    side = grad_down[FE:].reshape(128, 12, 128).transpose(1, 0, 2).reshape(8, 2, 96, 128)
    flat = jnp.concatenate([main, side], axis=2)
    flat = lax.psum_scatter(flat, "z", scatter_dimension=0, tiled=True)[0]
    main = exchange(flat[:, :1344].reshape(16, 168, 128), PLANE).reshape(4, 4, 168, 128)
    main = jnp.sum(main.astype(F32), axis=0).astype(BF).reshape(672, 128)
    to = (jnp.arange(2) == core)[None, :, None, None]
    side = jnp.where(to, flat[:, None, 1344:], 0).reshape(4, 96, 128)
    side = jnp.sum(exchange(side, ("ylo", "yhi")).astype(F32), axis=0).astype(BF)
    whole = lax.all_gather(jnp.concatenate([main, side], axis=0), REP)
    main = whole[:, :672].reshape(16, 2, 4, 168, 128).transpose(1, 2, 0, 3, 4)
    main = main.reshape(8, 2688, 128)
    up = main[:, :1920].reshape(8, 10, 192, 128)
    sum_expert_in = up[:, :8].transpose(2, 0, 1, 3).reshape(192, 8, 1024).astype(F32)
    sum_shared_in = up[:, 8:].transpose(2, 1, 0, 3).reshape(192, 2048).astype(F32)
    sum_expert_out = main[:, 1920:].reshape(8, 12, 64, 128).transpose(0, 2, 1, 3)
    sum_expert_out = sum_expert_out.reshape(8, 64, D).astype(F32)
    side = whole[:, 672:].reshape(16, 2, 96, 128)
    side = lax.dynamic_index_in_dim(side, half, 1, False).reshape(12, 128, 128)
    sum_shared_out = side.transpose(1, 0, 2).reshape(128, D).astype(F32)

    grad_gates = back_sum[:, D : D + 8] + back_sum[:, D + 8 : D + 16]
    grad_logits = (
        gates * (grad_gates - jnp.sum(gates * grad_gates, axis=-1, keepdims=True))
    ).astype(BF)
    grad_normed_two = back_sum[:, :D] + dot(grad_logits, router)
    grad_router = dot_cols(grad_logits, normed_two)
    grad_gain_ffn = jnp.sum(grad_normed_two * unit_two, axis=0, keepdims=True)
    grad_hidden = cotangent.astype(F32) + norm_back(
        grad_normed_two, unit_two, factor_two, gain_two
    )
    hidden_low = spread_x(grad_hidden.astype(BF))

    grad_out = dot_cols(attended, hidden_low).astype(BF)
    grad_att = dot_rows(hidden_low, w_o).astype(BF)
    grad_heads = grad_att.reshape(512, GROUP, HEAD).transpose(1, 0, 2)
    probs_again = jnp.exp(scores_of() - log_total)
    grad_probs = jnp.einsum("gtd,sd->gts", grad_heads, values, preferred_element_type=F32)
    inner = jnp.sum(probs_again * grad_probs, axis=-1, keepdims=True)
    grad_scores = (probs_again * (grad_probs - inner)).astype(BF)
    grad_query = jnp.einsum("gts,sd->tgd", grad_scores, keys, preferred_element_type=F32) * SCALE
    grad_query = grad_query.reshape(512, GROUP * HEAD).astype(BF)
    grad_keys = jnp.einsum("gts,gtd->sd", grad_scores, queries, preferred_element_type=F32) * SCALE
    grad_values = jnp.einsum(
        "gts,gtd->sd", probs_again.astype(BF), grad_heads, preferred_element_type=F32
    )
    grad_kv = jnp.concatenate([grad_keys, grad_values], axis=1)
    from_other = lax.ppermute(grad_kv[512:].astype(BF), "yhi", [(1, 0)])
    grad_kv = (grad_kv[:512] + from_other.astype(F32)).astype(BF)
    grad_qkv = jnp.concatenate([grad_query, grad_kv], axis=1)
    grad_normed_one = dot_rows(grad_qkv, w_qkv)
    grad_gain_attn = jnp.sum(grad_normed_one * unit_one, axis=0, keepdims=True)
    grad_weights = dot_cols(normed_one, grad_qkv).astype(BF)

    small = jnp.concatenate([grad_router, grad_gain_ffn, grad_gain_attn], axis=0).astype(BF)
    small = small.reshape(10, 8, 192).transpose(1, 0, 2).reshape(8, 15, 128)
    small = jnp.pad(small, ((0, 0), (0, 49), (0, 0)))
    cols = grad_weights.reshape(8, 192, 5, 128).transpose(0, 2, 1, 3).reshape(8, 960, 128)
    cols = jnp.concatenate([cols, small], axis=1).reshape(8, 16, 2, 32, 128)
    cols = cols.transpose(2, 1, 0, 3, 4).reshape(2, 16, 256, 128)
    outs = grad_out.reshape(2, 192, 12, 128).transpose(0, 2, 1, 3).reshape(2, 16, 2, 72, 128)
    outs = outs.transpose(2, 1, 0, 3, 4).reshape(2, 16, 144, 128)
    flat = jnp.concatenate([cols, outs], axis=2)
    keep = lax.dynamic_index_in_dim(flat, core, 0, False)
    give = lax.dynamic_index_in_dim(flat, 1 - core, 0, False)
    flat = (keep.astype(F32) + swap_core(give).astype(F32)).astype(BF).reshape(8, 2, 400, 128)
    flat = lax.psum_scatter(flat, "z", scatter_dimension=0, tiled=True)[0]
    outs = lax.dynamic_update_slice(
        jnp.zeros((2, 8, 72, 128), BF), flat[:, 256:].reshape(2, 2, 72, 128), (0, 2 * place, 0, 0)
    )
    flat = jnp.concatenate([flat[:, :256].reshape(2, 8, 32, 128), outs], axis=2)
    got = exchange(flat.reshape(16, 104, 128), PLANE).reshape(4, 4, 104, 128)
    got = jnp.sum(got.astype(F32), axis=0)
    outs = jnp.sum(got[:, 32:], axis=0)
    whole = lax.all_gather(
        jnp.concatenate([got[:, :32].reshape(128, 128), outs], axis=0).astype(BF), REP
    )
    cols = whole[:, :128].reshape(32, 4, 32, 128).transpose(1, 0, 2, 3).reshape(4, 1024, 128)
    big = cols[:, :960].reshape(4, 5, 192, 128)
    sum_query = big[:, :3].transpose(2, 0, 1, 3).reshape(192, D).astype(F32)
    sum_key = big[:, 3].transpose(1, 0, 2).reshape(192, 512).astype(F32)
    sum_value = big[:, 4].transpose(1, 0, 2).reshape(192, 512).astype(F32)
    small = jnp.sum(cols[:, 960:975].astype(F32), axis=0).reshape(10, 192)
    sum_out = whole[:, 128:].reshape(12, 192, 128).transpose(1, 0, 2).reshape(192, D).astype(F32)

    back_one = collect_x(grad_normed_one.astype(BF))
    unit_own, factor_own = normalize(inputs)
    grad_input = (grad_hidden + norm_back(back_one, unit_own, factor_own, gain_one)).astype(BF)

    return (
        result,
        grad_input,
        small[9],
        sum_query,
        sum_key,
        sum_value,
        sum_out,
        small[8],
        small[:8].T,
        sum_shared_in,
        sum_shared_out,
        sum_expert_in,
        sum_expert_out,
    )


def solution(mesh):
    fine = Mesh(mesh.devices.reshape(SIZES), AXES)
    tokens = P((*REP, *FSDP), None)
    first = P(FSDP, None)
    return jax.shard_map(
        shards,
        mesh=fine,
        in_specs=(
            tokens,
            P(REP),
            tokens,
            P(FSDP),
            first,
            first,
            first,
            first,
            P(FSDP),
            first,
            first,
            first,
            P(FSDP, None, None),
            P(None, FSDP, None),
            tokens,
        ),
        out_specs=(
            tokens,
            tokens,
            P(FSDP),
            first,
            first,
            first,
            first,
            P(FSDP),
            first,
            first,
            first,
            P(FSDP, None, None),
            P(None, FSDP, None),
        ),
        check_vma=False,
    )
```

```python
import math

import jax
import jax.numpy as jnp
from jax import lax
from jax.sharding import Mesh, PartitionSpec as P

HEADS = 12
KV_HEADS = 4
HEAD = 128
GROUP = HEADS // KV_HEADS
D = 1536
FE = 512
FS = 1024
EXPERTS = 8
EPS = 1e-05
SCALE = 1.0 / math.sqrt(HEAD)

AXES = ("z", "ylo", "core", "yhi", "x")
SIZES = (8, 2, 2, 2, 4)
REP = ("z", "ylo", "core")
FSDP = ("yhi", "x")
PLANE = ("ylo", "yhi", "x")
KEY_HEAD = (0, 2, 1, 3)
BF = jnp.bfloat16
F32 = jnp.float32


def dot(left, right):
    return jnp.dot(left, right, preferred_element_type=F32)


def dot_rows(left, right):
    return lax.dot_general(left, right, (((1,), (1,)), ((), ())), preferred_element_type=F32)


def dot_cols(left, right):
    return lax.dot_general(left, right, (((0,), (0,)), ((), ())), preferred_element_type=F32)


def exchange(blocks, axes):
    return lax.all_to_all(blocks, axes, 0, 0, tiled=True)


def up_x(rows):
    return lax.ppermute(rows, "x", [(i, (i + 1) % 4) for i in range(4)])


def down_x(rows):
    return lax.ppermute(rows, "x", [(i, (i + 3) % 4) for i in range(4)])


def spread_x(rows):
    cut = rows.shape[0] // 2
    below, above = up_x(rows), down_x(rows)
    far = up_x(below[:cut]), down_x(above[cut:])
    return jnp.concatenate([rows, below, above, *far], axis=0)


def collect_x(rows):
    size = rows.shape[0] // 4
    cut = size // 2
    own, below, above, far = (rows[k * size : (k + 1) * size] for k in range(4))
    far_up, far_down = up_x(far[:cut]), down_x(far[cut:])
    above = jnp.concatenate([plus(above[:cut], far_up), above[cut:]], axis=0)
    below = jnp.concatenate([below[:cut], plus(below[cut:], far_down)], axis=0)
    return own.astype(F32) + up_x(above).astype(F32) + down_x(below).astype(F32)


def plus(left, right):
    return (left.astype(F32) + right.astype(F32)).astype(BF)


def spread_z(rows, level):
    up = [(i, (i + 1) % 8) for i in range(8)]
    down = [(i, (i + 7) % 8) for i in range(8)]
    cut = rows.shape[0] // 2
    whole = jnp.zeros((8, *rows.shape), rows.dtype)

    def put(whole, block, distance, start=0):
        return lax.dynamic_update_slice(
            whole, block[None], (lax.rem(level + distance + 8, 8), start, 0)
        )

    whole = put(whole, rows, 0)
    below = above = rows
    for k in (1, 2, 3):
        below, above = lax.ppermute(below, "z", up), lax.ppermute(above, "z", down)
        whole = put(put(whole, below, -k), above, k)
    whole = put(whole, lax.ppermute(below[:cut], "z", up), 4)
    return put(whole, lax.ppermute(above[cut:], "z", down), 4, cut)


def swap_core(rows):
    return lax.ppermute(rows, "core", [(0, 1), (1, 0)])


def pair_of_float(values):
    high = values.astype(BF)
    return high, (values - high.astype(F32)).astype(BF)


def normalize(values):
    factor = lax.rsqrt(jnp.mean(values * values, axis=-1, keepdims=True) + EPS)
    return values * factor, factor


def norm_back(grad_normed, unit, factor, gain):
    scaled = grad_normed * gain
    inner = jnp.mean(scaled * unit, axis=-1, keepdims=True)
    return factor * (scaled - unit * inner)


def silu_slope(values, sig):
    return sig * (1.0 + values * (1.0 - sig))


def shards(
    tokens,
    segment_ids,
    routes,
    gain_attn,
    w_query,
    w_key,
    w_value,
    w_out,
    gain_ffn,
    w_router,
    w_shared_in,
    w_shared_out,
    w_expert_in,
    w_expert_out,
    cotangent,
):
    core, half, place = (lax.axis_index(a) for a in ("core", "yhi", "x"))
    rows = tokens.shape[0]
    own = w_query.shape[0]

    level = lax.axis_index("z")
    member = half * 4 + place
    key_head = jnp.array(KEY_HEAD, jnp.int32)[place]

    all_tokens = spread_x(tokens)
    slots = jnp.concatenate(
        [
            w_query.reshape(own, 4, GROUP * HEAD),
            w_key.reshape(own, 4, HEAD),
            w_value.reshape(own, 4, HEAD),
        ],
        axis=2,
    )
    slots = lax.dynamic_slice_in_dim(slots, core * 96, 96, 0)
    slots = jnp.stack([slots[:, k] for k in KEY_HEAD])
    small = jnp.concatenate([gain_attn, gain_ffn, w_router.T.reshape(-1)]).reshape(3, 640)
    small = jnp.pad(small, ((0, 5), (0, 0)))
    slots = jnp.concatenate([slots, jnp.broadcast_to(small[None], (4, 8, 640))], axis=1)
    got = exchange(jnp.concatenate([slots, slots], axis=0), FSDP)
    mine, other = got[:, :96], swap_core(got[:, :96])
    w_qkv = jnp.stack(
        [jnp.where(core == 0, mine, other), jnp.where(core == 0, other, mine)], axis=1
    ).reshape(D, 640)
    small = got[:, 96:99].reshape(8, 1920)
    gain_one = small[:, :192].reshape(1, D).astype(F32)
    gain_two = small[:, 192:384].reshape(1, D).astype(F32)
    router = small[:, 384:].reshape(8, EXPERTS, 192).transpose(1, 0, 2).reshape(EXPERTS, D)

    mine = lax.ppermute(
        w_out,
        ("core", "yhi", "x"),
        [(s * 8 + b, (b % 2) * 8 + s * 4 + KEY_HEAD[b // 2]) for s in range(2) for b in range(8)],
    )
    other = swap_core(mine)
    w_o = jnp.concatenate(
        [jnp.where(core == 0, mine, other), jnp.where(core == 0, other, mine)], axis=0
    )

    target = core * 4 + (member - level + 8) % 4
    block = jnp.concatenate(
        [
            lax.dynamic_index_in_dim(w_expert_in, target, 1, False),
            lax.dynamic_slice_in_dim(w_shared_in, target * 128, 128, 1),
            lax.dynamic_slice_in_dim(w_shared_in, FS + target * 128, 128, 1),
            lax.dynamic_index_in_dim(w_expert_out, target, 0, False)
            .reshape(64, 3, 512)
            .transpose(1, 0, 2)
            .reshape(192, 512),
        ],
        axis=1,
    )
    block = lax.ppermute(
        block,
        ("z", *FSDP),
        [(z * 8 + b, z * 8 + (b - z) % 8) for z in range(8) for b in range(8)],
    )
    blocks = lax.all_gather(block, "z")
    blocks = jnp.stack(
        [lax.dynamic_index_in_dim(blocks, (b - member + 8) % 8, 0, False) for b in range(8)]
    )
    w_in = blocks[:, :, :1280].reshape(D, 1280)
    w_down = blocks[:, :, 1280:].reshape(8, 3, 64, 512).transpose(0, 2, 1, 3).reshape(FE, D)
    other = lax.ppermute(w_shared_out, ("core", "yhi"), [(0, 1), (3, 2)])
    w_down = jnp.concatenate([w_down, jnp.where(core == half, w_shared_out, other)], axis=0)

    grad_own = spread_x(cotangent)
    grad_all = jnp.concatenate([grad_own, swap_core(grad_own)], axis=0)

    inputs = tokens.astype(F32)
    unit_one, factor_one = normalize(all_tokens.astype(F32))
    normed_one = (unit_one * gain_one).astype(BF)
    qkv = dot(normed_one, w_qkv).astype(BF)
    kv_own = qkv[:, GROUP * HEAD :]
    kv_other = lax.ppermute(kv_own, "yhi", [(0, 1)])
    kv = jnp.concatenate([kv_own, kv_other], axis=0)
    keys, values = kv[:, :HEAD], kv[:, HEAD:]
    queries = qkv[:, : GROUP * HEAD].reshape(512, GROUP, HEAD).transpose(1, 0, 2)
    starts = [lax.rem(place + k, 4) * 128 for k in (0, 3, 1, 2)]
    pos = jnp.concatenate([s + jnp.arange(128, dtype=jnp.int32) for s in starts])
    seg_own = jnp.concatenate(
        [lax.dynamic_slice_in_dim(segment_ids, half * 512 + s, 128) for s in starts]
    )
    seg_other = jnp.concatenate([lax.dynamic_slice_in_dim(segment_ids, s, 128) for s in starts])
    allowed_own = (pos[:, None] == pos[None, :]) | (pos[None, :] < pos[:, None]) & (
        seg_own[:, None] == seg_own[None, :]
    ) & (seg_own[None, :] != 0)
    allowed_other = (
        (seg_own[:, None] == seg_other[None, :]) & (seg_other[None, :] != 0) & (half == 1)
    )
    allowed = jnp.concatenate([allowed_own, allowed_other], axis=1)

    def scores_of():
        raw = jnp.einsum("gtd,sd->gts", queries, keys, preferred_element_type=F32) * SCALE
        return jnp.where(allowed[None], raw, -1e30)

    scores = scores_of()
    top_score = jnp.max(scores, axis=-1, keepdims=True)
    expo = jnp.exp(scores - top_score)
    total = jnp.sum(expo, axis=-1, keepdims=True)
    log_total = top_score + jnp.log(total)
    probs = (expo / total).astype(BF)
    attended = jnp.einsum("gts,sd->tgd", probs, values, preferred_element_type=F32)
    attended = attended.reshape(512, GROUP * HEAD).astype(BF)
    hidden = inputs + collect_x(dot(attended, w_o).astype(BF))

    unit_two, factor_two = normalize(hidden)
    normed_two = (unit_two * gain_two).astype(BF)
    logits = dot_rows(normed_two, router)
    chosen = jnp.sum(
        (routes[:, :, None] == jnp.arange(EXPERTS, dtype=jnp.int32)[None, None, :]).astype(F32),
        axis=1,
    )
    weighted = chosen * jnp.exp(logits)
    gates = weighted / jnp.sum(weighted, axis=-1, keepdims=True)
    packed = jnp.concatenate(
        [normed_two, *pair_of_float(gates), jnp.zeros((rows, 112), BF)], axis=1
    )
    packed = spread_x(packed)
    packed = jnp.concatenate([packed, swap_core(packed)], axis=0)
    normed_all = packed[:, :D]
    expert = core * 4 + place
    mine = (jnp.arange(EXPERTS, dtype=jnp.int32) == expert).astype(F32)[None]
    gates_all = packed[:, D : D + 8].astype(F32) + packed[:, D + 8 : D + 16].astype(F32)
    gate = jnp.sum(gates_all * mine, axis=1, keepdims=True)

    pre = dot(normed_all, w_in)
    gate_part, up_part = pre[:, :FE], pre[:, FE : 2 * FE]
    shared_gate, shared_up = pre[:, 2 * FE : 2 * FE + 128], pre[:, 2 * FE + 128 :]
    gate_sig = jax.nn.sigmoid(gate_part)
    activ = gate_part * gate_sig * up_part
    shared_sig = jax.nn.sigmoid(shared_gate)
    mixed = jnp.concatenate(
        [(gate * activ).astype(BF), (shared_gate * shared_sig * shared_up).astype(BF)], axis=1
    )
    back = dot_rows(grad_all, w_down)
    grad_mixed, grad_shared = back[:, :FE], back[:, FE:]
    grad_gate = jnp.sum(grad_mixed * activ, axis=1, keepdims=True)
    grad_activ = grad_mixed * gate
    grad_pre = jnp.concatenate(
        [
            (grad_activ * up_part * silu_slope(gate_part, gate_sig)).astype(BF),
            (grad_activ * gate_part * gate_sig).astype(BF),
            (grad_shared * shared_up * silu_slope(shared_gate, shared_sig)).astype(BF),
            (grad_shared * shared_gate * shared_sig).astype(BF),
        ],
        axis=1,
    )
    back_part = dot_rows(grad_pre, w_in).astype(BF)
    back_part = jnp.concatenate(
        [back_part, *pair_of_float(grad_gate * mine), jnp.zeros((1024, 112), BF)], axis=1
    )
    back_part = back_part[:512].astype(F32) + swap_core(back_part[512:]).astype(F32)
    back_sum = collect_x(back_part.astype(BF))

    result_part = dot(mixed, w_down).astype(BF)
    result_part = result_part[:512].astype(F32) + swap_core(result_part[512:]).astype(F32)
    result = (hidden + collect_x(result_part.astype(BF))).astype(BF)

    grad_in = dot_cols(normed_all, grad_pre).astype(BF)
    grad_down = dot_cols(mixed, grad_all).astype(BF)

    main = jnp.concatenate(
        [
            grad_in.reshape(8, 8, 24, 1280),
            grad_down[:FE]
            .reshape(8, 64, 3, 512)
            .transpose(0, 2, 1, 3)
            .reshape(8, 8, 24, 512),
        ],
        axis=3,
    )
    main = main.transpose(1, 0, 2, 3).reshape(8, 192, 1792)
    side = jnp.pad(grad_down[FE:].reshape(8, 16, D), ((0, 0), (0, 0), (0, 256)))
    flat = jnp.concatenate([main, side], axis=1)
    flat = lax.psum_scatter(flat, "z", scatter_dimension=0, tiled=True)[0]
    main = flat[:192].reshape(8, 24, 2, 896).transpose(2, 0, 1, 3).reshape(16, 24, 896)
    main = exchange(main, PLANE).reshape(4, 4, 24, 896)
    main = jnp.sum(main.astype(F32), axis=0).astype(BF).reshape(96, 896)
    to = (jnp.arange(2) == core)[None, :, None, None]
    side = flat[192:, :D].reshape(16, 2, 768).transpose(1, 0, 2)
    side = jnp.where(to, side[:, None], 0).reshape(4, 16, 768)
    side = jnp.sum(exchange(side, ("ylo", "yhi")).astype(F32), axis=0).astype(BF)
    side = jnp.pad(side, ((0, 0), (0, 128)))
    whole = lax.all_gather(jnp.concatenate([main, side], axis=0), REP)
    whole = whole.reshape(8, 2, 2, 112, 896)
    main = whole[:, :, :, :96].reshape(8, 2, 8, 24, 896)
    low, high = main[:, 0], main[:, 1]
    sum_expert_in = jnp.concatenate([low, high[..., :128]], axis=-1)
    sum_expert_in = sum_expert_in.transpose(0, 2, 1, 3).reshape(192, 8, 1024).astype(F32)
    sum_shared_in = high[..., 128:384].reshape(8, 8, 24, 2, 128).transpose(0, 2, 3, 1, 4)
    sum_shared_in = sum_shared_in.reshape(192, 2048).astype(F32)
    sum_expert_out = high[..., 384:].transpose(1, 0, 2, 3).reshape(8, 3, 64, 512)
    sum_expert_out = sum_expert_out.transpose(0, 2, 1, 3).reshape(8, 64, D).astype(F32)
    side = lax.dynamic_index_in_dim(whole[:, :, :, 96:, :768], half, 2, False)
    sum_shared_out = side.transpose(0, 2, 1, 3).reshape(128, D).astype(F32)

    grad_gates = back_sum[:, D : D + 8] + back_sum[:, D + 8 : D + 16]
    grad_logits = (
        gates * (grad_gates - jnp.sum(gates * grad_gates, axis=-1, keepdims=True))
    ).astype(BF)
    grad_normed_two = back_sum[:, :D] + dot(grad_logits, router)
    grad_router = dot_cols(normed_two, jnp.pad(grad_logits, ((0, 0), (0, 120))))
    grad_gain_ffn = jnp.sum(grad_normed_two * unit_two, axis=0, keepdims=True)
    grad_hidden = cotangent.astype(F32) + norm_back(
        grad_normed_two, unit_two, factor_two, gain_two
    )
    hidden_low = spread_x(grad_hidden.astype(BF))

    grad_out = dot_cols(attended, hidden_low).astype(BF)
    grad_att = dot_rows(hidden_low, w_o).astype(BF)
    grad_heads = grad_att.reshape(512, GROUP, HEAD).transpose(1, 0, 2)
    probs_again = jnp.exp(scores_of() - log_total)
    grad_probs = jnp.einsum("gtd,sd->gts", grad_heads, values, preferred_element_type=F32)
    inner = jnp.sum(probs_again * grad_probs, axis=-1, keepdims=True)
    grad_scores = (probs_again * (grad_probs - inner)).astype(BF)
    grad_query = jnp.einsum("gts,sd->tgd", grad_scores, keys, preferred_element_type=F32) * SCALE
    grad_query = grad_query.reshape(512, GROUP * HEAD).astype(BF)
    grad_keys = jnp.einsum("gts,gtd->sd", grad_scores, queries, preferred_element_type=F32) * SCALE
    grad_values = jnp.einsum(
        "gts,gtd->sd", probs_again.astype(BF), grad_heads, preferred_element_type=F32
    )
    grad_kv = jnp.concatenate([grad_keys, grad_values], axis=1)
    from_other = lax.ppermute(grad_kv[512:].astype(BF), "yhi", [(1, 0)])
    grad_kv = (grad_kv[:512] + from_other.astype(F32)).astype(BF)
    grad_qkv = jnp.concatenate([grad_query, grad_kv], axis=1)
    grad_normed_one = dot_rows(grad_qkv, w_qkv)
    grad_gain_attn = jnp.sum(grad_normed_one * unit_one, axis=0, keepdims=True)
    grad_weights = dot_cols(normed_one, grad_qkv).astype(BF)

    gains = jnp.concatenate([grad_gain_ffn, grad_gain_attn], axis=0).T
    small = (grad_router + jnp.pad(gains, ((0, 0), (8, 118)))).astype(BF)
    cols = jnp.concatenate([grad_weights, small], axis=1).reshape(8, 8, 24, 2, 384)
    cols = cols.transpose(3, 1, 0, 2, 4).reshape(2, 8, 192, 384)
    outs = grad_out.reshape(2, 8, 24, 2, 2, 384).transpose(3, 1, 0, 4, 2, 5)
    flat = jnp.concatenate([cols, outs.reshape(2, 8, 96, 384)], axis=2)
    keep = lax.dynamic_index_in_dim(flat, core, 0, False)
    give = lax.dynamic_index_in_dim(flat, 1 - core, 0, False)
    flat = exchange(plus(keep, swap_core(give)), "z")
    flat = jnp.sum(flat.astype(F32), axis=0).astype(BF)
    outs = lax.dynamic_update_slice(
        jnp.zeros((8, 48, 384), BF), flat[192:].reshape(2, 48, 384), (2 * key_head, 0, 0)
    )
    flat = jnp.concatenate([flat[:192].reshape(8, 24, 384), outs], axis=1)
    got = exchange(jnp.concatenate([flat, flat], axis=0), PLANE).reshape(4, 4, 72, 384)
    got = jnp.sum(got.astype(F32), axis=0)
    outs = jnp.sum(got[:, 24:], axis=0)
    mine = jnp.concatenate([got[:, :24].reshape(96, 384), outs], axis=0).astype(BF)
    mine = spread_z(mine, level)
    other = swap_core(mine)
    first, second = jnp.where(core == 0, mine, other), jnp.where(core == 0, other, mine)
    cols = first[:, :96].reshape(8, 4, 24, 384)
    cols = jnp.stack([cols[:, k] for k in KEY_HEAD], axis=2)
    sum_query = cols.reshape(192, D).astype(F32)
    cols = second[:, :96].reshape(8, 4, 24, 3, 128)
    small = jnp.sum(cols[..., 2, :].astype(F32), axis=1).reshape(192, 128)
    cols = jnp.stack([cols[:, k] for k in KEY_HEAD], axis=2)
    sum_key = cols[:, :, :, 0].reshape(192, 512).astype(F32)
    sum_value = cols[:, :, :, 1].reshape(192, 512).astype(F32)
    outs = jnp.stack([first[:, 96:], second[:, 96:]], axis=1).reshape(8, 4, 24, 384)
    sum_out = outs.transpose(0, 2, 1, 3).reshape(192, D).astype(F32)

    back_one = collect_x(grad_normed_one.astype(BF))
    unit_own, factor_own = normalize(inputs)
    grad_input = (grad_hidden + norm_back(back_one, unit_own, factor_own, gain_one)).astype(BF)

    return (
        result,
        grad_input,
        small[:, 9],
        sum_query,
        sum_key,
        sum_value,
        sum_out,
        small[:, 8],
        small[:, :8],
        sum_shared_in,
        sum_shared_out,
        sum_expert_in,
        sum_expert_out,
    )


def solution(mesh):
    fine = Mesh(mesh.devices.reshape(SIZES), AXES)
    tokens = P((*REP, *FSDP), None)
    first = P(FSDP, None)
    return jax.shard_map(
        shards,
        mesh=fine,
        in_specs=(
            tokens,
            P(REP),
            tokens,
            P(FSDP),
            first,
            first,
            first,
            first,
            P(FSDP),
            first,
            first,
            first,
            P(FSDP, None, None),
            P(None, FSDP, None),
            tokens,
        ),
        out_specs=(
            tokens,
            tokens,
            P(FSDP),
            first,
            first,
            first,
            first,
            P(FSDP),
            first,
            first,
            first,
            P(FSDP, None, None),
            P(None, FSDP, None),
        ),
        check_vma=False,
    )
```

```python
import math

import jax
import jax.numpy as jnp
from jax import lax
from jax.experimental import pallas as pl
from jax.experimental.pallas import tpu as pltpu
from jax.sharding import Mesh, PartitionSpec as P

HEADS = 12
KV_HEADS = 4
HEAD = 128
GROUP = HEADS // KV_HEADS
D = 1536
FE = 512
FS = 1024
EXPERTS = 8
EPS = 1e-05
SCALE = 1.0 / math.sqrt(HEAD)

AXES = ("z", "ylo", "core", "yhi", "x")
SIZES = (8, 2, 2, 2, 4)
REP = ("z", "ylo", "core")
FSDP = ("yhi", "x")
PLANE = ("ylo", "yhi", "x")
KEY_HEAD = (0, 2, 1, 3)
BF = jnp.bfloat16
F32 = jnp.float32


def dot(left, right):
    return jnp.dot(left, right, preferred_element_type=F32)


def dot_rows(left, right):
    return lax.dot_general(left, right, (((1,), (1,)), ((), ())), preferred_element_type=F32)


def dot_cols(left, right):
    return lax.dot_general(left, right, (((0,), (0,)), ((), ())), preferred_element_type=F32)


def exchange(blocks, axes):
    return lax.all_to_all(blocks, axes, 0, 0, tiled=True)


def up_x(rows):
    return lax.ppermute(rows, "x", [(i, (i + 1) % 4) for i in range(4)])


def down_x(rows):
    return lax.ppermute(rows, "x", [(i, (i + 3) % 4) for i in range(4)])


def spread_x(rows):
    cut = rows.shape[0] // 2
    below, above = up_x(rows), down_x(rows)
    return rows, below, above, up_x(below[:cut]), down_x(above[cut:])


def pieces_of(rows):
    return tuple(rows[at : at + size] for at, size in PIECES)


def collect_x(pieces, beside=None):
    own, below, above, far_up, far_down = pieces
    cut = far_up.shape[0]
    far_up, far_down = up_x(far_up), down_x(far_down)
    above = jnp.concatenate([plus(above[:cut], far_up), above[cut:]], axis=0)
    below = jnp.concatenate([below[:cut], plus(below[cut:], far_down)], axis=0)
    if beside is not None:
        above, below, beside = lax.optimization_barrier((above, below, beside))
    total = own.astype(F32) + up_x(above).astype(F32) + down_x(below).astype(F32)
    return total if beside is None else (total, beside)


def plus(left, right):
    return (left.astype(F32) + right.astype(F32)).astype(BF)


def spread_z(rows, level):
    up = [(i, (i + 1) % 8) for i in range(8)]
    down = [(i, (i + 7) % 8) for i in range(8)]
    cut = rows.shape[0] // 2
    whole = jnp.zeros((8, *rows.shape), rows.dtype)
    rest = (jnp.uint32(0),) * (rows.ndim - 1)

    level = level.astype(jnp.int32)

    def put(whole, block, distance, start=0):
        return lax.dynamic_update_slice(
            whole,
            block[None],
            ((level + distance + 8 & 7).astype(jnp.uint32), jnp.uint32(start), *rest)
        )

    whole = put(whole, rows, 0)
    below = above = rows
    for k in (1, 2, 3):
        below, above = lax.ppermute(below, "z", up), lax.ppermute(above, "z", down)
        whole = put(put(whole, below, -k), above, k)
    whole = put(whole, lax.ppermute(below[:cut], "z", up), 4)
    return put(whole, lax.ppermute(above[cut:], "z", down), 4, cut)


def swap_core(rows):
    return lax.ppermute(rows, "core", [(0, 1), (1, 0)])


def pair_of_float(values):
    high = values.astype(BF)
    return high, (values - high.astype(F32)).astype(BF)


def normalize(values):
    factor = lax.rsqrt(jnp.mean(values * values, axis=-1, keepdims=True) + EPS)
    return values * factor, factor


def norm_back(grad_normed, unit, factor, gain):
    scaled = grad_normed * gain
    inner = jnp.mean(scaled * unit, axis=-1, keepdims=True)
    return factor * (scaled - unit * inner)


def silu_slope(values, sig):
    return sig * (1.0 + values * (1.0 - sig))


def expert_kernel(member, own, below, above, far_up, far_down, own_o, below_o, above_o, far_up_o,
                  far_down_o, grad, blocks, shared_down, back_own, back_other, mixed, grad_pre, normed, w_down,
                  w_in, rows):
    step = pl.program_id(0)

    @pl.when(step == 0)
    def _():
        for b in range(8):
            at = lax.rem(b - member[0] + 8, 8)
            w_in[b * 192 : (b + 1) * 192] = blocks[at, :, :1280]
            for k in range(3):
                w_down[b * 64 : (b + 1) * 64, k * 512 : (k + 1) * 512] = blocks[
                    at, k * 64 : (k + 1) * 64, 1280:
                ]
        w_down[FE:] = shared_down[...]
        at = 0
        for piece in (own, below, above, far_up, far_down, own_o, below_o, above_o, far_up_o,
                      far_down_o):
            rows[at : at + piece.shape[0]] = piece[...]
            at += piece.shape[0]

    part = pl.ds(pl.multiple_of(step * 256, 256), 256)
    x = rows[part, :D]
    lane = lax.broadcasted_iota(jnp.int32, (256, 128), 1)
    expert = member[1]
    high, low = lane == expert, lane == expert + 8
    gate = jnp.sum(
        jnp.where(high | low, rows[part, D:].astype(F32), 0.0), axis=1, keepdims=True
    )
    back_down = dot_rows(grad[...], w_down[...])
    pre = dot(x, w_in[...])
    gate_part, up_part = pre[:, :FE], pre[:, FE : 2 * FE]
    shared_gate, shared_up = pre[:, 2 * FE : 2 * FE + 128], pre[:, 2 * FE + 128 :]
    gate_sig = jax.nn.sigmoid(gate_part)
    gate_act = gate_part * gate_sig
    activ = gate_act * up_part
    shared_sig = jax.nn.sigmoid(shared_gate)
    shared_silu = shared_gate * shared_sig
    grad_mixed, grad_shared = back_down[:, :FE], back_down[:, FE:]
    grad_gate = jnp.sum(grad_mixed * activ, axis=1, keepdims=True)
    grad_activ = grad_mixed * gate
    mixed[:, :FE] = (gate * activ).astype(BF)
    mixed[:, FE:] = (shared_silu * shared_up).astype(BF)
    grad_pre[:, :FE] = (grad_activ * up_part * silu_slope(gate_part, gate_sig)).astype(BF)
    grad_pre[:, FE : 2 * FE] = (grad_activ * gate_act).astype(BF)
    grad_pre[:, 2 * FE : 2 * FE + 128] = (
        grad_shared * shared_up * silu_slope(shared_gate, shared_sig)
    ).astype(BF)
    grad_pre[:, 2 * FE + 128 :] = (grad_shared * shared_silu).astype(BF)
    normed[...] = x
    back = dot_rows(grad_pre[...], w_in[...]).astype(BF)
    top = grad_gate.astype(BF).astype(F32)
    tail = jnp.where(high, top, jnp.where(low, grad_gate - top, 0.0)).astype(BF)

    @pl.when(step < 2)
    def _():
        back_own[:, :D], back_own[:, D:] = back, tail

    @pl.when(step >= 2)
    def _():
        back_other[:, :D], back_other[:, D:] = back, tail


def expert_pass(member, expert, pieces, grad_all, blocks, shared_down):
    whole = lambda a: pl.BlockSpec(a.shape, lambda i, *_, n=a.ndim: (0,) * n)
    chunk = lambda n: pl.BlockSpec((256, n), lambda i, *_: (i, 0))
    shape = lambda n, rows=1024: jax.ShapeDtypeStruct((rows, n), BF)
    return pl.pallas_call(
        expert_kernel,
        out_shape=(shape(1664, 512), shape(1664, 512), shape(640), shape(1280), shape(D), shape(D, 640)),
        grid_spec=pltpu.PrefetchScalarGridSpec(
            num_scalar_prefetch=1,
            grid=(4,),
            in_specs=[*(whole(p) for p in pieces), chunk(D), whole(blocks), whole(shared_down)],
            out_specs=(
                pl.BlockSpec((256, 1664), lambda i, *_: (jnp.minimum(i, 1), 0)),
                pl.BlockSpec((256, 1664), lambda i, *_: (jnp.maximum(i - 2, 0), 0)),
                chunk(640),
                chunk(1280),
                chunk(D),
                pl.BlockSpec((640, D), lambda i, *_: (0, 0)),
            ),
            scratch_shapes=[
                pltpu.VMEM((D, 1280), BF),
                pltpu.VMEM((1024, 1664), BF),
            ],
        ),
        compiler_params=pltpu.CompilerParams(vmem_limit_bytes=56 << 20),
        cost_estimate=pl.CostEstimate(
            flops=2 * 1024 * D * 3200, bytes_accessed=30 << 20, transcendentals=1024 * 640
        ),
    )(jnp.stack([member, expert]).astype(jnp.int32), *pieces, grad_all, blocks, shared_down)


def expert_grad_kernel(normed, grad_pre, mixed, shared, grad, grad_cols, out):
    into = dot_cols(normed[...], grad_pre[...])
    down = dot_cols(mixed[...], grad[...])
    side = dot_cols(shared[...], grad_cols[...])
    for b in range(2):
        folded = jnp.concatenate(
            [down[b * 64 : (b + 1) * 64, k * 512 : (k + 1) * 512] for k in range(3)], axis=0
        )
        for z in range(8):
            mine = jnp.concatenate(
                [side[z * 16 + b * 8 : z * 16 + b * 8 + 8, k * 128 : (k + 1) * 128] for k in range(3)],
                axis=0,
            )
            out[z, b] = jnp.concatenate(
                [
                    into[b * 192 + z * 24 : b * 192 + z * 24 + 24],
                    folded[z * 24 : z * 24 + 24],
                    mine,
                ],
                axis=1,
            ).astype(BF)


def expert_grads(normed, grad_pre, mixed, grad_all):
    return pl.pallas_call(
        expert_grad_kernel,
        out_shape=jax.ShapeDtypeStruct((8, 8, 24, 1920), BF),
        grid=(4,),
        in_specs=[
            pl.BlockSpec((1024, 384), lambda j: (0, j)),
            pl.BlockSpec((1024, 1280), lambda j: (0, 0)),
            pl.BlockSpec((1024, 128), lambda j: (0, j)),
            pl.BlockSpec((1024, 128), lambda j: (0, 4)),
            pl.BlockSpec((1024, D), lambda j: (0, 0)),
            pl.BlockSpec((1024, 384), lambda j: (0, j)),
        ],
        out_specs=pl.BlockSpec((8, 2, 24, 1920), lambda j: (0, j, 0, 0)),
        compiler_params=pltpu.CompilerParams(vmem_limit_bytes=56 << 20),
        cost_estimate=pl.CostEstimate(
            flops=2 * 1024 * D * 1920, bytes_accessed=22 << 20, transcendentals=0
        ),
    )(normed, grad_pre, mixed, mixed, grad_all, grad_all)


def full(a):
    return pl.BlockSpec(a.shape, lambda *_, n=len(a.shape): (0,) * n)


def on_chip(kernel, scalars, args, outs, scratch=(), flops=0, exps=0):
    size = sum(math.prod(a.shape) * a.dtype.itemsize for a in (*args, *outs))
    return pl.pallas_call(
        kernel,
        out_shape=tuple(outs),
        grid_spec=pltpu.PrefetchScalarGridSpec(
            num_scalar_prefetch=1,
            grid=(1,),
            in_specs=[full(a) for a in args],
            out_specs=tuple(full(a) for a in outs),
            scratch_shapes=list(scratch),
        ),
        compiler_params=pltpu.CompilerParams(vmem_limit_bytes=56 << 20),
        cost_estimate=pl.CostEstimate(flops=flops, bytes_accessed=size, transcendentals=exps),
    )(scalars, *args)


def out(*shape, dtype=BF):
    return jax.ShapeDtypeStruct(shape, dtype)


PIECES = ((0, 128), (128, 128), (256, 128), (384, 64), (448, 64))


def pack_kernel(core, query, key, value, small, slots):
    rows = pl.ds(pl.multiple_of(core[0] * 96, 32), 96)
    for k, head in enumerate(KEY_HEAD):
        for slot in (k, k + 4):
            slots[slot, :96, :384] = query[rows, head * 384 : (head + 1) * 384]
            slots[slot, :96, 384:512] = key[rows, head * 128 : (head + 1) * 128]
            slots[slot, :96, 512:] = value[rows, head * 128 : (head + 1) * 128]
            slots[slot, 96:] = small[...]


def project_kernel(core, own, below, above, far_up, far_down, gain, got, other, normed, query, kv, weight):
    for b in range(8):
        first = pl.multiple_of(b * 192 + core[0] * 96, 32)
        second = pl.multiple_of(b * 192 + (1 - core[0]) * 96, 32)
        weight[pl.ds(first, 96)] = got[b, :96]
        weight[pl.ds(second, 96)] = other[b]
    for (at, size), piece in zip(PIECES, (own, below, above, far_up, far_down)):
        unit, _ = normalize(piece[...].astype(F32))
        normed[at : at + size] = (unit * gain[...]).astype(BF)
    both = dot(normed[...], weight[...]).astype(BF)
    query[...] = both[:, : GROUP * HEAD]
    kv[...] = both[:, GROUP * HEAD :]


def mask_of(query_at, query_seg, key_at, key_seg):
    return (query_at == key_at) | (
        (key_at < query_at) & (query_seg == key_seg) & (key_seg != 0)
    )


def attend_kernel(core, query, kv, kv_other, qat, qseg, kat, kseg, mine, other, own, below, above, far_up,
                  far_down, attended, logs, weight):
    for c in range(2):
        @pl.when(core[0] == c)
        def _():
            weight[c * 192 : (c + 1) * 192] = mine[...]
            weight[(1 - c) * 192 : (2 - c) * 192] = other[...]
    allowed = mask_of(qat[...], qseg[...], kat[...], kseg[...])
    keys = jnp.concatenate([kv[:, :HEAD], kv_other[:, :HEAD]], axis=0)
    values = jnp.concatenate([kv[:, HEAD:], kv_other[:, HEAD:]], axis=0)
    lane = lax.broadcasted_iota(jnp.int32, (512, 128), 1)
    kept = jnp.zeros((512, 128), F32)
    for g in range(GROUP):
        scores = dot_rows(query[:, g * HEAD : (g + 1) * HEAD], keys) * SCALE
        scores = jnp.where(allowed, scores, -1e30)
        top = jnp.max(scores, axis=1, keepdims=True)
        expo = jnp.exp(scores - top)
        total = jnp.sum(expo, axis=1, keepdims=True)
        kept = jnp.where(lane == g, top + jnp.log(total), kept)
        attended[:, g * HEAD : (g + 1) * HEAD] = dot((expo / total).astype(BF), values).astype(BF)
    logs[...] = kept
    whole = dot(attended[...], weight[...]).astype(BF)
    for (at, size), piece in zip(PIECES, (own, below, above, far_up, far_down)):
        piece[...] = whole[at : at + size]


def attend_back_kernel(core, own, below, above, far_up, far_down, query, kv, kv_other, qat, qseg, kat, kseg,
                       mine, other, logs, grad, grad_query, grad_own, grad_other, weight):
    for c in range(2):
        @pl.when(core[0] == c)
        def _():
            weight[c * 192 : (c + 1) * 192] = mine[...]
            weight[(1 - c) * 192 : (2 - c) * 192] = other[...]
    for (at, size), piece in zip(PIECES, (own, below, above, far_up, far_down)):
        grad[at : at + size] = piece[...]
    grad_att = dot_rows(grad[...], weight[...]).astype(BF)
    allowed = mask_of(qat[...], qseg[...], kat[...], kseg[...])
    keys = jnp.concatenate([kv[:, :HEAD], kv_other[:, :HEAD]], axis=0)
    values = jnp.concatenate([kv[:, HEAD:], kv_other[:, HEAD:]], axis=0)
    grad_keys = jnp.zeros((1024, HEAD), F32)
    grad_values = jnp.zeros((1024, HEAD), F32)
    for g in range(GROUP):
        queries = query[:, g * HEAD : (g + 1) * HEAD]
        heads = grad_att[:, g * HEAD : (g + 1) * HEAD]
        scores = jnp.where(allowed, dot_rows(queries, keys) * SCALE, -1e30)
        probs = jnp.exp(scores - logs[:, g : g + 1])
        grad_probs = dot_rows(heads, values)
        inner = jnp.sum(probs * grad_probs, axis=1, keepdims=True)
        grad_scores = (probs * (grad_probs - inner)).astype(BF)
        grad_query[:, g * HEAD : (g + 1) * HEAD] = (dot(grad_scores, keys) * SCALE).astype(BF)
        grad_keys += dot_cols(grad_scores, queries)
        grad_values += dot_cols(probs.astype(BF), heads)
    grad_keys = grad_keys * SCALE
    grad_own[:, :HEAD] = grad_keys[:512]
    grad_own[:, HEAD:] = grad_values[:512]
    grad_other[:, :HEAD] = grad_keys[512:].astype(BF)
    grad_other[:, HEAD:] = grad_values[512:].astype(BF)


def project_back_kernel(core, tok_own, tok_below, tok_above, tok_up, tok_down, grad_query, grad_kv, from_other, weight,
                        normed, attended, grad, small, keep, give, own, below, above, far_up,
                        far_down, both):
    both[:, : GROUP * HEAD] = grad_query[...]
    both[:, GROUP * HEAD :] = (grad_kv[...] + from_other[...].astype(F32)).astype(BF)
    gain_grad = jnp.zeros((1, D), F32)
    for (at, size), tok, piece in zip(
        PIECES,
        (tok_own, tok_below, tok_above, tok_up, tok_down),
        (own, below, above, far_up, far_down),
    ):
        unit, _ = normalize(tok[...].astype(F32))
        back = dot_rows(both[at : at + size], weight[...])
        gain_grad += jnp.sum(back * unit, axis=0, keepdims=True)
        piece[...] = back.astype(BF)
    column = jnp.broadcast_to(gain_grad, (128, D)).T
    lane = lax.broadcasted_iota(jnp.int32, (D, 128), 1)
    side = jnp.where(lane == 9, column, small[...])
    into = dot_cols(normed[...], both[...])
    outs = dot_cols(attended[...], grad[...])
    for c in range(2):
        def put(ref):
            for z in range(8):
                for b in range(8):
                    rows = slice(b * 192 + z * 24, b * 192 + z * 24 + 24)
                    if c == 0:
                        block = into[rows, :384]
                    else:
                        block = jnp.concatenate([into[rows, 384:], side[rows]], axis=1)
                    ref[z, b] = block.astype(BF)
                for j in range(2):
                    for k in range(2):
                        block = outs[
                            j * 192 + z * 24 : j * 192 + z * 24 + 24,
                            c * 768 + k * 384 : c * 768 + (k + 1) * 384,
                        ]
                        ref[z, 8 + j * 2 + k] = block.astype(BF)

        @pl.when(core[0] == c)
        def _():
            put(keep)

        @pl.when(core[0] != c)
        def _():
            put(give)


def settle_kernel(core, mine, other, query, key, value, small, outs):
    def put(first, second):
        for z in range(8):
            rows = slice(z * 24, (z + 1) * 24)
            sums = jnp.zeros((24, 128), F32)
            for k, head in enumerate(KEY_HEAD):
                query[rows, head * 384 : (head + 1) * 384] = first[z, k].astype(F32)
                key[rows, head * 128 : (head + 1) * 128] = second[z, k, :, :128].astype(F32)
                value[rows, head * 128 : (head + 1) * 128] = second[z, k, :, 128:256].astype(F32)
                sums += second[z, k, :, 256:].astype(F32)
            small[rows] = sums
            for k in range(2):
                outs[rows, k * 384 : (k + 1) * 384] = first[z, 4 + k].astype(F32)
                outs[rows, (2 + k) * 384 : (3 + k) * 384] = second[z, 4 + k].astype(F32)

    @pl.when(core[0] == 0)
    def _():
        put(mine, other)

    @pl.when(core[0] == 1)
    def _():
        put(other, mine)


def shards(
    tokens,
    segment_ids,
    routes,
    gain_attn,
    w_query,
    w_key,
    w_value,
    w_out,
    gain_ffn,
    w_router,
    w_shared_in,
    w_shared_out,
    w_expert_in,
    w_expert_out,
    cotangent,
):
    level, core, half, place = (
        lax.axis_index(a).astype(jnp.uint32) for a in ("z", "core", "yhi", "x")
    )
    rows = tokens.shape[0]
    own = w_query.shape[0]

    member = half * 4 + place
    key_head = jnp.where((place == 1) | (place == 2), 3 - place, place)

    tokens_x = spread_x(tokens)
    at_core = core.reshape(1).astype(jnp.int32)
    small = jnp.concatenate([gain_attn[None], gain_ffn[None], w_router.T], axis=0)
    small = jnp.pad(small, ((0, 6), (0, 448)))
    (slots,) = on_chip(
        pack_kernel, at_core, (w_query, w_key, w_value, small), (out(8, 112, 640),)
    )
    got = exchange(slots, FSDP)
    small = got[:, 96:106, :192].transpose(1, 0, 2).reshape(10, D)
    gain_one = small[:1].astype(F32)
    gain_two = small[1:2].astype(F32)
    router = small[2:]

    w_out_late, *_ = lax.optimization_barrier((w_out, *tokens_x[1:3]))
    out_mine = lax.ppermute(
        w_out_late,
        ("core", "yhi", "x"),
        [(s * 8 + b, (b % 2) * 8 + s * 4 + KEY_HEAD[b // 2]) for s in range(2) for b in range(8)],
    )

    target = core * 4 + ((member - level + 8) & 3)
    block = jnp.concatenate(
        [
            lax.dynamic_index_in_dim(w_expert_in, target, 1, False),
            lax.dynamic_slice_in_dim(w_shared_in, target * 128, 128, 1),
            lax.dynamic_slice_in_dim(w_shared_in, FS + target * 128, 128, 1),
            lax.dynamic_index_in_dim(w_expert_out, target, 0, False)
            .reshape(64, 3, 512)
            .transpose(1, 0, 2)
            .reshape(192, 512),
        ],
        axis=1,
    )
    block, *_ = lax.optimization_barrier((block, *tokens_x[1:3]))
    block = lax.ppermute(
        block,
        ("z", *FSDP),
        [(z * 8 + b, z * 8 + (b - z) % 8) for z in range(8) for b in range(8)],
    )
    half_qkv, block, *_ = lax.optimization_barrier((got[:, :96], block, *tokens_x[3:]))
    qkv_other = swap_core(half_qkv)
    blocks = lax.all_gather(block, "z")
    cotangent_late, shared_late, _ = lax.optimization_barrier((cotangent, w_shared_out, got))
    other = lax.ppermute(shared_late, ("core", "yhi"), [(0, 1), (3, 2)])
    shared_down = jnp.where(core == half, w_shared_out, other)

    grad_own = jnp.concatenate(spread_x(cotangent_late), axis=0)
    grad_all = jnp.concatenate([grad_own, swap_core(grad_own)], axis=0)

    inputs = tokens.astype(F32)
    normed_one, query, kv, w_qkv = on_chip(
        project_kernel,
        at_core,
        (*tokens_x, gain_one, got, qkv_other),
        (out(512, D), out(512, 384), out(512, 256), out(D, 640)),
        flops=2 * 512 * D * 640,
    )
    kv_other = lax.ppermute(kv, "yhi", [(0, 1)])
    out_mine, _ = lax.optimization_barrier((out_mine, kv))
    out_other = swap_core(out_mine)
    starts = [((place + k) & 3) * 128 for k in (0, 3, 1, 2)]
    pos = jnp.concatenate([s.astype(jnp.int32) + jnp.arange(128, dtype=jnp.int32) for s in starts])
    seg_own = jnp.concatenate(
        [lax.dynamic_slice_in_dim(segment_ids, half * 512 + s, 128) for s in starts]
    )
    seg_other = jnp.concatenate([lax.dynamic_slice_in_dim(segment_ids, s, 128) for s in starts])
    pos_other = jnp.where(half == 1, pos - 512, 1 << 20)
    places = (
        pos[:, None],
        seg_own[:, None],
        jnp.concatenate([pos, pos_other])[None],
        jnp.concatenate([seg_own, seg_other])[None],
    )
    part = [out(size, D) for _, size in PIECES]
    *hidden_part, attended, logs = on_chip(
        attend_kernel,
        at_core,
        (query, kv, kv_other, *places, out_mine, out_other),
        (*part, out(512, 384), out(512, 128, dtype=F32)),
        scratch=[pltpu.VMEM((384, D), BF)],
        flops=2 * 512 * 384 * 3584,
        exps=3 * 512 * 1024,
    )
    hidden = inputs + collect_x(hidden_part)

    unit_two, factor_two = normalize(hidden)
    normed_two = (unit_two * gain_two).astype(BF)
    logits = dot_rows(normed_two, router)
    chosen = jnp.sum(
        (routes[:, :, None] == jnp.arange(EXPERTS, dtype=jnp.int32)[None, None, :]).astype(F32),
        axis=1,
    )
    weighted = chosen * jnp.exp(logits)
    gates = weighted / jnp.sum(weighted, axis=-1, keepdims=True)
    packed = jnp.concatenate(
        [normed_two, *pair_of_float(gates), jnp.zeros((rows, 112), BF)], axis=1
    )
    packed = spread_x(packed)
    packed = (*packed, *(swap_core(p) for p in packed))

    back_own, back_other, mixed, grad_pre, normed_all, w_down = expert_pass(
        member, core * 4 + place, packed, grad_all, blocks, shared_down
    )
    back_other = swap_core(back_other)
    back_part = [plus(o, s) for o, s in zip(pieces_of(back_own), pieces_of(back_other))]
    normed_all, _, _ = lax.optimization_barrier((normed_all, back_part[3], back_part[4]))
    flat = expert_grads(normed_all, grad_pre, mixed, grad_all)
    back_sum, flat_ffn = collect_x(back_part, flat)

    grad_gates = back_sum[:, D : D + 8] + back_sum[:, D + 8 : D + 16]
    grad_logits = (
        gates * (grad_gates - jnp.sum(gates * grad_gates, axis=-1, keepdims=True))
    ).astype(BF)
    grad_normed_two = back_sum[:, :D] + dot(grad_logits, router)
    grad_router = dot_cols(normed_two, jnp.pad(grad_logits, ((0, 0), (0, 120))))
    grad_gain_ffn = jnp.sum(grad_normed_two * unit_two, axis=0, keepdims=True)
    grad_hidden = cotangent.astype(F32) + norm_back(
        grad_normed_two, unit_two, factor_two, gain_two
    )
    hidden_low = spread_x(grad_hidden.astype(BF))

    mixed, _ = lax.optimization_barrier((mixed, hidden_low[1]))
    result_part = dot(mixed, w_down).astype(BF)
    result_part, _ = lax.optimization_barrier((result_part, hidden_low[3]))
    result_other = swap_core(result_part[512:])
    result_part = [
        plus(o, s) for o, s in zip(pieces_of(result_part[:512]), pieces_of(result_other))
    ]
    result = (hidden + collect_x(result_part)).astype(BF)

    grad_low, grad_query, grad_kv, to_other = on_chip(
        attend_back_kernel,
        at_core,
        (*hidden_low, query, kv, kv_other, *places, out_mine, out_other, logs),
        (out(512, D), out(512, 384), out(512, 256, dtype=F32), out(512, 256)),
        scratch=[pltpu.VMEM((384, D), BF)],
        flops=2 * 512 * 384 * 6656,
        exps=3 * 512 * 1024,
    )
    from_other = lax.ppermute(to_other, "yhi", [(1, 0)])
    small = grad_router + jnp.pad(grad_gain_ffn.T, ((0, 0), (8, 119)))
    keep, give, *back_one = on_chip(
        project_back_kernel,
        at_core,
        (*tokens_x, grad_query, grad_kv, from_other, w_qkv, normed_one, attended, grad_low, small),
        (out(8, 12, 24, 384), out(8, 12, 24, 384), *part),
        scratch=[pltpu.VMEM((512, 640), BF)],
        flops=2 * 512 * D * 1664,
    )

    flat = plus(keep, swap_core(give))
    ffn = lax.psum_scatter(flat_ffn, "z", scatter_dimension=0, tiled=True)[0]
    ffn, flat = lax.optimization_barrier((ffn, flat))
    main = ffn[..., :1792].reshape(8, 24, 2, 896).transpose(2, 0, 1, 3).reshape(16, 24, 896)
    main = exchange(main, PLANE).reshape(4, 4, 24, 896)
    main = jnp.sum(main.astype(F32), axis=0).astype(BF).reshape(96, 896)
    to = (jnp.arange(2) == core)[None, :, None, None]
    side = ffn[..., 1792:].reshape(2, 96, 128)
    side = jnp.where(to, side[:, None], 0).reshape(4, 96, 128)
    side = jnp.sum(exchange(side, ("ylo", "yhi")).astype(F32), axis=0).astype(BF)
    piece, flat = lax.optimization_barrier((jnp.concatenate([main, side], axis=1), flat))
    whole = lax.all_gather(piece, REP)
    whole = whole.reshape(8, 2, 2, 96, 1024)
    main = whole[..., :896].reshape(8, 2, 8, 24, 896)
    low, high = main[:, 0], main[:, 1]
    sum_expert_in = jnp.concatenate([low, high[..., :128]], axis=-1)
    sum_expert_in = sum_expert_in.transpose(0, 2, 1, 3).reshape(192, 8, 1024).astype(F32)
    sum_shared_in = high[..., 128:384].reshape(8, 8, 24, 2, 128).transpose(0, 2, 3, 1, 4)
    sum_shared_in = sum_shared_in.reshape(192, 2048).astype(F32)
    sum_expert_out = high[..., 384:].transpose(1, 0, 2, 3).reshape(8, 3, 64, 512)
    sum_expert_out = sum_expert_out.transpose(0, 2, 1, 3).reshape(8, 64, D).astype(F32)
    side = lax.dynamic_index_in_dim(whole[..., 896:], half, 2, False)
    side = side.reshape(8, 2, 2, 2, 3, 8, 128).transpose(0, 3, 5, 1, 2, 4, 6)
    sum_shared_out = side.reshape(128, D).astype(F32)

    flat = exchange(flat, "z")
    flat = jnp.sum(flat.astype(F32), axis=0).astype(BF)
    outs = lax.dynamic_update_slice(
        jnp.zeros((8, 2, 24, 384), BF), flat[8:].reshape(2, 2, 24, 384), (2 * key_head, *(jnp.uint32(0),) * 3)
    )
    flat = jnp.concatenate([flat[:8, None], outs], axis=1)
    got = exchange(jnp.concatenate([flat, flat], axis=0), PLANE).reshape(4, 4, 3, 24, 384)
    got = jnp.sum(got.astype(F32), axis=0)
    mine = jnp.concatenate([got[:, 0], jnp.sum(got[:, 1:], axis=0)], axis=0).astype(BF)
    mine = spread_z(mine, level)
    mine, sum_shared_in, sum_shared_out, sum_expert_in, sum_expert_out = lax.optimization_barrier(
        (mine, sum_shared_in, sum_shared_out, sum_expert_in, sum_expert_out)
    )
    sum_query, sum_key, sum_value, small, sum_out = on_chip(
        settle_kernel,
        at_core,
        (mine, swap_core(mine)),
        (
            out(192, D, dtype=F32),
            out(192, 512, dtype=F32),
            out(192, 512, dtype=F32),
            out(192, 128, dtype=F32),
            out(192, D, dtype=F32),
        ),
    )

    back_one = collect_x(back_one)
    unit_own, factor_own = normalize(inputs)
    grad_input = (grad_hidden + norm_back(back_one, unit_own, factor_own, gain_one)).astype(BF)

    return (
        result,
        grad_input,
        small[:, 9],
        sum_query,
        sum_key,
        sum_value,
        sum_out,
        small[:, 8],
        small[:, :8],
        sum_shared_in,
        sum_shared_out,
        sum_expert_in,
        sum_expert_out,
    )


def solution(mesh):
    fine = Mesh(mesh.devices.reshape(SIZES), AXES)
    tokens = P((*REP, *FSDP), None)
    first = P(FSDP, None)
    return jax.shard_map(
        shards,
        mesh=fine,
        in_specs=(
            tokens,
            P(REP),
            tokens,
            P(FSDP),
            first,
            first,
            first,
            first,
            P(FSDP),
            first,
            first,
            first,
            P(FSDP, None, None),
            P(None, FSDP, None),
            tokens,
        ),
        out_specs=(
            tokens,
            tokens,
            P(FSDP),
            first,
            first,
            first,
            first,
            P(FSDP),
            first,
            first,
            first,
            P(FSDP, None, None),
            P(None, FSDP, None),
        ),
        check_vma=False,
    )
```

```python
import math

import jax
import jax.numpy as jnp
from jax import lax
from jax.experimental import pallas as pl
from jax.experimental.pallas import tpu as pltpu
from jax.sharding import Mesh, PartitionSpec as P

HEADS = 12
KV_HEADS = 4
HEAD = 128
GROUP = HEADS // KV_HEADS
D = 1536
FE = 512
FS = 1024
EXPERTS = 8
EPS = 1e-05
SCALE = 1.0 / math.sqrt(HEAD)

AXES = ("z", "ylo", "core", "yhi", "x")
SIZES = (8, 2, 2, 2, 4)
REP = ("z", "ylo", "core")
FSDP = ("yhi", "x")
PLANE = ("ylo", "yhi", "x")
KEY_HEAD = (0, 2, 1, 3)
BF = jnp.bfloat16
F32 = jnp.float32


def dot(left, right):
    return jnp.dot(left, right, preferred_element_type=F32)


def dot_rows(left, right):
    return lax.dot_general(left, right, (((1,), (1,)), ((), ())), preferred_element_type=F32)


def dot_cols(left, right):
    return lax.dot_general(left, right, (((0,), (0,)), ((), ())), preferred_element_type=F32)


def exchange(blocks, axes):
    return lax.all_to_all(blocks, axes, 0, 0, tiled=True)


def up_x(rows):
    return lax.ppermute(rows, "x", [(i, (i + 1) % 4) for i in range(4)])


def down_x(rows):
    return lax.ppermute(rows, "x", [(i, (i + 3) % 4) for i in range(4)])


def spread_x(rows):
    cut = rows.shape[0] // 2
    below, above = up_x(rows), down_x(rows)
    return rows, below, above, up_x(below[:cut]), down_x(above[cut:])


def pieces_of(rows):
    return tuple(rows[at : at + size] for at, size in PIECES)


def collect_x(pieces, beside=None):
    own, below, above, far_up, far_down = pieces
    cut = far_up.shape[0]
    far_up, far_down = up_x(far_up), down_x(far_down)
    above = jnp.concatenate([plus(above[:cut], far_up), above[cut:]], axis=0)
    below = jnp.concatenate([below[:cut], plus(below[cut:], far_down)], axis=0)
    if beside is not None:
        above, below, beside = lax.optimization_barrier((above, below, beside))
    total = own.astype(F32) + up_x(above).astype(F32) + down_x(below).astype(F32)
    return total if beside is None else (total, beside)


def plus(left, right):
    return (left.astype(F32) + right.astype(F32)).astype(BF)


def spread_z(rows, level):
    up = [(i, (i + 1) % 8) for i in range(8)]
    down = [(i, (i + 7) % 8) for i in range(8)]
    cut = rows.shape[0] // 2
    whole = jnp.zeros((8, *rows.shape), rows.dtype)
    rest = (jnp.uint32(0),) * (rows.ndim - 1)

    level = level.astype(jnp.int32)

    def put(whole, block, distance, start=0):
        return lax.dynamic_update_slice(
            whole,
            block[None],
            ((level + distance + 8 & 7).astype(jnp.uint32), jnp.uint32(start), *rest)
        )

    whole = put(whole, rows, 0)
    below = above = rows
    for k in (1, 2, 3):
        below, above = lax.ppermute(below, "z", up), lax.ppermute(above, "z", down)
        whole = put(put(whole, below, -k), above, k)
    whole = put(whole, lax.ppermute(below[:cut], "z", up), 4)
    return put(whole, lax.ppermute(above[cut:], "z", down), 4, cut)


def after(value, *others):
    return lax.optimization_barrier((value, *others))[0]


def swap_core(rows):
    return lax.ppermute(rows, "core", [(0, 1), (1, 0)])


def pair_of_float(values):
    high = values.astype(BF)
    return high, (values - high.astype(F32)).astype(BF)


def normalize(values):
    factor = lax.rsqrt(jnp.mean(values * values, axis=-1, keepdims=True) + EPS)
    return values * factor, factor


def norm_back(grad_normed, unit, factor, gain):
    scaled = grad_normed * gain
    inner = jnp.mean(scaled * unit, axis=-1, keepdims=True)
    return factor * (scaled - unit * inner)


def silu_slope(values, sig):
    return sig * (1.0 + values * (1.0 - sig))


def expert_kernel(member, own, below, above, far_up, far_down, own_o, below_o, above_o, far_up_o,
                  far_down_o, grad, blocks, shared_down, back_own, back_other, mixed, grad_pre, normed, w_down,
                  w_in, rows):
    step = pl.program_id(0)

    @pl.when(step == 0)
    def _():
        for b in range(8):
            at = lax.rem(b - member[0] + 8, 8)
            w_in[b * 192 : (b + 1) * 192] = blocks[at, :, :1280]
            for k in range(3):
                w_down[b * 64 : (b + 1) * 64, k * 512 : (k + 1) * 512] = blocks[
                    at, k * 64 : (k + 1) * 64, 1280:
                ]
        w_down[FE:] = shared_down[...]
        at = 0
        for piece in (own, below, above, far_up, far_down, own_o, below_o, above_o, far_up_o,
                      far_down_o):
            rows[at : at + piece.shape[0]] = piece[...]
            at += piece.shape[0]

    part = pl.ds(pl.multiple_of(step * 256, 256), 256)
    x = rows[part, :D]
    lane = lax.broadcasted_iota(jnp.int32, (256, 128), 1)
    expert = member[1]
    high, low = lane == expert, lane == expert + 8
    gate = jnp.sum(
        jnp.where(high | low, rows[part, D:].astype(F32), 0.0), axis=1, keepdims=True
    )
    back_down = dot_rows(grad[...], w_down[...])
    pre = dot(x, w_in[...])
    gate_part, up_part = pre[:, :FE], pre[:, FE : 2 * FE]
    shared_gate, shared_up = pre[:, 2 * FE : 2 * FE + 128], pre[:, 2 * FE + 128 :]
    gate_sig = jax.nn.sigmoid(gate_part)
    gate_act = gate_part * gate_sig
    activ = gate_act * up_part
    shared_sig = jax.nn.sigmoid(shared_gate)
    shared_silu = shared_gate * shared_sig
    grad_mixed, grad_shared = back_down[:, :FE], back_down[:, FE:]
    grad_gate = jnp.sum(grad_mixed * activ, axis=1, keepdims=True)
    grad_activ = grad_mixed * gate
    mixed[:, :FE] = (gate * activ).astype(BF)
    mixed[:, FE:] = (shared_silu * shared_up).astype(BF)
    grad_pre[:, :FE] = (grad_activ * up_part * silu_slope(gate_part, gate_sig)).astype(BF)
    grad_pre[:, FE : 2 * FE] = (grad_activ * gate_act).astype(BF)
    grad_pre[:, 2 * FE : 2 * FE + 128] = (
        grad_shared * shared_up * silu_slope(shared_gate, shared_sig)
    ).astype(BF)
    grad_pre[:, 2 * FE + 128 :] = (grad_shared * shared_silu).astype(BF)
    normed[...] = x
    back = dot_rows(grad_pre[...], w_in[...]).astype(BF)
    top = grad_gate.astype(BF).astype(F32)
    tail = jnp.where(high, top, jnp.where(low, grad_gate - top, 0.0)).astype(BF)

    @pl.when(step < 2)
    def _():
        back_own[:, :D], back_own[:, D:] = back, tail

    @pl.when(step >= 2)
    def _():
        back_other[:, :D], back_other[:, D:] = back, tail


def expert_pass(member, expert, pieces, grad_all, blocks, shared_down):
    whole = lambda a: pl.BlockSpec(a.shape, lambda i, *_, n=a.ndim: (0,) * n)
    chunk = lambda n: pl.BlockSpec((256, n), lambda i, *_: (i, 0))
    shape = lambda n, rows=1024: jax.ShapeDtypeStruct((rows, n), BF)
    return pl.pallas_call(
        expert_kernel,
        out_shape=(shape(1664, 512), shape(1664, 512), shape(640), shape(1280), shape(D), shape(D, 640)),
        grid_spec=pltpu.PrefetchScalarGridSpec(
            num_scalar_prefetch=1,
            grid=(4,),
            in_specs=[*(whole(p) for p in pieces), chunk(D), whole(blocks), whole(shared_down)],
            out_specs=(
                pl.BlockSpec((256, 1664), lambda i, *_: (jnp.minimum(i, 1), 0)),
                pl.BlockSpec((256, 1664), lambda i, *_: (jnp.maximum(i - 2, 0), 0)),
                chunk(640),
                chunk(1280),
                chunk(D),
                pl.BlockSpec((640, D), lambda i, *_: (0, 0)),
            ),
            scratch_shapes=[
                pltpu.VMEM((D, 1280), BF),
                pltpu.VMEM((1024, 1664), BF),
            ],
        ),
        compiler_params=pltpu.CompilerParams(vmem_limit_bytes=56 << 20),
        cost_estimate=pl.CostEstimate(
            flops=2 * 1024 * D * 3200, bytes_accessed=30 << 20, transcendentals=1024 * 640
        ),
    )(jnp.stack([member, expert]).astype(jnp.int32), *pieces, grad_all, blocks, shared_down)


def expert_grad_kernel(normed, grad_pre, mixed, shared, grad, grad_cols, out):
    into = dot_cols(normed[...], grad_pre[...])
    down = dot_cols(mixed[...], grad[...])
    side = dot_cols(shared[...], grad_cols[...])
    for b in range(2):
        for z in range(8):
            at = b * 64 + z * 8
            folded = jnp.concatenate(
                [down[at : at + 8, k * 512 : (k + 1) * 512] for k in range(3)], axis=0
            )
            mine = jnp.concatenate(
                [side[z * 16 + b * 8 : z * 16 + b * 8 + 8, k * 128 : (k + 1) * 128] for k in range(3)],
                axis=0,
            )
            out[z, b] = jnp.concatenate(
                [
                    into[b * 192 + z * 24 : b * 192 + z * 24 + 24],
                    folded,
                    mine,
                ],
                axis=1,
            ).astype(BF)


def expert_grads(normed, grad_pre, mixed, grad_all):
    return pl.pallas_call(
        expert_grad_kernel,
        out_shape=jax.ShapeDtypeStruct((8, 8, 24, 1920), BF),
        grid=(4,),
        in_specs=[
            pl.BlockSpec((1024, 384), lambda j: (0, j)),
            pl.BlockSpec((1024, 1280), lambda j: (0, 0)),
            pl.BlockSpec((1024, 128), lambda j: (0, j)),
            pl.BlockSpec((1024, 128), lambda j: (0, 4)),
            pl.BlockSpec((1024, D), lambda j: (0, 0)),
            pl.BlockSpec((1024, 384), lambda j: (0, j)),
        ],
        out_specs=pl.BlockSpec((8, 2, 24, 1920), lambda j: (0, j, 0, 0)),
        compiler_params=pltpu.CompilerParams(vmem_limit_bytes=56 << 20),
        cost_estimate=pl.CostEstimate(
            flops=2 * 1024 * D * 1920, bytes_accessed=22 << 20, transcendentals=0
        ),
    )(normed, grad_pre, mixed, mixed, grad_all, grad_all)


def full(a):
    return pl.BlockSpec(a.shape, lambda *_, n=len(a.shape): (0,) * n)


def on_chip(kernel, scalars, args, outs, scratch=(), flops=0, exps=0):
    size = sum(math.prod(a.shape) * a.dtype.itemsize for a in (*args, *outs))
    return pl.pallas_call(
        kernel,
        out_shape=tuple(outs),
        grid_spec=pltpu.PrefetchScalarGridSpec(
            num_scalar_prefetch=1,
            grid=(1,),
            in_specs=[full(a) for a in args],
            out_specs=tuple(full(a) for a in outs),
            scratch_shapes=list(scratch),
        ),
        compiler_params=pltpu.CompilerParams(vmem_limit_bytes=56 << 20),
        cost_estimate=pl.CostEstimate(flops=flops, bytes_accessed=size, transcendentals=exps),
    )(scalars, *args)


def out(*shape, dtype=BF):
    return jax.ShapeDtypeStruct(shape, dtype)


PIECES = ((0, 128), (128, 128), (256, 128), (384, 64), (448, 64))


def pack_kernel(core, query, key, value, small, slots):
    rows = pl.ds(pl.multiple_of(core[0] * 96, 32), 96)
    for k, head in enumerate(KEY_HEAD):
        for slot in (k, k + 4):
            slots[slot, :96, :384] = query[rows, head * 384 : (head + 1) * 384]
            slots[slot, :96, 384:512] = key[rows, head * 128 : (head + 1) * 128]
            slots[slot, :96, 512:] = value[rows, head * 128 : (head + 1) * 128]
            slots[slot, 96:] = small[...]


def keys_kernel(core, own, below, above, far_up, far_down, gain, got, other, normed, kv, weight):
    for b in range(8):
        first = pl.multiple_of(b * 192 + core[0] * 96, 32)
        second = pl.multiple_of(b * 192 + (1 - core[0]) * 96, 32)
        weight[pl.ds(first, 96)] = got[b, :96]
        weight[pl.ds(second, 96)] = other[b]
    for (at, size), piece in zip(PIECES, (own, below, above, far_up, far_down)):
        unit, _ = normalize(piece[...].astype(F32))
        normed[at : at + size] = (unit * gain[...]).astype(BF)
    kv[...] = dot(normed[...], weight[:, GROUP * HEAD :]).astype(BF)


def query_kernel(core, normed, weight, kv, query):
    query[...] = dot(normed[...], weight[:, : GROUP * HEAD]).astype(BF)


def mask_of(query_at, query_seg, key_at, key_seg):
    return (query_at == key_at) | (
        (key_at < query_at) & (query_seg == key_seg) & (key_seg != 0)
    )


def attend_kernel(core, query, kv, kv_other, qat, qseg, kat, kseg, attended, logs):
    allowed = mask_of(qat[...], qseg[...], kat[...], kseg[...])
    keys = jnp.concatenate([kv[:, :HEAD], kv_other[:, :HEAD]], axis=0)
    values = jnp.concatenate([kv[:, HEAD:], kv_other[:, HEAD:]], axis=0)
    lane = lax.broadcasted_iota(jnp.int32, (512, 128), 1)
    kept = jnp.zeros((512, 128), F32)
    for g in range(GROUP):
        scores = dot_rows(query[:, g * HEAD : (g + 1) * HEAD], keys) * SCALE
        scores = jnp.where(allowed, scores, -1e30)
        top = jnp.max(scores, axis=1, keepdims=True)
        expo = jnp.exp(scores - top)
        total = jnp.sum(expo, axis=1, keepdims=True)
        kept = jnp.where(lane == g, top + jnp.log(total), kept)
        attended[:, g * HEAD : (g + 1) * HEAD] = dot((expo / total).astype(BF), values).astype(BF)
    logs[...] = kept


def output_kernel(core, attended, mine, other, own, below, above, far_up, far_down, weight):
    for c in range(2):
        @pl.when(core[0] == c)
        def _():
            weight[c * 192 : (c + 1) * 192] = mine[...]
            weight[(1 - c) * 192 : (2 - c) * 192] = other[...]
    whole = dot(attended[...], weight[...]).astype(BF)
    for (at, size), piece in zip(PIECES, (own, below, above, far_up, far_down)):
        piece[...] = whole[at : at + size]


def attend_back_kernel(core, own, below, above, far_up, far_down, query, kv, kv_other, qat, qseg, kat, kseg,
                       mine, other, logs, grad, grad_query, grad_own, grad_other, weight):
    for c in range(2):
        @pl.when(core[0] == c)
        def _():
            weight[c * 192 : (c + 1) * 192] = mine[...]
            weight[(1 - c) * 192 : (2 - c) * 192] = other[...]
    for (at, size), piece in zip(PIECES, (own, below, above, far_up, far_down)):
        grad[at : at + size] = piece[...]
    grad_att = dot_rows(grad[...], weight[...]).astype(BF)
    allowed = mask_of(qat[...], qseg[...], kat[...], kseg[...])
    keys = jnp.concatenate([kv[:, :HEAD], kv_other[:, :HEAD]], axis=0)
    values = jnp.concatenate([kv[:, HEAD:], kv_other[:, HEAD:]], axis=0)
    grad_keys = jnp.zeros((1024, HEAD), F32)
    grad_values = jnp.zeros((1024, HEAD), F32)
    for g in range(GROUP):
        queries = query[:, g * HEAD : (g + 1) * HEAD]
        heads = grad_att[:, g * HEAD : (g + 1) * HEAD]
        scores = jnp.where(allowed, dot_rows(queries, keys) * SCALE, -1e30)
        probs = jnp.exp(scores - logs[:, g : g + 1])
        grad_probs = dot_rows(heads, values)
        inner = jnp.sum(probs * grad_probs, axis=1, keepdims=True)
        grad_scores = (probs * (grad_probs - inner)).astype(BF)
        grad_query[:, g * HEAD : (g + 1) * HEAD] = (dot(grad_scores, keys) * SCALE).astype(BF)
        grad_keys += dot_cols(grad_scores, queries)
        grad_values += dot_cols(probs.astype(BF), heads)
    grad_keys = grad_keys * SCALE
    grad_own[:, :HEAD] = grad_keys[:512]
    grad_own[:, HEAD:] = grad_values[:512]
    grad_other[:, :HEAD] = grad_keys[512:].astype(BF)
    grad_other[:, HEAD:] = grad_values[512:].astype(BF)


def weight_grads_kernel(core, grad_query, grad_kv, from_other, weight, normed, attended, grad, small,
                        gain, keep, give, both):
    both[:, : GROUP * HEAD] = grad_query[...]
    both[:, GROUP * HEAD :] = (grad_kv[...] + from_other[...].astype(F32)).astype(BF)
    into = dot_cols(normed[...], both[...])
    column = jnp.sum(into * weight[...].astype(F32), axis=1, keepdims=True) / gain[...]
    lane = lax.broadcasted_iota(jnp.int32, (D, 128), 1)
    side = jnp.where(lane == 9, column, small[...])
    outs = dot_cols(attended[...], grad[...])
    for c in range(2):
        def put(ref):
            for z in range(8):
                for b in range(8):
                    rows = slice(b * 192 + z * 24, b * 192 + z * 24 + 24)
                    if c == 0:
                        block = into[rows, :384]
                    else:
                        block = jnp.concatenate([into[rows, 384:], side[rows]], axis=1)
                    ref[z, b] = block.astype(BF)
                for j in range(2):
                    for k in range(2):
                        block = outs[
                            j * 192 + z * 24 : j * 192 + z * 24 + 24,
                            c * 768 + k * 384 : c * 768 + (k + 1) * 384,
                        ]
                        ref[z, 8 + j * 2 + k] = block.astype(BF)

        @pl.when(core[0] == c)
        def _():
            put(keep)

        @pl.when(core[0] != c)
        def _():
            put(give)


def input_back_kernel(core, both, weight, own, below, above, far_up, far_down):
    back = dot_rows(both[...], weight[...]).astype(BF)
    for (at, size), piece in zip(PIECES, (own, below, above, far_up, far_down)):
        piece[...] = back[at : at + size]


def settle_experts_kernel(half, whole, expert_in, shared_in, expert_out, shared_out):
    for c in range(2):
        for x in range(4):
            e = c * 4 + x
            rows = slice(x * 24, (x + 1) * 24)
            low = whole[0, 0, c, rows, :896].astype(F32)
            high = whole[0, 1, c, rows, :896].astype(F32)
            expert_in[:, e, :896] = low
            expert_in[:, e, 896:] = high[:, :128]
            shared_in[:, e * 128 : (e + 1) * 128] = high[:, 128:256]
            shared_in[:, FS + e * 128 : FS + (e + 1) * 128] = high[:, 256:384]
            for k in range(3):
                expert_out[e, :, k * 512 : (k + 1) * 512] = high[k * 8 : (k + 1) * 8, 384:]
    for y in range(2):
        side = whole[0, y, half[0], :, 896:].astype(F32)
        for j in range(2):
            for b in range(2):
                for k in range(3):
                    at = (j * 2 + b) * 24 + k * 8
                    lanes = (y * 2 + j) * 384 + k * 128
                    shared_out[b * 8 : (b + 1) * 8, lanes : lanes + 128] = side[at : at + 8]


def settle_experts(half, whole):
    f32 = lambda *s: jax.ShapeDtypeStruct(s, F32)
    return pl.pallas_call(
        settle_experts_kernel,
        out_shape=(f32(192, EXPERTS, 1024), f32(192, 2 * FS), f32(8, 64, D), f32(128, D)),
        grid_spec=pltpu.PrefetchScalarGridSpec(
            num_scalar_prefetch=1,
            grid=(8,),
            in_specs=[pl.BlockSpec((1, 2, 2, 96, 1024), lambda z, *_: (z, 0, 0, 0, 0))],
            out_specs=(
                pl.BlockSpec((24, EXPERTS, 1024), lambda z, *_: (z, 0, 0)),
                pl.BlockSpec((24, 2 * FS), lambda z, *_: (z, 0)),
                pl.BlockSpec((8, 8, D), lambda z, *_: (0, z, 0)),
                pl.BlockSpec((16, D), lambda z, *_: (z, 0)),
            ),
        ),
        compiler_params=pltpu.CompilerParams(vmem_limit_bytes=56 << 20),
        cost_estimate=pl.CostEstimate(flops=0, bytes_accessed=19 << 20, transcendentals=0),
    )(half, whole)


def settle_kernel(core, mine, other, query, key, value, small, outs):
    def put(first, second):
        for z in range(8):
            rows = slice(z * 24, (z + 1) * 24)
            sums = jnp.zeros((24, 128), F32)
            for k, head in enumerate(KEY_HEAD):
                query[rows, head * 384 : (head + 1) * 384] = first[z, k].astype(F32)
                key[rows, head * 128 : (head + 1) * 128] = second[z, k, :, :128].astype(F32)
                value[rows, head * 128 : (head + 1) * 128] = second[z, k, :, 128:256].astype(F32)
                sums += second[z, k, :, 256:].astype(F32)
            small[rows] = sums
            for k in range(2):
                outs[rows, k * 384 : (k + 1) * 384] = first[z, 4 + k].astype(F32)
                outs[rows, (2 + k) * 384 : (3 + k) * 384] = second[z, 4 + k].astype(F32)

    @pl.when(core[0] == 0)
    def _():
        put(mine, other)

    @pl.when(core[0] == 1)
    def _():
        put(other, mine)


def shards(
    tokens,
    segment_ids,
    routes,
    gain_attn,
    w_query,
    w_key,
    w_value,
    w_out,
    gain_ffn,
    w_router,
    w_shared_in,
    w_shared_out,
    w_expert_in,
    w_expert_out,
    cotangent,
):
    level, core, half, place = (
        lax.axis_index(a).astype(jnp.uint32) for a in ("z", "core", "yhi", "x")
    )
    rows = tokens.shape[0]
    own = w_query.shape[0]

    member = half * 4 + place
    key_head = jnp.where((place == 1) | (place == 2), 3 - place, place)

    tokens_x = spread_x(tokens)
    at_core = core.reshape(1).astype(jnp.int32)
    small = jnp.concatenate([gain_attn[None], gain_ffn[None], w_router.T], axis=0)
    small = jnp.pad(small, ((0, 6), (0, 448)))
    (slots,) = on_chip(
        pack_kernel, at_core, (w_query, w_key, w_value, small), (out(8, 112, 640),)
    )
    got = exchange(slots, FSDP)
    small = got[:, 96:106, :192].transpose(1, 0, 2).reshape(10, D)
    gain_one = small[:1].astype(F32)
    gain_two = small[1:2].astype(F32)
    router = small[2:]

    w_out_late, *_ = lax.optimization_barrier((w_out, *tokens_x[1:3]))
    out_mine = lax.ppermute(
        w_out_late,
        ("core", "yhi", "x"),
        [(s * 8 + b, (b % 2) * 8 + s * 4 + KEY_HEAD[b // 2]) for s in range(2) for b in range(8)],
    )

    target = core * 4 + ((member - level + 8) & 3)
    block = jnp.concatenate(
        [
            lax.dynamic_index_in_dim(w_expert_in, target, 1, False),
            lax.dynamic_slice_in_dim(w_shared_in, target * 128, 128, 1),
            lax.dynamic_slice_in_dim(w_shared_in, FS + target * 128, 128, 1),
            lax.dynamic_index_in_dim(w_expert_out, target, 0, False)
            .reshape(64, 3, 512)
            .transpose(1, 0, 2)
            .reshape(192, 512),
        ],
        axis=1,
    )
    block, *_ = lax.optimization_barrier((block, *tokens_x[1:3]))
    block = lax.ppermute(
        block,
        ("z", *FSDP),
        [(z * 8 + b, z * 8 + (b - z) % 8) for z in range(8) for b in range(8)],
    )
    half_qkv, block, *_ = lax.optimization_barrier((got[:, :96], block, *tokens_x[3:]))
    qkv_other = swap_core(half_qkv)
    blocks = lax.all_gather(block, "z")
    inputs = tokens.astype(F32)
    normed_one, kv, w_qkv = on_chip(
        keys_kernel,
        at_core,
        (*tokens_x, gain_one, got, qkv_other),
        (out(512, D), out(512, 256), out(D, 640)),
        flops=2 * 512 * D * 256,
    )
    kv_other = lax.ppermute(kv, "yhi", [(0, 1)])
    (query,) = on_chip(
        query_kernel, at_core, (normed_one, w_qkv, kv), (out(512, 384),), flops=2 * 512 * D * 384
    )
    grad_late, shared_late, _ = lax.optimization_barrier((cotangent, w_shared_out, kv))
    grad_x = spread_x(grad_late)
    shared_other = lax.ppermute(shared_late, ("core", "yhi"), [(0, 1), (3, 2)])
    out_other = swap_core(after(out_mine, kv_other))
    starts = [((place + k) & 3) * 128 for k in (0, 3, 1, 2)]
    pos = jnp.concatenate([s.astype(jnp.int32) + jnp.arange(128, dtype=jnp.int32) for s in starts])
    seg_own = jnp.concatenate(
        [lax.dynamic_slice_in_dim(segment_ids, half * 512 + s, 128) for s in starts]
    )
    seg_other = jnp.concatenate([lax.dynamic_slice_in_dim(segment_ids, s, 128) for s in starts])
    pos_other = jnp.where(half == 1, pos - 512, 1 << 20)
    places = (
        pos[:, None],
        seg_own[:, None],
        jnp.concatenate([pos, pos_other])[None],
        jnp.concatenate([seg_own, seg_other])[None],
    )
    part = [out(size, D) for _, size in PIECES]
    attended, logs = on_chip(
        attend_kernel,
        at_core,
        (query, kv, kv_other, *places),
        (out(512, 384), out(512, 128, dtype=F32)),
        flops=2 * 512 * 384 * 2048,
        exps=3 * 512 * 1024,
    )
    hidden_part = on_chip(
        output_kernel,
        at_core,
        (after(attended, *grad_x[1:3], shared_other), out_mine, out_other),
        part,
        scratch=[pltpu.VMEM((384, D), BF)],
        flops=2 * 512 * 384 * D,
    )
    shared_down = jnp.where(core == half, w_shared_out, shared_other)
    grad_own = jnp.concatenate(grad_x, axis=0)
    grad_all = jnp.concatenate([grad_own, swap_core(grad_own)], axis=0)
    hidden = inputs + collect_x(hidden_part)

    unit_two, factor_two = normalize(hidden)
    normed_two = (unit_two * gain_two).astype(BF)
    logits = dot_rows(normed_two, router)
    chosen = jnp.sum(
        (routes[:, :, None] == jnp.arange(EXPERTS, dtype=jnp.int32)[None, None, :]).astype(F32),
        axis=1,
    )
    weighted = chosen * jnp.exp(logits)
    gates = weighted / jnp.sum(weighted, axis=-1, keepdims=True)
    packed = jnp.concatenate(
        [normed_two, *pair_of_float(gates), jnp.zeros((rows, 112), BF)], axis=1
    )
    packed = spread_x(after(packed, *grad_x[3:]))
    packed = (*packed, *(swap_core(p) for p in packed))

    back_own, back_other, mixed, grad_pre, normed_all, w_down = expert_pass(
        member, core * 4 + place, packed, grad_all, blocks, shared_down
    )
    back_other = swap_core(back_other)
    back_part = [plus(o, s) for o, s in zip(pieces_of(back_own), pieces_of(back_other))]
    normed_all, _, _ = lax.optimization_barrier((normed_all, back_part[3], back_part[4]))
    flat = expert_grads(normed_all, grad_pre, mixed, grad_all)
    back_sum, flat_ffn = collect_x(back_part, flat)

    grad_gates = back_sum[:, D : D + 8] + back_sum[:, D + 8 : D + 16]
    grad_logits = (
        gates * (grad_gates - jnp.sum(gates * grad_gates, axis=-1, keepdims=True))
    ).astype(BF)
    grad_normed_two = back_sum[:, :D] + dot(grad_logits, router)
    grad_router = dot_cols(normed_two, jnp.pad(grad_logits, ((0, 0), (0, 120))))
    grad_gain_ffn = jnp.sum(grad_normed_two * unit_two, axis=0, keepdims=True)
    grad_hidden = cotangent.astype(F32) + norm_back(
        grad_normed_two, unit_two, factor_two, gain_two
    )
    grad_hidden_low = grad_hidden.astype(BF)
    hidden_low = spread_x(grad_hidden_low)
    result_part = dot(after(mixed, grad_hidden_low), w_down).astype(BF)
    hidden_low = (after(hidden_low[0], result_part), *hidden_low[1:])

    grad_low, grad_query, grad_kv, to_other = on_chip(
        attend_back_kernel,
        at_core,
        (*hidden_low, query, kv, kv_other, *places, out_mine, out_other, logs),
        (out(512, D), out(512, 384), out(512, 256, dtype=F32), out(512, 256)),
        scratch=[pltpu.VMEM((384, D), BF)],
        flops=2 * 512 * 384 * 6656,
        exps=3 * 512 * 1024,
    )
    from_other = lax.ppermute(to_other, "yhi", [(1, 0)])
    result_other = swap_core(after(result_part[512:], to_other))
    from_other, result_other = lax.optimization_barrier((from_other, result_other))
    small = grad_router + jnp.pad(grad_gain_ffn.T, ((0, 0), (8, 119)))
    keep, give, grad_both = on_chip(
        weight_grads_kernel,
        at_core,
        (
            grad_query,
            grad_kv,
            from_other,
            w_qkv,
            normed_one,
            attended,
            grad_low,
            small,
            gain_one.reshape(D, 1),
        ),
        (out(8, 12, 24, 384), out(8, 12, 24, 384), out(512, 640)),
        flops=2 * 512 * D * 1024,
    )

    flat = plus(keep, swap_core(give))
    result_part = [
        plus(o, s)
        for o, s in zip(pieces_of(result_part[:512]), pieces_of(after(result_other, flat)))
    ]
    result = (hidden + collect_x(result_part)).astype(BF)
    flat = exchange(flat, "z")
    ffn = lax.psum_scatter(flat_ffn, "z", scatter_dimension=0, tiled=True)[0]
    ffn, flat, result = lax.optimization_barrier((ffn, flat, result))
    main = ffn[..., :1792].reshape(8, 24, 2, 896).transpose(2, 0, 1, 3).reshape(16, 24, 896)
    main = exchange(main, PLANE).reshape(4, 4, 24, 896)
    main = jnp.sum(main.astype(F32), axis=0).astype(BF).reshape(96, 896)
    side = ffn[..., 1792:].reshape(2, 96, 128)
    side = plus(side, lax.ppermute(side, ("core", "yhi"), [(1, 0), (2, 3)]))
    here = lax.axis_index("ylo").astype(jnp.uint32)
    away = lax.dynamic_index_in_dim(side, 1 - here, 0, False)
    away = lax.ppermute(away, "ylo", [(0, 1), (1, 0)])
    side = plus(lax.dynamic_index_in_dim(side, here, 0, False), away)
    piece, flat = lax.optimization_barrier((jnp.concatenate([main, side], axis=1), flat))
    whole = lax.all_gather(piece, REP).reshape(8, 2, 2, 96, 1024)
    at_half = half.reshape(1).astype(jnp.int32)
    sum_expert_in, sum_shared_in, sum_expert_out, sum_shared_out = settle_experts(at_half, whole)

    flat = jnp.sum(flat.astype(F32), axis=0).astype(BF)
    outs = lax.dynamic_update_slice(
        jnp.zeros((8, 2, 24, 384), BF), flat[8:].reshape(2, 2, 24, 384), (2 * key_head, *(jnp.uint32(0),) * 3)
    )
    flat = jnp.concatenate([flat[:8, None], outs], axis=1)
    flat = jnp.concatenate([flat, flat], axis=0)
    back_one = on_chip(
        input_back_kernel, at_core, (after(grad_both, flat), w_qkv), part, flops=2 * 512 * D * 640
    )
    got = exchange(flat, PLANE).reshape(4, 4, 3, 24, 384)
    got = jnp.sum(got.astype(F32), axis=0)
    mine = jnp.concatenate([got[:, 0], jnp.sum(got[:, 1:], axis=0)], axis=0).astype(BF)
    mine = spread_z(mine, level)
    mine, sum_shared_in, sum_shared_out, sum_expert_in, sum_expert_out = lax.optimization_barrier(
        (mine, sum_shared_in, sum_shared_out, sum_expert_in, sum_expert_out)
    )
    sum_query, sum_key, sum_value, small, sum_out = on_chip(
        settle_kernel,
        at_core,
        (mine, swap_core(mine)),
        (
            out(192, D, dtype=F32),
            out(192, 512, dtype=F32),
            out(192, 512, dtype=F32),
            out(192, 128, dtype=F32),
            out(192, D, dtype=F32),
        ),
    )

    back_one = collect_x(back_one)
    unit_own, factor_own = normalize(inputs)
    grad_input = (grad_hidden + norm_back(back_one, unit_own, factor_own, gain_one)).astype(BF)

    return (
        result,
        grad_input,
        small[:, 9],
        sum_query,
        sum_key,
        sum_value,
        sum_out,
        small[:, 8],
        small[:, :8],
        sum_shared_in,
        sum_shared_out,
        sum_expert_in,
        sum_expert_out,
    )


def solution(mesh):
    fine = Mesh(mesh.devices.reshape(SIZES), AXES)
    tokens = P((*REP, *FSDP), None)
    first = P(FSDP, None)
    return jax.shard_map(
        shards,
        mesh=fine,
        in_specs=(
            tokens,
            P(REP),
            tokens,
            P(FSDP),
            first,
            first,
            first,
            first,
            P(FSDP),
            first,
            first,
            first,
            P(FSDP, None, None),
            P(None, FSDP, None),
            tokens,
        ),
        out_specs=(
            tokens,
            tokens,
            P(FSDP),
            first,
            first,
            first,
            first,
            P(FSDP),
            first,
            first,
            first,
            P(FSDP, None, None),
            P(None, FSDP, None),
        ),
        check_vma=False,
    )
```

```python
import math

import jax
import jax.numpy as jnp
from jax import lax
from jax.experimental import pallas as pl
from jax.experimental.pallas import tpu as pltpu
from jax.sharding import Mesh, PartitionSpec as P

HEADS = 12
KV_HEADS = 4
HEAD = 128
GROUP = HEADS // KV_HEADS
D = 1536
FE = 512
FS = 1024
EXPERTS = 8
EPS = 1e-05
SCALE = 1.0 / math.sqrt(HEAD)

AXES = ("z", "ylo", "core", "yhi", "x")
SIZES = (8, 2, 2, 2, 4)
REP = ("z", "ylo", "core")
FSDP = ("yhi", "x")
PLANE = ("ylo", "yhi", "x")
KEY_HEAD = (0, 2, 1, 3)
BF = jnp.bfloat16
F32 = jnp.float32


def dot(left, right):
    return jnp.dot(left, right, preferred_element_type=F32)


def dot_rows(left, right):
    return lax.dot_general(left, right, (((1,), (1,)), ((), ())), preferred_element_type=F32)


def dot_cols(left, right):
    return lax.dot_general(left, right, (((0,), (0,)), ((), ())), preferred_element_type=F32)


def exchange(blocks, axes):
    return lax.all_to_all(blocks, axes, 0, 0, tiled=True)


def up_x(rows):
    return lax.ppermute(rows, "x", [(i, (i + 1) % 4) for i in range(4)])


def down_x(rows):
    return lax.ppermute(rows, "x", [(i, (i + 3) % 4) for i in range(4)])


def spread_x(rows):
    cut = rows.shape[0] // 2
    below, above = up_x(rows), down_x(rows)
    return rows, below, above, up_x(below[:cut]), down_x(above[cut:])


def pieces_of(rows):
    return tuple(rows[at : at + size] for at, size in PIECES)


def collect_x(pieces, beside=None):
    own, below, above, far_up, far_down = pieces
    cut = far_up.shape[0]
    far_up, far_down = up_x(far_up), down_x(far_down)
    above = jnp.concatenate([plus(above[:cut], far_up), above[cut:]], axis=0)
    below = jnp.concatenate([below[:cut], plus(below[cut:], far_down)], axis=0)
    if beside is not None:
        above, below, beside = lax.optimization_barrier((above, below, beside))
    total = own.astype(F32) + up_x(above).astype(F32) + down_x(below).astype(F32)
    return total if beside is None else (total, beside)


def plus(left, right):
    return (left.astype(F32) + right.astype(F32)).astype(BF)


def spread_z(rows, level):
    up = [(i, (i + 1) % 8) for i in range(8)]
    down = [(i, (i + 7) % 8) for i in range(8)]
    cut = rows.shape[0] // 2
    whole = jnp.zeros((8, *rows.shape), rows.dtype)
    rest = (jnp.uint32(0),) * (rows.ndim - 1)

    level = level.astype(jnp.int32)

    def put(whole, block, distance, start=0):
        return lax.dynamic_update_slice(
            whole,
            block[None],
            ((level + distance + 8 & 7).astype(jnp.uint32), jnp.uint32(start), *rest)
        )

    whole = put(whole, rows, 0)
    below = above = rows
    for k in (1, 2, 3):
        below, above = lax.ppermute(below, "z", up), lax.ppermute(above, "z", down)
        whole = put(put(whole, below, -k), above, k)
    whole = put(whole, lax.ppermute(below[:cut], "z", up), 4)
    return put(whole, lax.ppermute(above[cut:], "z", down), 4, cut)


def after(value, *others):
    return lax.optimization_barrier((value, *others))[0]


def after_all(values, *others):
    return lax.optimization_barrier((*values, *others))[: len(values)]


def swap_core(rows):
    return lax.ppermute(rows, "core", [(0, 1), (1, 0)])


def pair_of_float(values):
    high = values.astype(BF)
    return high, (values - high.astype(F32)).astype(BF)


def normalize(values):
    factor = lax.rsqrt(jnp.mean(values * values, axis=-1, keepdims=True) + EPS)
    return values * factor, factor


def norm_back(grad_normed, unit, factor, gain):
    scaled = grad_normed * gain
    inner = jnp.mean(scaled * unit, axis=-1, keepdims=True)
    return factor * (scaled - unit * inner)


def silu_slope(values, sig):
    return sig * (1.0 + values * (1.0 - sig))


def expert_kernel(member, own, below, above, far_up, far_down, own_o, below_o, above_o, far_up_o,
                  far_down_o, grad_own, grad_other, blocks, shared_mine, shared_other, back_own, back_other, mixed, grad_pre, normed, w_down,
                  w_in, rows):
    step = pl.program_id(0)

    @pl.when(step == 0)
    def _():
        for b in range(8):
            flip = (b >> 2) ^ (member[0] >> 2)
            first = flip * 4 + ((b - member[0]) & 3)
            second = (1 - flip) * 4 + ((b - member[0] - 2) & 3)
            w_in[b * 192 : (b + 1) * 192, :896] = blocks[first, :, :896]
            w_in[b * 192 : (b + 1) * 192, 896:] = blocks[second, :, 896:1280]
            for k in range(3):
                w_down[b * 64 : (b + 1) * 64, k * 512 : (k + 1) * 512] = blocks[
                    second, k * 64 : (k + 1) * 64, 1280:
                ]

        @pl.when(member[2] == 0)
        def _():
            w_down[FE:] = shared_other[...]

        @pl.when(member[2] != 0)
        def _():
            w_down[FE:] = shared_mine[...]

        at = 0
        for piece in (own, below, above, far_up, far_down, own_o, below_o, above_o, far_up_o,
                      far_down_o):
            rows[at : at + piece.shape[0]] = piece[...]
            at += piece.shape[0]

    part = pl.ds(pl.multiple_of(step * 256, 256), 256)
    x = rows[part, :D]
    lane = lax.broadcasted_iota(jnp.int32, (256, 128), 1)
    expert = member[1]
    high, low = lane == expert, lane == expert + 8
    gate = jnp.sum(
        jnp.where(high | low, rows[part, D:].astype(F32), 0.0), axis=1, keepdims=True
    )
    back_down = dot_rows(jnp.where(step < 2, grad_own[...], grad_other[...]), w_down[...])
    pre = dot(x, w_in[...])
    gate_part, up_part = pre[:, :FE], pre[:, FE : 2 * FE]
    shared_gate, shared_up = pre[:, 2 * FE : 2 * FE + 128], pre[:, 2 * FE + 128 :]
    gate_sig = jax.nn.sigmoid(gate_part)
    gate_act = gate_part * gate_sig
    activ = gate_act * up_part
    shared_sig = jax.nn.sigmoid(shared_gate)
    shared_silu = shared_gate * shared_sig
    grad_mixed, grad_shared = back_down[:, :FE], back_down[:, FE:]
    grad_gate = jnp.sum(grad_mixed * activ, axis=1, keepdims=True)
    grad_activ = grad_mixed * gate
    mixed[:, :FE] = (gate * activ).astype(BF)
    mixed[:, FE:] = (shared_silu * shared_up).astype(BF)
    grad_pre[:, :FE] = (grad_activ * up_part * silu_slope(gate_part, gate_sig)).astype(BF)
    grad_pre[:, FE : 2 * FE] = (grad_activ * gate_act).astype(BF)
    grad_pre[:, 2 * FE : 2 * FE + 128] = (
        grad_shared * shared_up * silu_slope(shared_gate, shared_sig)
    ).astype(BF)
    grad_pre[:, 2 * FE + 128 :] = (grad_shared * shared_silu).astype(BF)
    normed[...] = x
    back = dot_rows(grad_pre[...], w_in[...]).astype(BF)
    top = grad_gate.astype(BF).astype(F32)
    tail = jnp.where(high, top, jnp.where(low, grad_gate - top, 0.0)).astype(BF)

    @pl.when(step < 2)
    def _():
        back_own[:, :D], back_own[:, D:] = back, tail

    @pl.when(step >= 2)
    def _():
        back_other[:, :D], back_other[:, D:] = back, tail


def lower_chunk(n):
    return pl.BlockSpec((256, n), lambda i, *_: (jnp.minimum(i, 1), 0))


def upper_chunk(n):
    return pl.BlockSpec((256, n), lambda i, *_: (jnp.maximum(i - 2, 0), 0))


def expert_pass(scalars, pieces, grad_own, grad_other, blocks, shared_mine, shared_other):
    whole = lambda a: pl.BlockSpec(a.shape, lambda i, *_, n=a.ndim: (0,) * n)
    chunk = lambda n: pl.BlockSpec((256, n), lambda i, *_: (i, 0))
    shape = lambda n, rows=1024: jax.ShapeDtypeStruct((rows, n), BF)
    return pl.pallas_call(
        expert_kernel,
        out_shape=(shape(1664, 512), shape(1664, 512), shape(640), shape(1280), shape(D), shape(D, 640)),
        grid_spec=pltpu.PrefetchScalarGridSpec(
            num_scalar_prefetch=1,
            grid=(4,),
            in_specs=[
                *(whole(p) for p in pieces),
                lower_chunk(D),
                upper_chunk(D),
                whole(blocks),
                whole(shared_mine),
                whole(shared_other),
            ],
            out_specs=(
                lower_chunk(1664),
                upper_chunk(1664),
                chunk(640),
                chunk(1280),
                chunk(D),
                pl.BlockSpec((640, D), lambda i, *_: (0, 0)),
            ),
            scratch_shapes=[
                pltpu.VMEM((D, 1280), BF),
                pltpu.VMEM((1024, 1664), BF),
            ],
        ),
        compiler_params=pltpu.CompilerParams(vmem_limit_bytes=56 << 20),
        cost_estimate=pl.CostEstimate(
            flops=2 * 1024 * D * 3200, bytes_accessed=30 << 20, transcendentals=1024 * 640
        ),
    )(scalars, *pieces, grad_own, grad_other, blocks, shared_mine, shared_other)


def expert_grad_kernel(normed, grad_pre, mixed, shared, own, other, own_cols, other_cols, out):
    into = dot_cols(normed[...], grad_pre[...])
    down = dot_cols(mixed[:512], own[...]) + dot_cols(mixed[512:], other[...])
    side = dot_cols(shared[:512], own_cols[...]) + dot_cols(shared[512:], other_cols[...])
    for b in range(2):
        for z in range(8):
            at = b * 64 + z * 8
            folded = jnp.concatenate(
                [down[at : at + 8, k * 512 : (k + 1) * 512] for k in range(3)], axis=0
            )
            mine = jnp.concatenate(
                [side[z * 16 + b * 8 : z * 16 + b * 8 + 8, k * 128 : (k + 1) * 128] for k in range(3)],
                axis=0,
            )
            out[z, b] = jnp.concatenate(
                [
                    into[b * 192 + z * 24 : b * 192 + z * 24 + 24],
                    folded,
                    mine,
                ],
                axis=1,
            ).astype(BF)


def expert_grads(normed, grad_pre, mixed, grad_own, grad_other):
    return pl.pallas_call(
        expert_grad_kernel,
        out_shape=jax.ShapeDtypeStruct((8, 8, 24, 1920), BF),
        grid=(4,),
        in_specs=[
            pl.BlockSpec((1024, 384), lambda j: (0, j)),
            pl.BlockSpec((1024, 1280), lambda j: (0, 0)),
            pl.BlockSpec((1024, 128), lambda j: (0, j)),
            pl.BlockSpec((1024, 128), lambda j: (0, 4)),
            pl.BlockSpec((512, D), lambda j: (0, 0)),
            pl.BlockSpec((512, D), lambda j: (0, 0)),
            pl.BlockSpec((512, 384), lambda j: (0, j)),
            pl.BlockSpec((512, 384), lambda j: (0, j)),
        ],
        out_specs=pl.BlockSpec((8, 2, 24, 1920), lambda j: (0, j, 0, 0)),
        compiler_params=pltpu.CompilerParams(vmem_limit_bytes=56 << 20),
        cost_estimate=pl.CostEstimate(
            flops=2 * 1024 * D * 1920, bytes_accessed=22 << 20, transcendentals=0
        ),
    )(normed, grad_pre, mixed, mixed, grad_own, grad_other, grad_own, grad_other)


def full(a):
    return pl.BlockSpec(a.shape, lambda *_, n=len(a.shape): (0,) * n)


def on_chip(kernel, scalars, args, outs, scratch=(), flops=0, exps=0):
    size = sum(math.prod(a.shape) * a.dtype.itemsize for a in (*args, *outs))
    return pl.pallas_call(
        kernel,
        out_shape=tuple(outs),
        grid_spec=pltpu.PrefetchScalarGridSpec(
            num_scalar_prefetch=1,
            grid=(1,),
            in_specs=[full(a) for a in args],
            out_specs=tuple(full(a) for a in outs),
            scratch_shapes=list(scratch),
        ),
        compiler_params=pltpu.CompilerParams(vmem_limit_bytes=56 << 20),
        cost_estimate=pl.CostEstimate(flops=flops, bytes_accessed=size, transcendentals=exps),
    )(scalars, *args)


def out(*shape, dtype=BF):
    return jax.ShapeDtypeStruct(shape, dtype)


PIECES = ((0, 128), (128, 128), (256, 128), (384, 64), (448, 64))


def pack_kernel(core, query, key, value, small, slots):
    rows = pl.ds(pl.multiple_of(core[0] * 96, 32), 96)
    for k, head in enumerate(KEY_HEAD):
        for slot in (k, k + 4):
            slots[slot, :96, :384] = query[rows, head * 384 : (head + 1) * 384]
            slots[slot, :96, 384:512] = key[rows, head * 128 : (head + 1) * 128]
            slots[slot, :96, 512:] = value[rows, head * 128 : (head + 1) * 128]
            slots[slot, 96:] = small[...]


def keys_kernel(core, own, below, above, far_up, far_down, gain, got, other, normed, kv, weight):
    for b in range(8):
        first = pl.multiple_of(b * 192 + core[0] * 96, 32)
        second = pl.multiple_of(b * 192 + (1 - core[0]) * 96, 32)
        weight[pl.ds(first, 96)] = got[b, :96]
        weight[pl.ds(second, 96)] = other[b]
    for (at, size), piece in zip(PIECES, (own, below, above, far_up, far_down)):
        unit, _ = normalize(piece[...].astype(F32))
        normed[at : at + size] = (unit * gain[...]).astype(BF)
    kv[...] = dot(normed[...], weight[:, GROUP * HEAD :]).astype(BF)


def query_kernel(core, normed, weight, kv, query):
    query[...] = dot(normed[...], weight[:, : GROUP * HEAD]).astype(BF)


def mask_of(query_at, query_seg, key_at, key_seg):
    return (query_at == key_at) | (
        (key_at < query_at) & (query_seg == key_seg) & (key_seg != 0)
    )


def attend_kernel(core, query, kv, kv_other, qat, qseg, kat, kseg, attended, logs):
    allowed = mask_of(qat[...], qseg[...], kat[...], kseg[...])
    keys = jnp.concatenate([kv[:, :HEAD], kv_other[:, :HEAD]], axis=0)
    values = jnp.concatenate([kv[:, HEAD:], kv_other[:, HEAD:]], axis=0)
    lane = lax.broadcasted_iota(jnp.int32, (512, 128), 1)
    kept = jnp.zeros((512, 128), F32)
    for g in range(GROUP):
        scores = dot_rows(query[:, g * HEAD : (g + 1) * HEAD], keys) * SCALE
        scores = jnp.where(allowed, scores, -1e30)
        top = jnp.max(scores, axis=1, keepdims=True)
        expo = jnp.exp(scores - top)
        total = jnp.sum(expo, axis=1, keepdims=True)
        kept = jnp.where(lane == g, top + jnp.log(total), kept)
        attended[:, g * HEAD : (g + 1) * HEAD] = dot((expo / total).astype(BF), values).astype(BF)
    logs[...] = kept


def output_kernel(core, attended, mine, other, own, below, above, far_up, far_down, weight):
    for c in range(2):
        @pl.when(core[0] == c)
        def _():
            weight[c * 192 : (c + 1) * 192] = mine[...]
            weight[(1 - c) * 192 : (2 - c) * 192] = other[...]
    whole = dot(attended[...], weight[...]).astype(BF)
    for (at, size), piece in zip(PIECES, (own, below, above, far_up, far_down)):
        piece[...] = whole[at : at + size]


def attend_back_kernel(core, own, below, above, far_up, far_down, query, kv, kv_other, qat, qseg, kat, kseg,
                       mine, other, logs, grad, grad_query, grad_own, grad_other, weight):
    for c in range(2):
        @pl.when(core[0] == c)
        def _():
            weight[c * 192 : (c + 1) * 192] = mine[...]
            weight[(1 - c) * 192 : (2 - c) * 192] = other[...]
    for (at, size), piece in zip(PIECES, (own, below, above, far_up, far_down)):
        grad[at : at + size] = piece[...]
    grad_att = dot_rows(grad[...], weight[...]).astype(BF)
    allowed = mask_of(qat[...], qseg[...], kat[...], kseg[...])
    keys = jnp.concatenate([kv[:, :HEAD], kv_other[:, :HEAD]], axis=0)
    values = jnp.concatenate([kv[:, HEAD:], kv_other[:, HEAD:]], axis=0)
    grad_keys = jnp.zeros((1024, HEAD), F32)
    grad_values = jnp.zeros((1024, HEAD), F32)
    for g in range(GROUP):
        queries = query[:, g * HEAD : (g + 1) * HEAD]
        heads = grad_att[:, g * HEAD : (g + 1) * HEAD]
        scores = jnp.where(allowed, dot_rows(queries, keys) * SCALE, -1e30)
        probs = jnp.exp(scores - logs[:, g : g + 1])
        grad_probs = dot_rows(heads, values)
        inner = jnp.sum(probs * grad_probs, axis=1, keepdims=True)
        grad_scores = (probs * (grad_probs - inner)).astype(BF)
        grad_query[:, g * HEAD : (g + 1) * HEAD] = (dot(grad_scores, keys) * SCALE).astype(BF)
        grad_keys += dot_cols(grad_scores, queries)
        grad_values += dot_cols(probs.astype(BF), heads)
    grad_keys = grad_keys * SCALE
    grad_own[:, :HEAD] = grad_keys[:512]
    grad_own[:, HEAD:] = grad_values[:512]
    grad_other[:, :HEAD] = grad_keys[512:].astype(BF)
    grad_other[:, HEAD:] = grad_values[512:].astype(BF)


def weight_grads_kernel(core, grad_query, grad_kv, from_other, weight, normed, attended, grad, small,
                        gain, keep, give, both):
    both[:, : GROUP * HEAD] = grad_query[...]
    both[:, GROUP * HEAD :] = (grad_kv[...] + from_other[...].astype(F32)).astype(BF)
    into = dot_cols(normed[...], both[...])
    column = jnp.sum(into * weight[...].astype(F32), axis=1, keepdims=True) / gain[...]
    lane = lax.broadcasted_iota(jnp.int32, (D, 128), 1)
    side = jnp.where(lane == 9, column, small[...])
    outs = dot_cols(attended[...], grad[...])
    for c in range(2):
        def put(ref):
            for z in range(8):
                for b in range(8):
                    rows = slice(b * 192 + z * 24, b * 192 + z * 24 + 24)
                    if c == 0:
                        block = into[rows, :384]
                    else:
                        block = jnp.concatenate([into[rows, 384:], side[rows]], axis=1)
                    ref[z, b] = block.astype(BF)
                for j in range(2):
                    for k in range(2):
                        block = outs[
                            j * 192 + z * 24 : j * 192 + z * 24 + 24,
                            c * 768 + k * 384 : c * 768 + (k + 1) * 384,
                        ]
                        ref[z, 8 + j * 2 + k] = block.astype(BF)

        @pl.when(core[0] == c)
        def _():
            put(keep)

        @pl.when(core[0] != c)
        def _():
            put(give)


def input_back_kernel(core, both, weight, own, below, above, far_up, far_down):
    back = dot_rows(both[...], weight[...]).astype(BF)
    for (at, size), piece in zip(PIECES, (own, below, above, far_up, far_down)):
        piece[...] = back[at : at + size]


def settle_experts_kernel(half, whole, expert_in, shared_in, expert_out, shared_out):
    low = [whole[0, 0, e // 4, e % 4, :, :896].astype(F32) for e in range(8)]
    high = [whole[0, 1, e // 4, e % 4, :, :896].astype(F32) for e in range(8)]
    expert_in[:, :, :896] = jnp.transpose(jnp.stack(low), (1, 0, 2))
    expert_in[:, :, 896:] = jnp.transpose(jnp.stack([h[:, :128] for h in high]), (1, 0, 2))
    for e in range(8):
        shared_in[:, e * 128 : (e + 1) * 128] = high[e][:, 128:256]
        shared_in[:, FS + e * 128 : FS + (e + 1) * 128] = high[e][:, 256:384]
        for k in range(3):
            expert_out[e, :, k * 512 : (k + 1) * 512] = high[e][k * 8 : (k + 1) * 8, 384:]
    for y in range(2):
        for j in range(4):
            side = whole[0, y, half[0], j, :, 896:].astype(F32)
            for k in range(3):
                lanes = j * 384 + k * 128
                shared_out[y * 8 : (y + 1) * 8, lanes : lanes + 128] = side[k * 8 : (k + 1) * 8]


def settle_experts(half, whole):
    f32 = lambda *s: jax.ShapeDtypeStruct(s, F32)
    return pl.pallas_call(
        settle_experts_kernel,
        out_shape=(f32(192, EXPERTS, 1024), f32(192, 2 * FS), f32(8, 64, D), f32(128, D)),
        grid_spec=pltpu.PrefetchScalarGridSpec(
            num_scalar_prefetch=1,
            grid=(8,),
            in_specs=[pl.BlockSpec((1, 2, 2, 4, 24, 1024), lambda z, *_: (z,) + (0,) * 5)],
            out_specs=(
                pl.BlockSpec((24, EXPERTS, 1024), lambda z, *_: (z, 0, 0)),
                pl.BlockSpec((24, 2 * FS), lambda z, *_: (z, 0)),
                pl.BlockSpec((8, 8, D), lambda z, *_: (0, z, 0)),
                pl.BlockSpec((16, D), lambda z, *_: (z, 0)),
            ),
        ),
        compiler_params=pltpu.CompilerParams(vmem_limit_bytes=56 << 20),
        cost_estimate=pl.CostEstimate(flops=0, bytes_accessed=19 << 20, transcendentals=0),
    )(half, whole)


def piece_kernel(place, same, below, above, across, side, piece):
    for ref, distance in ((same, 0), (below, 3), (above, 1), (across, 2)):
        piece[lax.rem(place[0] + distance, 4), :, :896] = ref[...]
    piece[:, :, 896:] = side[...]


def settle_kernel(core, mine, other, query, key, value, small, outs):
    def put(first, second):
        for z in range(8):
            rows = slice(z * 24, (z + 1) * 24)
            sums = jnp.zeros((24, 128), F32)
            for k, head in enumerate(KEY_HEAD):
                query[rows, head * 384 : (head + 1) * 384] = first[z, k].astype(F32)
                key[rows, head * 128 : (head + 1) * 128] = second[z, k, :, :128].astype(F32)
                value[rows, head * 128 : (head + 1) * 128] = second[z, k, :, 128:256].astype(F32)
                sums += second[z, k, :, 256:].astype(F32)
            small[rows] = sums
            for k in range(2):
                outs[rows, k * 384 : (k + 1) * 384] = first[z, 4 + k].astype(F32)
                outs[rows, (2 + k) * 384 : (3 + k) * 384] = second[z, 4 + k].astype(F32)

    @pl.when(core[0] == 0)
    def _():
        put(mine, other)

    @pl.when(core[0] == 1)
    def _():
        put(other, mine)


def shards(
    tokens,
    segment_ids,
    routes,
    gain_attn,
    w_query,
    w_key,
    w_value,
    w_out,
    gain_ffn,
    w_router,
    w_shared_in,
    w_shared_out,
    w_expert_in,
    w_expert_out,
    cotangent,
):
    level, core, half, place = (
        lax.axis_index(a).astype(jnp.uint32) for a in ("z", "core", "yhi", "x")
    )
    rows = tokens.shape[0]
    zero = jnp.uint32(0)

    member = half * 4 + place
    key_head = jnp.where((place == 1) | (place == 2), 3 - place, place)

    tokens_x = spread_x(tokens)
    at_core = core.reshape(1).astype(jnp.int32)
    small = jnp.concatenate([gain_attn[None], gain_ffn[None], w_router.T], axis=0)
    small = jnp.pad(small, ((0, 6), (0, 448)))
    (slots,) = on_chip(
        pack_kernel, at_core, (w_query, w_key, w_value, small), (out(8, 112, 640),)
    )
    got = exchange(slots, FSDP)
    small = got[:, 96:106, :192].transpose(1, 0, 2).reshape(10, D)
    gain_one = small[:1].astype(F32)
    gain_two = small[1:2].astype(F32)
    router = small[2:]

    w_out_late, *_ = lax.optimization_barrier((w_out, *tokens_x[1:3]))
    out_mine = lax.ppermute(
        w_out_late,
        ("core", "yhi", "x"),
        [(s * 8 + b, (b % 2) * 8 + s * 4 + KEY_HEAD[b // 2]) for s in range(2) for b in range(8)],
    )

    qkv_other = swap_core(after(got[:, :96], *tokens_x[3:]))
    turn, flip = level & 3, level >> 2
    first, second = core * 4 + ((place - turn) & 3), core * 4 + ((place - turn - 2) & 3)
    halves = (
        lax.dynamic_slice(w_expert_in, (zero, first, zero), (192, 1, 896)).reshape(192, 896),
        jnp.concatenate(
            [
                lax.dynamic_slice(w_expert_in, (zero, second, zero + 896), (192, 1, 128)).reshape(
                    192, 128
                ),
                lax.dynamic_slice(w_shared_in, (zero, second * 128), (192, 128)),
                lax.dynamic_slice(w_shared_in, (zero, second * 128 + FS), (192, 128)),
                lax.dynamic_slice(w_expert_out, (second, zero, zero), (1, 64, D))
                .reshape(64, 3, 512)
                .transpose(1, 0, 2)
                .reshape(192, 512),
            ],
            axis=1,
        ),
    )
    halves = after_all(halves, slots)
    halves = [
        lax.ppermute(
            part,
            ("z", *FSDP),
            [
                (z * 8 + h * 4 + x, z * 8 + (h ^ (z >> 2) ^ k) * 4 + ((x - z - 2 * k) & 3))
                for z in range(8)
                for h in range(2)
                for x in range(4)
            ],
        )
        for k, part in enumerate(halves)
    ]
    block = after(jnp.concatenate(halves, axis=1), got, *tokens_x[3:])
    blocks = lax.all_gather(block, "z")
    inputs = tokens.astype(F32)
    normed_one, kv, w_qkv = on_chip(
        keys_kernel,
        at_core,
        (*tokens_x, gain_one, got, qkv_other),
        (out(512, D), out(512, 256), out(D, 640)),
        flops=2 * 512 * D * 256,
    )
    kv_other = lax.ppermute(kv, "yhi", [(0, 1)])
    (query,) = on_chip(
        query_kernel, at_core, (normed_one, w_qkv, kv), (out(512, 384),), flops=2 * 512 * D * 384
    )
    grad_late, shared_late, _ = lax.optimization_barrier((cotangent, w_shared_out, kv))
    grad_x = spread_x(grad_late)
    shared_other = lax.ppermute(shared_late, ("core", "yhi"), [(0, 1), (3, 2)])
    out_other = swap_core(after(out_mine, kv_other))
    starts = [((place + k) & 3) * 128 for k in (0, 3, 1, 2)]
    pos = jnp.concatenate([s.astype(jnp.int32) + jnp.arange(128, dtype=jnp.int32) for s in starts])
    seg_own = jnp.concatenate(
        [lax.dynamic_slice_in_dim(segment_ids, half * 512 + s, 128) for s in starts]
    )
    seg_other = jnp.concatenate([lax.dynamic_slice_in_dim(segment_ids, s, 128) for s in starts])
    pos_other = jnp.where(half == 1, pos - 512, 1 << 20)
    places = (
        pos[:, None],
        seg_own[:, None],
        jnp.concatenate([pos, pos_other])[None],
        jnp.concatenate([seg_own, seg_other])[None],
    )
    part = [out(size, D) for _, size in PIECES]
    attended, logs = on_chip(
        attend_kernel,
        at_core,
        (query, kv, kv_other, *places),
        (out(512, 384), out(512, 128, dtype=F32)),
        flops=2 * 512 * 384 * 2048,
        exps=3 * 512 * 1024,
    )
    hidden_part = on_chip(
        output_kernel,
        at_core,
        (after(attended, *grad_x[1:3], shared_other), out_mine, out_other),
        part,
        scratch=[pltpu.VMEM((384, D), BF)],
        flops=2 * 512 * 384 * D,
    )
    grad_own = jnp.concatenate(grad_x, axis=0)
    grad_other = swap_core(grad_own)
    hidden = inputs + collect_x(hidden_part)

    unit_two, factor_two = normalize(hidden)
    normed_two = (unit_two * gain_two).astype(BF)
    logits = dot_rows(normed_two, router)
    chosen = jnp.sum(
        (routes[:, :, None] == jnp.arange(EXPERTS, dtype=jnp.int32)[None, None, :]).astype(F32),
        axis=1,
    )
    weighted = chosen * jnp.exp(logits)
    gates = weighted / jnp.sum(weighted, axis=-1, keepdims=True)
    packed = jnp.concatenate(
        [normed_two, *pair_of_float(gates), jnp.zeros((rows, 112), BF)], axis=1
    )
    packed = spread_x(after(packed, *grad_x[3:]))
    packed = (*packed, *(swap_core(p) for p in packed))

    scalars = jnp.stack([member, core * 4 + place, (core == half).astype(jnp.uint32)])
    back_own, back_other, mixed, grad_pre, normed_all, w_down = expert_pass(
        scalars.astype(jnp.int32), packed, grad_own, grad_other, blocks, w_shared_out, shared_other
    )
    back_other = swap_core(back_other)
    back_part = [plus(o, s) for o, s in zip(pieces_of(back_own), pieces_of(back_other))]
    normed_all, _, _ = lax.optimization_barrier((normed_all, back_part[3], back_part[4]))
    flat = expert_grads(normed_all, grad_pre, mixed, grad_own, grad_other)
    back_sum, flat_ffn = collect_x(back_part, flat)

    grad_gates = back_sum[:, D : D + 8] + back_sum[:, D + 8 : D + 16]
    grad_logits = (
        gates * (grad_gates - jnp.sum(gates * grad_gates, axis=-1, keepdims=True))
    ).astype(BF)
    grad_normed_two = back_sum[:, :D] + dot(grad_logits, router)
    grad_router = dot_cols(normed_two, jnp.pad(grad_logits, ((0, 0), (0, 120))))
    grad_gain_ffn = jnp.sum(grad_normed_two * unit_two, axis=0, keepdims=True)
    grad_hidden = cotangent.astype(F32) + norm_back(
        grad_normed_two, unit_two, factor_two, gain_two
    )
    grad_hidden_low = grad_hidden.astype(BF)
    hidden_low = spread_x(grad_hidden_low)
    result_part = dot(after(mixed, grad_hidden_low), w_down).astype(BF)
    hidden_low = (after(hidden_low[0], result_part), *hidden_low[1:])

    grad_low, grad_query, grad_kv, to_other = on_chip(
        attend_back_kernel,
        at_core,
        (*hidden_low, query, kv, kv_other, *places, out_mine, out_other, logs),
        (out(512, D), out(512, 384), out(512, 256, dtype=F32), out(512, 256)),
        scratch=[pltpu.VMEM((384, D), BF)],
        flops=2 * 512 * 384 * 6656,
        exps=3 * 512 * 1024,
    )
    from_other = lax.ppermute(to_other, "yhi", [(1, 0)])
    result_other = swap_core(after(result_part[512:], to_other))
    from_other, result_other = lax.optimization_barrier((from_other, result_other))
    small = grad_router + jnp.pad(grad_gain_ffn.T, ((0, 0), (8, 119)))
    keep, give, grad_both = on_chip(
        weight_grads_kernel,
        at_core,
        (
            grad_query,
            grad_kv,
            from_other,
            w_qkv,
            normed_one,
            attended,
            grad_low,
            small,
            gain_one.reshape(D, 1),
        ),
        (out(8, 12, 24, 384), out(8, 12, 24, 384), out(512, 640)),
        flops=2 * 512 * D * 1024,
    )

    flat = plus(keep, swap_core(give))
    flat_sent = flat
    flat = exchange(flat, "z")
    ffn = lax.psum_scatter(flat_ffn, "z", scatter_dimension=0, tiled=True)[0]
    ffn = after(ffn, flat_sent)
    side = ffn[..., 1792:].reshape(4, 2, 24, 128)
    main = ffn[..., :1792].reshape(2, 4, 24, 1792)
    both = [
        jnp.concatenate([m[..., :896], side[:, 0], m[..., 896:], side[:, 1]], axis=-1)
        for m in (main[0], main[1])
    ]
    keep = jnp.where(half == 0, both[0], both[1])
    away = jnp.where(half == 0, both[1], both[0])
    ffn = plus(keep, lax.ppermute(away, "yhi", [(0, 1), (1, 0)]))
    here = lax.axis_index("ylo")
    keep = jnp.where(here == 0, ffn[..., :1024], ffn[..., 1024:])
    away = jnp.where(here == 0, ffn[..., 1024:], ffn[..., :1024])
    ffn = plus(keep, lax.ppermute(away, "ylo", [(0, 1), (1, 0)]))
    to = [
        lax.dynamic_index_in_dim(ffn[..., :896], (place + k) & 3, 0, False) for k in (0, 1, 3, 2)
    ]
    across = lax.ppermute(to[3], "x", [(i, (i + 2) % 4) for i in range(4)])
    (piece,) = on_chip(
        piece_kernel,
        place.reshape(1).astype(jnp.int32),
        (to[0], up_x(to[1]), down_x(to[2]), across, ffn[..., 896:]),
        (out(4, 24, 1024),),
    )
    whole = lax.all_gather(after(piece, flat), REP).reshape(8, 2, 2, 4, 24, 1024)
    at_half = half.reshape(1).astype(jnp.int32)
    sum_expert_in, sum_shared_in, sum_expert_out, sum_shared_out = settle_experts(at_half, whole)

    flat = jnp.sum(flat.astype(F32), axis=0).astype(BF)
    outs = lax.dynamic_update_slice(
        jnp.zeros((8, 2, 24, 384), BF), flat[8:].reshape(2, 2, 24, 384), (2 * key_head, *(jnp.uint32(0),) * 3)
    )
    flat = jnp.concatenate([flat[:8, None], outs], axis=1)
    flat = jnp.concatenate([flat, flat], axis=0)
    back_one = on_chip(
        input_back_kernel, at_core, (after(grad_both, flat), w_qkv), part, flops=2 * 512 * D * 640
    )
    result_part = [
        plus(o, s)
        for o, s in zip(pieces_of(result_part[:512]), pieces_of(after(result_other, flat)))
    ]
    result = (hidden + collect_x(result_part)).astype(BF)
    got = exchange(flat, PLANE).reshape(4, 4, 3, 24, 384)
    got = jnp.sum(got.astype(F32), axis=0)
    mine = jnp.concatenate([got[:, 0], jnp.sum(got[:, 1:], axis=0)], axis=0).astype(BF)
    mine = spread_z(mine, level)
    mine, sum_shared_in, sum_shared_out, sum_expert_in, sum_expert_out = lax.optimization_barrier(
        (mine, sum_shared_in, sum_shared_out, sum_expert_in, sum_expert_out)
    )
    sum_query, sum_key, sum_value, small, sum_out = on_chip(
        settle_kernel,
        at_core,
        (mine, swap_core(mine)),
        (
            out(192, D, dtype=F32),
            out(192, 512, dtype=F32),
            out(192, 512, dtype=F32),
            out(192, 128, dtype=F32),
            out(192, D, dtype=F32),
        ),
    )

    back_one = collect_x(back_one)
    unit_own, factor_own = normalize(inputs)
    grad_input = (grad_hidden + norm_back(back_one, unit_own, factor_own, gain_one)).astype(BF)

    return (
        result,
        grad_input,
        small[:, 9],
        sum_query,
        sum_key,
        sum_value,
        sum_out,
        small[:, 8],
        small[:, :8],
        sum_shared_in,
        sum_shared_out,
        sum_expert_in,
        sum_expert_out,
    )


def solution(mesh):
    fine = Mesh(mesh.devices.reshape(SIZES), AXES)
    tokens = P((*REP, *FSDP), None)
    first = P(FSDP, None)
    return jax.shard_map(
        shards,
        mesh=fine,
        in_specs=(
            tokens,
            P(REP),
            tokens,
            P(FSDP),
            first,
            first,
            first,
            first,
            P(FSDP),
            first,
            first,
            first,
            P(FSDP, None, None),
            P(None, FSDP, None),
            tokens,
        ),
        out_specs=(
            tokens,
            tokens,
            P(FSDP),
            first,
            first,
            first,
            first,
            P(FSDP),
            first,
            first,
            first,
            P(FSDP, None, None),
            P(None, FSDP, None),
        ),
        check_vma=False,
    )
```

```python
import math

import jax
import jax.numpy as jnp
from jax import lax
from jax.experimental import pallas as pl
from jax.experimental.pallas import tpu as pltpu
from jax.sharding import Mesh, PartitionSpec as P

HEADS = 12
KV_HEADS = 4
HEAD = 128
GROUP = HEADS // KV_HEADS
D = 1536
FE = 512
FS = 1024
EXPERTS = 8
EPS = 1e-05
SCALE = 1.0 / math.sqrt(HEAD)

AXES = ("z", "ylo", "core", "yhi", "x")
SIZES = (8, 2, 2, 2, 4)
REP = ("z", "ylo", "core")
FSDP = ("yhi", "x")
PLANE = ("ylo", "yhi", "x")
KEY_HEAD = (0, 2, 1, 3)
BF = jnp.bfloat16
F32 = jnp.float32


def dot(left, right):
    return jnp.dot(left, right, preferred_element_type=F32)


def dot_rows(left, right):
    return lax.dot_general(left, right, (((1,), (1,)), ((), ())), preferred_element_type=F32)


def dot_cols(left, right):
    return lax.dot_general(left, right, (((0,), (0,)), ((), ())), preferred_element_type=F32)


def exchange(blocks, axes):
    return lax.all_to_all(blocks, axes, 0, 0, tiled=True)


def up_x(rows):
    return lax.ppermute(rows, "x", [(i, (i + 1) % 4) for i in range(4)])


def down_x(rows):
    return lax.ppermute(rows, "x", [(i, (i + 3) % 4) for i in range(4)])


def spread_x(rows):
    cut = rows.shape[0] // 2
    below, above = up_x(rows), down_x(rows)
    return rows, below, above, up_x(below[:cut]), down_x(above[cut:])


def pieces_of(rows):
    return tuple(rows[at : at + size] for at, size in PIECES)


def collect_x(pieces, beside=None, gate=None):
    own, below, above, far_up, far_down = pieces
    cut = far_up.shape[0]
    far_up, far_down = up_x(far_up), down_x(far_down)
    above = jnp.concatenate([plus(above[:cut], far_up), above[cut:]], axis=0)
    below = jnp.concatenate([below[:cut], plus(below[cut:], far_down)], axis=0)
    if gate is not None:
        above, below = after_all((above, below), gate)
    if beside is not None:
        above, below, beside = lax.optimization_barrier((above, below, beside))
    total = own.astype(F32) + up_x(above).astype(F32) + down_x(below).astype(F32)
    return total if beside is None else (total, beside)


def plus(left, right):
    return (left.astype(F32) + right.astype(F32)).astype(BF)


def spread_z(rows, level):
    up = [(i, (i + 1) % 8) for i in range(8)]
    down = [(i, (i + 7) % 8) for i in range(8)]
    cut = rows.shape[0] // 2
    whole = jnp.zeros((8, *rows.shape), rows.dtype)
    rest = (jnp.uint32(0),) * (rows.ndim - 1)

    level = level.astype(jnp.int32)

    def put(whole, block, distance, start=0):
        return lax.dynamic_update_slice(
            whole,
            block[None],
            ((level + distance + 8 & 7).astype(jnp.uint32), jnp.uint32(start), *rest)
        )

    whole = put(whole, rows, 0)
    below = above = rows
    for k in (1, 2, 3):
        below, above = lax.ppermute(below, "z", up), lax.ppermute(above, "z", down)
        begun = (below, above) if k == 1 else begun
        whole = put(put(whole, below, -k), above, k)
    whole = put(whole, lax.ppermute(below[:cut], "z", up), 4)
    return put(whole, lax.ppermute(above[cut:], "z", down), 4, cut), begun


def after(value, *others):
    return lax.optimization_barrier((value, *others))[0]


def after_all(values, *others):
    return lax.optimization_barrier((*values, *others))[: len(values)]


def swap_core(rows):
    return lax.ppermute(rows, "core", [(0, 1), (1, 0)])


def pair_of_float(values):
    high = values.astype(BF)
    return high, (values - high.astype(F32)).astype(BF)


def normalize(values):
    factor = lax.rsqrt(jnp.mean(values * values, axis=-1, keepdims=True) + EPS)
    return values * factor, factor


def norm_back(grad_normed, unit, factor, gain):
    scaled = grad_normed * gain
    inner = jnp.mean(scaled * unit, axis=-1, keepdims=True)
    return factor * (scaled - unit * inner)


def silu_slope(values, sig):
    return sig * (1.0 + values * (1.0 - sig))


def expert_kernel(member, own, below, above, far_up, far_down, own_o, below_o, above_o, far_up_o,
                  far_down_o, grad_own, grad_other, blocks, shared_mine, shared_other, back_own, back_other, mixed, grad_pre, normed, w_down,
                  w_in, rows):
    step = pl.program_id(0)

    @pl.when(step == 0)
    def _():
        for b in range(8):
            flip = (b >> 2) ^ (member[0] >> 2)
            first = flip * 4 + ((b - member[0]) & 3)
            second = (1 - flip) * 4 + ((b - member[0] - 2) & 3)
            w_in[b * 192 : (b + 1) * 192, :896] = blocks[first, :, :896]
            w_in[b * 192 : (b + 1) * 192, 896:] = blocks[second, :, 896:1280]
            for k in range(3):
                w_down[b * 64 : (b + 1) * 64, k * 512 : (k + 1) * 512] = blocks[
                    second, k * 64 : (k + 1) * 64, 1280:
                ]

        @pl.when(member[2] == 0)
        def _():
            w_down[FE:] = shared_other[...]

        @pl.when(member[2] != 0)
        def _():
            w_down[FE:] = shared_mine[...]

        at = 0
        for piece in (own, below, above, far_up, far_down, own_o, below_o, above_o, far_up_o,
                      far_down_o):
            rows[at : at + piece.shape[0]] = piece[...]
            at += piece.shape[0]

    part = pl.ds(pl.multiple_of(step * 256, 256), 256)
    x = rows[part, :D]
    lane = lax.broadcasted_iota(jnp.int32, (256, 128), 1)
    expert = member[1]
    high, low = lane == expert, lane == expert + 8
    gate = jnp.sum(
        jnp.where(high | low, rows[part, D:].astype(F32), 0.0), axis=1, keepdims=True
    )
    back_down = dot_rows(jnp.where(step < 2, grad_own[...], grad_other[...]), w_down[...])
    pre = dot(x, w_in[...])
    gate_part, up_part = pre[:, :FE], pre[:, FE : 2 * FE]
    shared_gate, shared_up = pre[:, 2 * FE : 2 * FE + 128], pre[:, 2 * FE + 128 :]
    gate_sig = jax.nn.sigmoid(gate_part)
    gate_act = gate_part * gate_sig
    activ = gate_act * up_part
    shared_sig = jax.nn.sigmoid(shared_gate)
    shared_silu = shared_gate * shared_sig
    grad_mixed, grad_shared = back_down[:, :FE], back_down[:, FE:]
    grad_gate = jnp.sum(grad_mixed * activ, axis=1, keepdims=True)
    grad_activ = grad_mixed * gate
    mixed[:, :FE] = (gate * activ).astype(BF)
    mixed[:, FE:] = (shared_silu * shared_up).astype(BF)
    grad_pre[:, :FE] = (grad_activ * up_part * silu_slope(gate_part, gate_sig)).astype(BF)
    grad_pre[:, FE : 2 * FE] = (grad_activ * gate_act).astype(BF)
    grad_pre[:, 2 * FE : 2 * FE + 128] = (
        grad_shared * shared_up * silu_slope(shared_gate, shared_sig)
    ).astype(BF)
    grad_pre[:, 2 * FE + 128 :] = (grad_shared * shared_silu).astype(BF)
    normed[...] = x
    back = dot_rows(grad_pre[...], w_in[...]).astype(BF)
    top = grad_gate.astype(BF).astype(F32)
    tail = jnp.where(high, top, jnp.where(low, grad_gate - top, 0.0)).astype(BF)

    @pl.when(step < 2)
    def _():
        back_own[:, :D], back_own[:, D:] = back, tail

    @pl.when(step >= 2)
    def _():
        back_other[:, :D], back_other[:, D:] = back, tail


def lower_chunk(n):
    return pl.BlockSpec((256, n), lambda i, *_: (jnp.minimum(i, 1), 0))


def upper_chunk(n):
    return pl.BlockSpec((256, n), lambda i, *_: (jnp.maximum(i - 2, 0), 0))


def expert_pass(scalars, pieces, grad_own, grad_other, blocks, shared_mine, shared_other):
    whole = lambda a: pl.BlockSpec(a.shape, lambda i, *_, n=a.ndim: (0,) * n)
    chunk = lambda n: pl.BlockSpec((256, n), lambda i, *_: (i, 0))
    shape = lambda n, rows=1024: jax.ShapeDtypeStruct((rows, n), BF)
    return pl.pallas_call(
        expert_kernel,
        out_shape=(shape(1664, 512), shape(1664, 512), shape(640), shape(1280), shape(D), shape(D, 640)),
        grid_spec=pltpu.PrefetchScalarGridSpec(
            num_scalar_prefetch=1,
            grid=(4,),
            in_specs=[
                *(whole(p) for p in pieces),
                lower_chunk(D),
                upper_chunk(D),
                whole(blocks),
                whole(shared_mine),
                whole(shared_other),
            ],
            out_specs=(
                lower_chunk(1664),
                upper_chunk(1664),
                chunk(640),
                chunk(1280),
                chunk(D),
                pl.BlockSpec((640, D), lambda i, *_: (0, 0)),
            ),
            scratch_shapes=[
                pltpu.VMEM((D, 1280), BF),
                pltpu.VMEM((1024, 1664), BF),
            ],
        ),
        compiler_params=pltpu.CompilerParams(vmem_limit_bytes=56 << 20),
        cost_estimate=pl.CostEstimate(
            flops=2 * 1024 * D * 3200, bytes_accessed=30 << 20, transcendentals=1024 * 640
        ),
    )(scalars, *pieces, grad_own, grad_other, blocks, shared_mine, shared_other)


def expert_grad_kernel(normed, grad_pre, mixed, shared, own, other, own_cols, other_cols, out):
    into = dot_cols(normed[...], grad_pre[...])
    down = dot_cols(mixed[:512], own[...]) + dot_cols(mixed[512:], other[...])
    side = dot_cols(shared[:512], own_cols[...]) + dot_cols(shared[512:], other_cols[...])
    for b in range(2):
        for z in range(8):
            at = b * 64 + z * 8
            folded = jnp.concatenate(
                [down[at : at + 8, k * 512 : (k + 1) * 512] for k in range(3)], axis=0
            )
            mine = jnp.concatenate(
                [side[z * 16 + b * 8 : z * 16 + b * 8 + 8, k * 128 : (k + 1) * 128] for k in range(3)],
                axis=0,
            )
            out[z, b] = jnp.concatenate(
                [
                    into[b * 192 + z * 24 : b * 192 + z * 24 + 24],
                    folded,
                    mine,
                ],
                axis=1,
            ).astype(BF)


def expert_grads(normed, grad_pre, mixed, grad_own, grad_other):
    return pl.pallas_call(
        expert_grad_kernel,
        out_shape=jax.ShapeDtypeStruct((8, 8, 24, 1920), BF),
        grid=(4,),
        in_specs=[
            pl.BlockSpec((1024, 384), lambda j: (0, j)),
            pl.BlockSpec((1024, 1280), lambda j: (0, 0)),
            pl.BlockSpec((1024, 128), lambda j: (0, j)),
            pl.BlockSpec((1024, 128), lambda j: (0, 4)),
            pl.BlockSpec((512, D), lambda j: (0, 0)),
            pl.BlockSpec((512, D), lambda j: (0, 0)),
            pl.BlockSpec((512, 384), lambda j: (0, j)),
            pl.BlockSpec((512, 384), lambda j: (0, j)),
        ],
        out_specs=pl.BlockSpec((8, 2, 24, 1920), lambda j: (0, j, 0, 0)),
        compiler_params=pltpu.CompilerParams(vmem_limit_bytes=56 << 20),
        cost_estimate=pl.CostEstimate(
            flops=2 * 1024 * D * 1920, bytes_accessed=22 << 20, transcendentals=0
        ),
    )(normed, grad_pre, mixed, mixed, grad_own, grad_other, grad_own, grad_other)


def full(a):
    return pl.BlockSpec(a.shape, lambda *_, n=len(a.shape): (0,) * n)


def on_chip(kernel, scalars, args, outs, scratch=(), flops=0, exps=0):
    size = sum(math.prod(a.shape) * a.dtype.itemsize for a in (*args, *outs))
    return pl.pallas_call(
        kernel,
        out_shape=tuple(outs),
        grid_spec=pltpu.PrefetchScalarGridSpec(
            num_scalar_prefetch=1,
            grid=(1,),
            in_specs=[full(a) for a in args],
            out_specs=tuple(full(a) for a in outs),
            scratch_shapes=list(scratch),
        ),
        compiler_params=pltpu.CompilerParams(vmem_limit_bytes=56 << 20),
        cost_estimate=pl.CostEstimate(flops=flops, bytes_accessed=size, transcendentals=exps),
    )(scalars, *args)


def out(*shape, dtype=BF):
    return jax.ShapeDtypeStruct(shape, dtype)


PIECES = ((0, 128), (128, 128), (256, 128), (384, 64), (448, 64))


def pack_kernel(core, query, key, value, small, slots):
    rows = pl.ds(pl.multiple_of(core[0] * 96, 32), 96)
    for k, head in enumerate(KEY_HEAD):
        for slot in (k, k + 4):
            slots[slot, :96, :384] = query[rows, head * 384 : (head + 1) * 384]
            slots[slot, :96, 384:512] = key[rows, head * 128 : (head + 1) * 128]
            slots[slot, :96, 512:] = value[rows, head * 128 : (head + 1) * 128]
            slots[slot, 96:] = small[...]


def keys_kernel(core, own, below, above, far_up, far_down, gain, got, other, normed, kv, weight):
    for b in range(8):
        first = pl.multiple_of(b * 192 + core[0] * 96, 32)
        second = pl.multiple_of(b * 192 + (1 - core[0]) * 96, 32)
        weight[pl.ds(first, 96)] = got[b, :96]
        weight[pl.ds(second, 96)] = other[b]
    for (at, size), piece in zip(PIECES, (own, below, above, far_up, far_down)):
        unit, _ = normalize(piece[...].astype(F32))
        normed[at : at + size] = (unit * gain[...]).astype(BF)
    kv[...] = dot(normed[...], weight[:, GROUP * HEAD :]).astype(BF)


def query_kernel(core, normed, weight, kv, query):
    query[...] = dot(normed[...], weight[:, : GROUP * HEAD]).astype(BF)


def mask_of(query_at, query_seg, key_at, key_seg):
    return (query_at == key_at) | (
        (key_at < query_at) & (query_seg == key_seg) & (key_seg != 0)
    )


def attend_kernel(core, query, kv, kv_other, qat, qseg, kat, kseg, attended, logs):
    allowed = mask_of(qat[...], qseg[...], kat[...], kseg[...])
    keys = jnp.concatenate([kv[:, :HEAD], kv_other[:, :HEAD]], axis=0)
    values = jnp.concatenate([kv[:, HEAD:], kv_other[:, HEAD:]], axis=0)
    lane = lax.broadcasted_iota(jnp.int32, (512, 128), 1)
    kept = jnp.zeros((512, 128), F32)
    for g in range(GROUP):
        scores = dot_rows(query[:, g * HEAD : (g + 1) * HEAD], keys) * SCALE
        scores = jnp.where(allowed, scores, -1e30)
        top = jnp.max(scores, axis=1, keepdims=True)
        expo = jnp.exp(scores - top)
        total = jnp.sum(expo, axis=1, keepdims=True)
        kept = jnp.where(lane == g, top + jnp.log(total), kept)
        attended[:, g * HEAD : (g + 1) * HEAD] = dot((expo / total).astype(BF), values).astype(BF)
    logs[...] = kept


def output_kernel(core, attended, mine, other, own, below, above, far_up, far_down, weight):
    for c in range(2):
        @pl.when(core[0] == c)
        def _():
            weight[c * 192 : (c + 1) * 192] = mine[...]
            weight[(1 - c) * 192 : (2 - c) * 192] = other[...]
    whole = dot(attended[...], weight[...]).astype(BF)
    for (at, size), piece in zip(PIECES, (own, below, above, far_up, far_down)):
        piece[...] = whole[at : at + size]


def attend_back_kernel(core, own, below, above, far_up, far_down, query, kv, kv_other, qat, qseg, kat, kseg,
                       mine, other, logs, grad, grad_query, grad_own, grad_other, weight):
    for c in range(2):
        @pl.when(core[0] == c)
        def _():
            weight[c * 192 : (c + 1) * 192] = mine[...]
            weight[(1 - c) * 192 : (2 - c) * 192] = other[...]
    for (at, size), piece in zip(PIECES, (own, below, above, far_up, far_down)):
        grad[at : at + size] = piece[...]
    grad_att = dot_rows(grad[...], weight[...]).astype(BF)
    allowed = mask_of(qat[...], qseg[...], kat[...], kseg[...])
    keys = jnp.concatenate([kv[:, :HEAD], kv_other[:, :HEAD]], axis=0)
    values = jnp.concatenate([kv[:, HEAD:], kv_other[:, HEAD:]], axis=0)
    grad_keys = jnp.zeros((1024, HEAD), F32)
    grad_values = jnp.zeros((1024, HEAD), F32)
    for g in range(GROUP):
        queries = query[:, g * HEAD : (g + 1) * HEAD]
        heads = grad_att[:, g * HEAD : (g + 1) * HEAD]
        scores = jnp.where(allowed, dot_rows(queries, keys) * SCALE, -1e30)
        probs = jnp.exp(scores - logs[:, g : g + 1])
        grad_probs = dot_rows(heads, values)
        inner = jnp.sum(probs * grad_probs, axis=1, keepdims=True)
        grad_scores = (probs * (grad_probs - inner)).astype(BF)
        grad_query[:, g * HEAD : (g + 1) * HEAD] = (dot(grad_scores, keys) * SCALE).astype(BF)
        grad_keys += dot_cols(grad_scores, queries)
        grad_values += dot_cols(probs.astype(BF), heads)
    grad_keys = grad_keys * SCALE
    grad_own[:, :HEAD] = grad_keys[:512]
    grad_own[:, HEAD:] = grad_values[:512]
    grad_other[:, :HEAD] = grad_keys[512:].astype(BF)
    grad_other[:, HEAD:] = grad_values[512:].astype(BF)


def early_grads_kernel(core, grad_query, weight, normed, attended, grad, query, outs, column):
    into = dot_cols(normed[...], grad_query[...])
    column[...] = jnp.sum(into * weight[:, : GROUP * HEAD].astype(F32), axis=1, keepdims=True)
    sums = dot_cols(attended[...], grad[...])
    for z in range(8):
        for b in range(8):
            query[z, b] = into[b * 192 + z * 24 : b * 192 + z * 24 + 24].astype(BF)
        for c in range(2):
            for j in range(2):
                for k in range(2):
                    outs[c, z, j * 2 + k] = sums[
                        j * 192 + z * 24 : j * 192 + z * 24 + 24,
                        c * 768 + k * 384 : c * 768 + (k + 1) * 384,
                    ].astype(BF)


def weight_grads_kernel(core, grad_kv, from_other, weight, normed, small, gain, column, query, outs,
                        keep, give, back_kv):
    back_kv[...] = (grad_kv[...] + from_other[...].astype(F32)).astype(BF)
    into = dot_cols(normed[...], back_kv[...])
    late = jnp.sum(into * weight[:, GROUP * HEAD :].astype(F32), axis=1, keepdims=True)
    lane = lax.broadcasted_iota(jnp.int32, (D, 128), 1)
    side = jnp.where(lane == 9, (column[...] + late) / gain[...], small[...])

    def put(first, second):
        first[:, :8] = query[...]
        first[:, 8:] = outs[0]
        second[:, 8:] = outs[1]
        for z in range(8):
            for b in range(8):
                rows = slice(b * 192 + z * 24, b * 192 + z * 24 + 24)
                second[z, b] = jnp.concatenate([into[rows], side[rows]], axis=1).astype(BF)

    @pl.when(core[0] == 0)
    def _():
        put(keep, give)

    @pl.when(core[0] == 1)
    def _():
        put(give, keep)


def input_back_kernel(core, query, kv, weight, own, below, above, far_up, far_down, both):
    both[:, : GROUP * HEAD] = query[...]
    both[:, GROUP * HEAD :] = kv[...]
    back = dot_rows(both[...], weight[...]).astype(BF)
    for (at, size), piece in zip(PIECES, (own, below, above, far_up, far_down)):
        piece[...] = back[at : at + size]


def settle_experts_kernel(half, whole, expert_in, shared_in, expert_out, shared_out):
    low = [whole[0, 0, e // 4, e % 4, :, :896].astype(F32) for e in range(8)]
    high = [whole[0, 1, e // 4, e % 4, :, :896].astype(F32) for e in range(8)]
    expert_in[:, :, :896] = jnp.transpose(jnp.stack(low), (1, 0, 2))
    expert_in[:, :, 896:] = jnp.transpose(jnp.stack([h[:, :128] for h in high]), (1, 0, 2))
    for e in range(8):
        shared_in[:, e * 128 : (e + 1) * 128] = high[e][:, 128:256]
        shared_in[:, FS + e * 128 : FS + (e + 1) * 128] = high[e][:, 256:384]
        for k in range(3):
            expert_out[e, :, k * 512 : (k + 1) * 512] = high[e][k * 8 : (k + 1) * 8, 384:]
    for y in range(2):
        for j in range(4):
            side = whole[0, y, half[0], j, :, 896:].astype(F32)
            for k in range(3):
                lanes = j * 384 + k * 128
                shared_out[y * 8 : (y + 1) * 8, lanes : lanes + 128] = side[k * 8 : (k + 1) * 8]


def settle_experts(half, whole):
    f32 = lambda *s: jax.ShapeDtypeStruct(s, F32)
    return pl.pallas_call(
        settle_experts_kernel,
        out_shape=(f32(192, EXPERTS, 1024), f32(192, 2 * FS), f32(8, 64, D), f32(128, D)),
        grid_spec=pltpu.PrefetchScalarGridSpec(
            num_scalar_prefetch=1,
            grid=(8,),
            in_specs=[pl.BlockSpec((1, 2, 2, 4, 24, 1024), lambda z, *_: (z,) + (0,) * 5)],
            out_specs=(
                pl.BlockSpec((24, EXPERTS, 1024), lambda z, *_: (z, 0, 0)),
                pl.BlockSpec((24, 2 * FS), lambda z, *_: (z, 0)),
                pl.BlockSpec((8, 8, D), lambda z, *_: (0, z, 0)),
                pl.BlockSpec((16, D), lambda z, *_: (z, 0)),
            ),
        ),
        compiler_params=pltpu.CompilerParams(vmem_limit_bytes=56 << 20),
        cost_estimate=pl.CostEstimate(flops=0, bytes_accessed=19 << 20, transcendentals=0),
    )(half, whole)


def piece_kernel(place, same, below, above, across, side, piece):
    for ref, distance in ((same, 0), (below, 3), (above, 1), (across, 2)):
        piece[lax.rem(place[0] + distance, 4), :, :896] = ref[...]
    piece[:, :, 896:] = side[...]


def settle_kernel(core, mine, other, query, key, value, small, outs):
    def put(first, second):
        for z in range(8):
            rows = slice(z * 24, (z + 1) * 24)
            sums = jnp.zeros((24, 128), F32)
            for k, head in enumerate(KEY_HEAD):
                query[rows, head * 384 : (head + 1) * 384] = first[z, k].astype(F32)
                key[rows, head * 128 : (head + 1) * 128] = second[z, k, :, :128].astype(F32)
                value[rows, head * 128 : (head + 1) * 128] = second[z, k, :, 128:256].astype(F32)
                sums += second[z, k, :, 256:].astype(F32)
            small[rows] = sums
            for k in range(2):
                outs[rows, k * 384 : (k + 1) * 384] = first[z, 4 + k].astype(F32)
                outs[rows, (2 + k) * 384 : (3 + k) * 384] = second[z, 4 + k].astype(F32)

    @pl.when(core[0] == 0)
    def _():
        put(mine, other)

    @pl.when(core[0] == 1)
    def _():
        put(other, mine)


def shards(
    tokens,
    segment_ids,
    routes,
    gain_attn,
    w_query,
    w_key,
    w_value,
    w_out,
    gain_ffn,
    w_router,
    w_shared_in,
    w_shared_out,
    w_expert_in,
    w_expert_out,
    cotangent,
):
    level, core, half, place = (
        lax.axis_index(a).astype(jnp.uint32) for a in ("z", "core", "yhi", "x")
    )
    rows = tokens.shape[0]
    zero = jnp.uint32(0)

    member = half * 4 + place
    key_head = jnp.where((place == 1) | (place == 2), 3 - place, place)

    tokens_x = spread_x(tokens)
    at_core = core.reshape(1).astype(jnp.int32)
    small = jnp.concatenate([gain_attn[None], gain_ffn[None], w_router.T], axis=0)
    small = jnp.pad(small, ((0, 6), (0, 448)))
    (slots,) = on_chip(
        pack_kernel, at_core, (w_query, w_key, w_value, small), (out(8, 112, 640),)
    )
    got = exchange(slots, FSDP)
    small = got[:, 96:106, :192].transpose(1, 0, 2).reshape(10, D)
    gain_one = small[:1].astype(F32)
    gain_two = small[1:2].astype(F32)
    router = small[2:]

    w_out_late, *_ = lax.optimization_barrier((w_out, *tokens_x[1:3]))
    out_mine = lax.ppermute(
        w_out_late,
        ("core", "yhi", "x"),
        [(s * 8 + b, (b % 2) * 8 + s * 4 + KEY_HEAD[b // 2]) for s in range(2) for b in range(8)],
    )

    qkv_other = swap_core(after(got[:, :96], *tokens_x[3:]))
    turn, flip = level & 3, level >> 2
    first, second = core * 4 + ((place - turn) & 3), core * 4 + ((place - turn - 2) & 3)
    halves = (
        lax.dynamic_slice(w_expert_in, (zero, first, zero), (192, 1, 896)).reshape(192, 896),
        jnp.concatenate(
            [
                lax.dynamic_slice(w_expert_in, (zero, second, zero + 896), (192, 1, 128)).reshape(
                    192, 128
                ),
                lax.dynamic_slice(w_shared_in, (zero, second * 128), (192, 128)),
                lax.dynamic_slice(w_shared_in, (zero, second * 128 + FS), (192, 128)),
                lax.dynamic_slice(w_expert_out, (second, zero, zero), (1, 64, D))
                .reshape(64, 3, 512)
                .transpose(1, 0, 2)
                .reshape(192, 512),
            ],
            axis=1,
        ),
    )
    halves = after_all(halves, slots)
    halves = [
        lax.ppermute(
            part,
            ("z", *FSDP),
            [
                (z * 8 + h * 4 + x, z * 8 + (h ^ (z >> 2) ^ k) * 4 + ((x - z - 2 * k) & 3))
                for z in range(8)
                for h in range(2)
                for x in range(4)
            ],
        )
        for k, part in enumerate(halves)
    ]
    block = after(jnp.concatenate(halves, axis=1), got, *tokens_x[3:])
    blocks = lax.all_gather(block, "z")
    inputs = tokens.astype(F32)
    normed_one, kv, w_qkv = on_chip(
        keys_kernel,
        at_core,
        (*tokens_x, gain_one, got, qkv_other),
        (out(512, D), out(512, 256), out(D, 640)),
        flops=2 * 512 * D * 256,
    )
    kv_other = lax.ppermute(kv, "yhi", [(0, 1)])
    (query,) = on_chip(
        query_kernel, at_core, (normed_one, w_qkv, kv), (out(512, 384),), flops=2 * 512 * D * 384
    )
    grad_late = after(cotangent, kv)
    grad_below, grad_above = up_x(grad_late), down_x(grad_late)
    out_other = swap_core(after(out_mine, kv_other, query))
    starts = [((place + k) & 3) * 128 for k in (0, 3, 1, 2)]
    pos = jnp.concatenate([s.astype(jnp.int32) + jnp.arange(128, dtype=jnp.int32) for s in starts])
    seg_own = jnp.concatenate(
        [lax.dynamic_slice_in_dim(segment_ids, half * 512 + s, 128) for s in starts]
    )
    seg_other = jnp.concatenate([lax.dynamic_slice_in_dim(segment_ids, s, 128) for s in starts])
    pos_other = jnp.where(half == 1, pos - 512, 1 << 20)
    places = (
        pos[:, None],
        seg_own[:, None],
        jnp.concatenate([pos, pos_other])[None],
        jnp.concatenate([seg_own, seg_other])[None],
    )
    part = [out(size, D) for _, size in PIECES]
    attended, logs = on_chip(
        attend_kernel,
        at_core,
        (query, kv, kv_other, *places),
        (out(512, 384), out(512, 128, dtype=F32)),
        flops=2 * 512 * 384 * 2048,
        exps=3 * 512 * 1024,
    )
    hidden_part = on_chip(
        output_kernel,
        at_core,
        (attended, out_mine, out_other),
        part,
        scratch=[pltpu.VMEM((384, D), BF)],
        flops=2 * 512 * 384 * D,
    )
    far_up, far_down = after_all((grad_below[:64], grad_above[64:]), hidden_part[0])
    grad_x = (cotangent, grad_below, grad_above, up_x(far_up), down_x(far_down))
    shared_other = lax.ppermute(after(w_shared_out, attended), ("core", "yhi"), [(0, 1), (3, 2)])
    grad_own = jnp.concatenate(grad_x, axis=0)
    grad_other = swap_core(grad_own)
    hidden = inputs + collect_x(hidden_part)

    unit_two, factor_two = normalize(hidden)
    normed_two = (unit_two * gain_two).astype(BF)
    logits = dot_rows(normed_two, router)
    chosen = jnp.sum(
        (routes[:, :, None] == jnp.arange(EXPERTS, dtype=jnp.int32)[None, None, :]).astype(F32),
        axis=1,
    )
    weighted = chosen * jnp.exp(logits)
    gates = weighted / jnp.sum(weighted, axis=-1, keepdims=True)
    packed = jnp.concatenate(
        [normed_two, *pair_of_float(gates), jnp.zeros((rows, 112), BF)], axis=1
    )
    packed = spread_x(after(packed, *grad_x[3:]))
    packed = (*packed, *(swap_core(p) for p in packed))

    scalars = jnp.stack([member, core * 4 + place, (core == half).astype(jnp.uint32)])
    back_own, back_other, mixed, grad_pre, normed_all, w_down = expert_pass(
        scalars.astype(jnp.int32), packed, grad_own, grad_other, blocks, w_shared_out, shared_other
    )
    back_other = swap_core(back_other)
    back_part = [plus(o, s) for o, s in zip(pieces_of(back_own), pieces_of(back_other))]
    normed_all, _, _ = lax.optimization_barrier((normed_all, back_part[3], back_part[4]))
    flat = expert_grads(normed_all, grad_pre, mixed, grad_own, grad_other)
    back_sum, flat_ffn = collect_x(back_part, flat)

    grad_gates = back_sum[:, D : D + 8] + back_sum[:, D + 8 : D + 16]
    grad_logits = (
        gates * (grad_gates - jnp.sum(gates * grad_gates, axis=-1, keepdims=True))
    ).astype(BF)
    grad_normed_two = back_sum[:, :D] + dot(grad_logits, router)
    grad_router = dot_cols(normed_two, jnp.pad(grad_logits, ((0, 0), (0, 120))))
    grad_gain_ffn = jnp.sum(grad_normed_two * unit_two, axis=0, keepdims=True)
    grad_hidden = cotangent.astype(F32) + norm_back(
        grad_normed_two, unit_two, factor_two, gain_two
    )
    grad_hidden_low = grad_hidden.astype(BF)
    hidden_low = spread_x(grad_hidden_low)
    result_part = dot(after(mixed, grad_hidden_low), w_down).astype(BF)
    hidden_low = (after(hidden_low[0], result_part), *hidden_low[1:])

    grad_low, grad_query, grad_kv, to_other = on_chip(
        attend_back_kernel,
        at_core,
        (*hidden_low, query, kv, kv_other, *places, out_mine, out_other, logs),
        (out(512, D), out(512, 384), out(512, 256, dtype=F32), out(512, 256)),
        scratch=[pltpu.VMEM((384, D), BF)],
        flops=2 * 512 * 384 * 6656,
        exps=3 * 512 * 1024,
    )
    from_other = lax.ppermute(to_other, "yhi", [(1, 0)])
    small = grad_router + jnp.pad(grad_gain_ffn.T, ((0, 0), (8, 119)))
    query_sums, outs_sums, column = on_chip(
        early_grads_kernel,
        at_core,
        (grad_query, w_qkv, normed_one, attended, grad_low),
        (out(8, 8, 24, 384), out(2, 8, 4, 24, 384), out(D, 1, dtype=F32)),
        flops=2 * 512 * D * 768,
    )
    result_other = swap_core(after(result_part[512:], query_sums))
    keep, give, back_kv = on_chip(
        weight_grads_kernel,
        at_core,
        (
            grad_kv,
            from_other,
            w_qkv,
            normed_one,
            small,
            gain_one.reshape(D, 1),
            column,
            query_sums,
            outs_sums,
        ),
        (out(8, 12, 24, 384), out(8, 12, 24, 384), out(512, 256)),
        flops=2 * 512 * D * 256,
    )

    flat = plus(keep, swap_core(give))
    flat_sent = flat
    flat = exchange(flat, "z")
    ffn = lax.psum_scatter(flat_ffn, "z", scatter_dimension=0, tiled=True)[0]
    ffn = after(ffn, flat_sent)
    side = ffn[..., 1792:].reshape(4, 2, 24, 128)
    main = ffn[..., :1792].reshape(2, 4, 24, 1792)
    both = [
        jnp.concatenate([m[..., :896], side[:, 0], m[..., 896:], side[:, 1]], axis=-1)
        for m in (main[0], main[1])
    ]
    keep = jnp.where(half == 0, both[0], both[1])
    away = jnp.where(half == 0, both[1], both[0])
    ffn = plus(keep, lax.ppermute(away, "yhi", [(0, 1), (1, 0)]))
    here = lax.axis_index("ylo")
    keep = jnp.where(here == 0, ffn[..., :1024], ffn[..., 1024:])
    away = jnp.where(here == 0, ffn[..., 1024:], ffn[..., :1024])
    ffn = plus(keep, lax.ppermute(away, "ylo", [(0, 1), (1, 0)]))
    to = [
        lax.dynamic_index_in_dim(ffn[..., :896], (place + k) & 3, 0, False) for k in (0, 1, 3, 2)
    ]
    across = lax.ppermute(to[3], "x", [(i, (i + 2) % 4) for i in range(4)])
    (piece,) = on_chip(
        piece_kernel,
        place.reshape(1).astype(jnp.int32),
        (to[0], up_x(to[1]), down_x(to[2]), across, ffn[..., 896:]),
        (out(4, 24, 1024),),
    )
    whole = lax.all_gather(after(piece, flat), REP).reshape(8, 2, 2, 4, 24, 1024)
    flat = jnp.sum(flat.astype(F32), axis=0).astype(BF)
    outs = lax.dynamic_update_slice(
        jnp.zeros((8, 2, 24, 384), BF), flat[8:].reshape(2, 2, 24, 384), (2 * key_head, *(jnp.uint32(0),) * 3)
    )
    flat = jnp.concatenate([flat[:8, None], outs], axis=1)
    flat = jnp.concatenate([flat, flat], axis=0)
    result_part = [
        plus(o, s)
        for o, s in zip(pieces_of(result_part[:512]), pieces_of(after(result_other, flat)))
    ]
    back_one = on_chip(
        input_back_kernel,
        at_core,
        (after(grad_query, flat), back_kv, w_qkv),
        part,
        scratch=[pltpu.VMEM((512, 640), BF)],
        flops=2 * 512 * D * 640,
    )
    got = exchange(flat, PLANE).reshape(4, 4, 3, 24, 384)
    got = jnp.sum(got.astype(F32), axis=0)
    mine = jnp.concatenate([got[:, 0], jnp.sum(got[:, 1:], axis=0)], axis=0).astype(BF)
    mine, begun = spread_z(mine, level)
    result = (hidden + collect_x(result_part, gate=begun[0])).astype(BF)
    back_one = collect_x(back_one, gate=begun[1])
    sum_query, sum_key, sum_value, small, sum_out = on_chip(
        settle_kernel,
        at_core,
        (mine, swap_core(mine)),
        (
            out(192, D, dtype=F32),
            out(192, 512, dtype=F32),
            out(192, 512, dtype=F32),
            out(192, 128, dtype=F32),
            out(192, D, dtype=F32),
        ),
    )

    unit_own, factor_own = normalize(inputs)
    grad_input = (grad_hidden + norm_back(back_one, unit_own, factor_own, gain_one)).astype(BF)

    at_half = half.reshape(1).astype(jnp.int32)
    sum_expert_in, sum_shared_in, sum_expert_out, sum_shared_out = settle_experts(
        at_half, after(whole, sum_query, grad_input, result)
    )

    return (
        result,
        grad_input,
        small[:, 9],
        sum_query,
        sum_key,
        sum_value,
        sum_out,
        small[:, 8],
        small[:, :8],
        sum_shared_in,
        sum_shared_out,
        sum_expert_in,
        sum_expert_out,
    )


def solution(mesh):
    fine = Mesh(mesh.devices.reshape(SIZES), AXES)
    tokens = P((*REP, *FSDP), None)
    first = P(FSDP, None)
    return jax.shard_map(
        shards,
        mesh=fine,
        in_specs=(
            tokens,
            P(REP),
            tokens,
            P(FSDP),
            first,
            first,
            first,
            first,
            P(FSDP),
            first,
            first,
            first,
            P(FSDP, None, None),
            P(None, FSDP, None),
            tokens,
        ),
        out_specs=(
            tokens,
            tokens,
            P(FSDP),
            first,
            first,
            first,
            first,
            P(FSDP),
            first,
            first,
            first,
            P(FSDP, None, None),
            P(None, FSDP, None),
        ),
        check_vma=False,
    )
```

```python
import math

import jax
import jax.numpy as jnp
from jax import lax
from jax.experimental import pallas as pl
from jax.experimental.pallas import tpu as pltpu
from jax.sharding import Mesh, PartitionSpec as P

HEADS = 12
KV_HEADS = 4
HEAD = 128
GROUP = HEADS // KV_HEADS
D = 1536
FE = 512
FS = 1024
EXPERTS = 8
EPS = 1e-05
SCALE = 1.0 / math.sqrt(HEAD)

AXES = ("z", "ylo", "core", "yhi", "x")
SIZES = (8, 2, 2, 2, 4)
REP = ("z", "ylo", "core")
FSDP = ("yhi", "x")
PLANE = ("ylo", "yhi", "x")
KEY_HEAD = (0, 2, 1, 3)
BF = jnp.bfloat16
F32 = jnp.float32


def dot(left, right):
    return jnp.dot(left, right, preferred_element_type=F32)


def dot_rows(left, right):
    return lax.dot_general(left, right, (((1,), (1,)), ((), ())), preferred_element_type=F32)


def dot_cols(left, right):
    return lax.dot_general(left, right, (((0,), (0,)), ((), ())), preferred_element_type=F32)


def exchange(blocks, axes):
    return lax.all_to_all(blocks, axes, 0, 0, tiled=True)


def up_x(rows):
    return lax.ppermute(rows, "x", [(i, (i + 1) % 4) for i in range(4)])


def down_x(rows):
    return lax.ppermute(rows, "x", [(i, (i + 3) % 4) for i in range(4)])


def spread_x(rows):
    cut = rows.shape[0] // 2
    below, above = up_x(rows), down_x(rows)
    return rows, below, above, up_x(below[:cut]), down_x(above[cut:])


def pieces_of(rows):
    return tuple(rows[at : at + size] for at, size in PIECES)


def collect_x(pieces, beside=None, gate=None):
    far = up_x(pieces[3]), down_x(pieces[4])
    above, below = near_pieces(pieces, far)
    if gate is not None:
        above, below = after_all((above, below), gate)
    if beside is not None:
        above, below, beside = lax.optimization_barrier((above, below, beside))
    total = near_sum(pieces[0], above, below)
    return total if beside is None else (total, beside)


def near_pieces(pieces, far):
    own, below, above, *_ = pieces
    cut = far[0].shape[0]
    above = jnp.concatenate([plus(above[:cut], far[0]), above[cut:]], axis=0)
    below = jnp.concatenate([below[:cut], plus(below[cut:], far[1])], axis=0)
    return above, below


def near_sum(own, above, below):
    return own.astype(F32) + up_x(above).astype(F32) + down_x(below).astype(F32)


def plus(left, right):
    return (left.astype(F32) + right.astype(F32)).astype(BF)


def spread_z(rows, level):
    up = [(i, (i + 1) % 8) for i in range(8)]
    down = [(i, (i + 7) % 8) for i in range(8)]
    cut = rows.shape[0] // 2
    whole = jnp.zeros((8, *rows.shape), rows.dtype)
    rest = (jnp.uint32(0),) * (rows.ndim - 1)

    level = level.astype(jnp.int32)

    def put(whole, block, distance, start=0):
        return lax.dynamic_update_slice(
            whole,
            block[None],
            ((level + distance + 8 & 7).astype(jnp.uint32), jnp.uint32(start), *rest)
        )

    whole = put(whole, rows, 0)
    below = above = rows
    for k in (1, 2, 3):
        below, above = lax.ppermute(below, "z", up), lax.ppermute(above, "z", down)
        below, above = lax.optimization_barrier((below, above))
        whole = put(put(whole, below, -k), above, k)
    whole = put(whole, lax.ppermute(below[:cut], "z", up), 4)
    return put(whole, lax.ppermute(above[cut:], "z", down), 4, cut)


def after(value, *others):
    return lax.optimization_barrier((value, *others))[0]


def after_all(values, *others):
    return lax.optimization_barrier((*values, *others))[: len(values)]


def swap_core(rows):
    return lax.ppermute(rows, "core", [(0, 1), (1, 0)])


def pair_of_float(values):
    high = values.astype(BF)
    return high, (values - high.astype(F32)).astype(BF)


def normalize(values):
    factor = lax.rsqrt(jnp.mean(values * values, axis=-1, keepdims=True) + EPS)
    return values * factor, factor


def norm_back(grad_normed, unit, factor, gain):
    scaled = grad_normed * gain
    inner = jnp.mean(scaled * unit, axis=-1, keepdims=True)
    return factor * (scaled - unit * inner)


def silu_slope(values, sig):
    return sig * (1.0 + values * (1.0 - sig))


def expert_kernel(member, own, below, above, far_up, far_down, own_o, below_o, above_o, far_up_o,
                  far_down_o, grad_own, grad_other, blocks, shared_mine, shared_other, back_own, back_other, mixed, grad_pre, normed, w_down,
                  w_in, rows):
    step = pl.program_id(0)

    @pl.when(step == 0)
    def _():
        for b in range(8):
            flip = (b >> 2) ^ (member[0] >> 2)
            first = flip * 4 + ((b - member[0]) & 3)
            second = (1 - flip) * 4 + ((b - member[0] - 2) & 3)
            w_in[b * 192 : (b + 1) * 192, :896] = blocks[first, :, :896]
            w_in[b * 192 : (b + 1) * 192, 896:] = blocks[second, :, 896:1280]
            for k in range(3):
                w_down[b * 64 : (b + 1) * 64, k * 512 : (k + 1) * 512] = blocks[
                    second, k * 64 : (k + 1) * 64, 1280:
                ]

        @pl.when(member[2] == 0)
        def _():
            w_down[FE:] = shared_other[...]

        @pl.when(member[2] != 0)
        def _():
            w_down[FE:] = shared_mine[...]

        at = 0
        for piece in (own, below, above, far_up, far_down, own_o, below_o, above_o, far_up_o,
                      far_down_o):
            rows[at : at + piece.shape[0]] = piece[...]
            at += piece.shape[0]

    part = pl.ds(pl.multiple_of(step * 256, 256), 256)
    x = rows[part, :D]
    lane = lax.broadcasted_iota(jnp.int32, (256, 128), 1)
    expert = member[1]
    high, low = lane == expert, lane == expert + 8
    gate = jnp.sum(
        jnp.where(high | low, rows[part, D:].astype(F32), 0.0), axis=1, keepdims=True
    )
    back_down = dot_rows(jnp.where(step < 2, grad_own[...], grad_other[...]), w_down[...])
    pre = dot(x, w_in[...])
    gate_part, up_part = pre[:, :FE], pre[:, FE : 2 * FE]
    shared_gate, shared_up = pre[:, 2 * FE : 2 * FE + 128], pre[:, 2 * FE + 128 :]
    gate_sig = jax.nn.sigmoid(gate_part)
    gate_act = gate_part * gate_sig
    activ = gate_act * up_part
    shared_sig = jax.nn.sigmoid(shared_gate)
    shared_silu = shared_gate * shared_sig
    grad_mixed, grad_shared = back_down[:, :FE], back_down[:, FE:]
    grad_gate = jnp.sum(grad_mixed * activ, axis=1, keepdims=True)
    grad_activ = grad_mixed * gate
    mixed[:, :FE] = (gate * activ).astype(BF)
    mixed[:, FE:] = (shared_silu * shared_up).astype(BF)
    grad_pre[:, :FE] = (grad_activ * up_part * silu_slope(gate_part, gate_sig)).astype(BF)
    grad_pre[:, FE : 2 * FE] = (grad_activ * gate_act).astype(BF)
    grad_pre[:, 2 * FE : 2 * FE + 128] = (
        grad_shared * shared_up * silu_slope(shared_gate, shared_sig)
    ).astype(BF)
    grad_pre[:, 2 * FE + 128 :] = (grad_shared * shared_silu).astype(BF)
    normed[...] = x
    back = dot_rows(grad_pre[...], w_in[...]).astype(BF)
    top = grad_gate.astype(BF).astype(F32)
    tail = jnp.where(high, top, jnp.where(low, grad_gate - top, 0.0)).astype(BF)

    @pl.when(step < 2)
    def _():
        back_own[:, :D], back_own[:, D:] = back, tail

    @pl.when(step >= 2)
    def _():
        back_other[:, :D], back_other[:, D:] = back, tail


def lower_chunk(n):
    return pl.BlockSpec((256, n), lambda i, *_: (jnp.minimum(i, 1), 0))


def upper_chunk(n):
    return pl.BlockSpec((256, n), lambda i, *_: (jnp.maximum(i - 2, 0), 0))


def expert_pass(scalars, pieces, grad_own, grad_other, blocks, shared_mine, shared_other):
    whole = lambda a: pl.BlockSpec(a.shape, lambda i, *_, n=a.ndim: (0,) * n)
    chunk = lambda n: pl.BlockSpec((256, n), lambda i, *_: (i, 0))
    shape = lambda n, rows=1024: jax.ShapeDtypeStruct((rows, n), BF)
    return pl.pallas_call(
        expert_kernel,
        out_shape=(shape(1664, 512), shape(1664, 512), shape(640), shape(1280), shape(D), shape(D, 640)),
        grid_spec=pltpu.PrefetchScalarGridSpec(
            num_scalar_prefetch=1,
            grid=(4,),
            in_specs=[
                *(whole(p) for p in pieces),
                lower_chunk(D),
                upper_chunk(D),
                whole(blocks),
                whole(shared_mine),
                whole(shared_other),
            ],
            out_specs=(
                lower_chunk(1664),
                upper_chunk(1664),
                chunk(640),
                chunk(1280),
                chunk(D),
                pl.BlockSpec((640, D), lambda i, *_: (0, 0)),
            ),
            scratch_shapes=[
                pltpu.VMEM((D, 1280), BF),
                pltpu.VMEM((1024, 1664), BF),
            ],
        ),
        compiler_params=pltpu.CompilerParams(vmem_limit_bytes=56 << 20),
        cost_estimate=pl.CostEstimate(
            flops=2 * 1024 * D * 3200, bytes_accessed=30 << 20, transcendentals=1024 * 640
        ),
    )(scalars, *pieces, grad_own, grad_other, blocks, shared_mine, shared_other)


def expert_grad_kernel(normed, grad_pre, mixed, shared, own, other, own_cols, other_cols, out):
    into = dot_cols(normed[...], grad_pre[...])
    down = dot_cols(mixed[:512], own[...]) + dot_cols(mixed[512:], other[...])
    side = dot_cols(shared[:512], own_cols[...]) + dot_cols(shared[512:], other_cols[...])
    for b in range(2):
        for z in range(8):
            at = b * 64 + z * 8
            folded = jnp.concatenate(
                [down[at : at + 8, k * 512 : (k + 1) * 512] for k in range(3)], axis=0
            )
            mine = jnp.concatenate(
                [side[z * 16 + b * 8 : z * 16 + b * 8 + 8, k * 128 : (k + 1) * 128] for k in range(3)],
                axis=0,
            )
            out[z, b] = jnp.concatenate(
                [
                    into[b * 192 + z * 24 : b * 192 + z * 24 + 24],
                    folded,
                    mine,
                ],
                axis=1,
            ).astype(BF)


def expert_grads(normed, grad_pre, mixed, grad_own, grad_other):
    return pl.pallas_call(
        expert_grad_kernel,
        out_shape=jax.ShapeDtypeStruct((8, 8, 24, 1920), BF),
        grid=(4,),
        in_specs=[
            pl.BlockSpec((1024, 384), lambda j: (0, j)),
            pl.BlockSpec((1024, 1280), lambda j: (0, 0)),
            pl.BlockSpec((1024, 128), lambda j: (0, j)),
            pl.BlockSpec((1024, 128), lambda j: (0, 4)),
            pl.BlockSpec((512, D), lambda j: (0, 0)),
            pl.BlockSpec((512, D), lambda j: (0, 0)),
            pl.BlockSpec((512, 384), lambda j: (0, j)),
            pl.BlockSpec((512, 384), lambda j: (0, j)),
        ],
        out_specs=pl.BlockSpec((8, 2, 24, 1920), lambda j: (0, j, 0, 0)),
        compiler_params=pltpu.CompilerParams(vmem_limit_bytes=56 << 20),
        cost_estimate=pl.CostEstimate(
            flops=2 * 1024 * D * 1920, bytes_accessed=22 << 20, transcendentals=0
        ),
    )(normed, grad_pre, mixed, mixed, grad_own, grad_other, grad_own, grad_other)


def full(a):
    return pl.BlockSpec(a.shape, lambda *_, n=len(a.shape): (0,) * n)


def on_chip(kernel, scalars, args, outs, scratch=(), flops=0, exps=0):
    size = sum(math.prod(a.shape) * a.dtype.itemsize for a in (*args, *outs))
    return pl.pallas_call(
        kernel,
        out_shape=tuple(outs),
        grid_spec=pltpu.PrefetchScalarGridSpec(
            num_scalar_prefetch=1,
            grid=(1,),
            in_specs=[full(a) for a in args],
            out_specs=tuple(full(a) for a in outs),
            scratch_shapes=list(scratch),
        ),
        compiler_params=pltpu.CompilerParams(vmem_limit_bytes=56 << 20),
        cost_estimate=pl.CostEstimate(flops=flops, bytes_accessed=size, transcendentals=exps),
    )(scalars, *args)


def out(*shape, dtype=BF):
    return jax.ShapeDtypeStruct(shape, dtype)


PIECES = ((0, 128), (128, 128), (256, 128), (384, 64), (448, 64))


def pack_kernel(core, query, key, value, small, slots):
    rows = pl.ds(pl.multiple_of(core[0] * 96, 32), 96)
    for k, head in enumerate(KEY_HEAD):
        for slot in (k, k + 4):
            slots[slot, :96, :384] = query[rows, head * 384 : (head + 1) * 384]
            slots[slot, :96, 384:512] = key[rows, head * 128 : (head + 1) * 128]
            slots[slot, :96, 512:] = value[rows, head * 128 : (head + 1) * 128]
            slots[slot, 96:] = small[...]


def keys_kernel(core, own, below, above, far_up, far_down, gain, got, other, normed, kv, weight):
    for b in range(8):
        first = pl.multiple_of(b * 192 + core[0] * 96, 32)
        second = pl.multiple_of(b * 192 + (1 - core[0]) * 96, 32)
        weight[pl.ds(first, 96)] = got[b, :96]
        weight[pl.ds(second, 96)] = other[b]
    for (at, size), piece in zip(PIECES, (own, below, above, far_up, far_down)):
        unit, _ = normalize(piece[...].astype(F32))
        normed[at : at + size] = (unit * gain[...]).astype(BF)
    kv[...] = dot(normed[...], weight[:, GROUP * HEAD :]).astype(BF)


def query_kernel(core, normed, weight, kv, query):
    query[...] = dot(normed[...], weight[:, : GROUP * HEAD]).astype(BF)


def mask_of(query_at, query_seg, key_at, key_seg):
    return (query_at == key_at) | (
        (key_at < query_at) & (query_seg == key_seg) & (key_seg != 0)
    )


def attend_kernel(core, query, kv, kv_other, qat, qseg, kat, kseg, attended, logs):
    allowed = mask_of(qat[...], qseg[...], kat[...], kseg[...])
    keys = jnp.concatenate([kv[:, :HEAD], kv_other[:, :HEAD]], axis=0)
    values = jnp.concatenate([kv[:, HEAD:], kv_other[:, HEAD:]], axis=0)
    lane = lax.broadcasted_iota(jnp.int32, (512, 128), 1)
    kept = jnp.zeros((512, 128), F32)
    for g in range(GROUP):
        scores = dot_rows(query[:, g * HEAD : (g + 1) * HEAD], keys) * SCALE
        scores = jnp.where(allowed, scores, -1e30)
        top = jnp.max(scores, axis=1, keepdims=True)
        expo = jnp.exp(scores - top)
        total = jnp.sum(expo, axis=1, keepdims=True)
        kept = jnp.where(lane == g, top + jnp.log(total), kept)
        attended[:, g * HEAD : (g + 1) * HEAD] = dot((expo / total).astype(BF), values).astype(BF)
    logs[...] = kept


def output_kernel(core, attended, mine, other, own, below, above, far_up, far_down, weight):
    for c in range(2):
        @pl.when(core[0] == c)
        def _():
            weight[c * 192 : (c + 1) * 192] = mine[...]
            weight[(1 - c) * 192 : (2 - c) * 192] = other[...]
    whole = dot(attended[...], weight[...]).astype(BF)
    for (at, size), piece in zip(PIECES, (own, below, above, far_up, far_down)):
        piece[...] = whole[at : at + size]


def attend_back_kernel(core, own, below, above, far_up, far_down, query, kv, kv_other, qat, qseg, kat, kseg,
                       mine, other, logs, grad, grad_query, grad_own, grad_other, weight):
    for c in range(2):
        @pl.when(core[0] == c)
        def _():
            weight[c * 192 : (c + 1) * 192] = mine[...]
            weight[(1 - c) * 192 : (2 - c) * 192] = other[...]
    for (at, size), piece in zip(PIECES, (own, below, above, far_up, far_down)):
        grad[at : at + size] = piece[...]
    grad_att = dot_rows(grad[...], weight[...]).astype(BF)
    allowed = mask_of(qat[...], qseg[...], kat[...], kseg[...])
    keys = jnp.concatenate([kv[:, :HEAD], kv_other[:, :HEAD]], axis=0)
    values = jnp.concatenate([kv[:, HEAD:], kv_other[:, HEAD:]], axis=0)
    grad_keys = jnp.zeros((1024, HEAD), F32)
    grad_values = jnp.zeros((1024, HEAD), F32)
    for g in range(GROUP):
        queries = query[:, g * HEAD : (g + 1) * HEAD]
        heads = grad_att[:, g * HEAD : (g + 1) * HEAD]
        scores = jnp.where(allowed, dot_rows(queries, keys) * SCALE, -1e30)
        probs = jnp.exp(scores - logs[:, g : g + 1])
        grad_probs = dot_rows(heads, values)
        inner = jnp.sum(probs * grad_probs, axis=1, keepdims=True)
        grad_scores = (probs * (grad_probs - inner)).astype(BF)
        grad_query[:, g * HEAD : (g + 1) * HEAD] = (dot(grad_scores, keys) * SCALE).astype(BF)
        grad_keys += dot_cols(grad_scores, queries)
        grad_values += dot_cols(probs.astype(BF), heads)
    grad_keys = grad_keys * SCALE
    grad_own[:, :HEAD] = grad_keys[:512]
    grad_own[:, HEAD:] = grad_values[:512]
    grad_other[:, :HEAD] = grad_keys[512:].astype(BF)
    grad_other[:, HEAD:] = grad_values[512:].astype(BF)


def early_grads_kernel(core, grad_query, weight, normed, attended, grad, query, outs, column):
    into = dot_cols(normed[...], grad_query[...])
    column[...] = jnp.sum(into * weight[:, : GROUP * HEAD].astype(F32), axis=1, keepdims=True)
    sums = dot_cols(attended[...], grad[...])
    for z in range(8):
        for b in range(8):
            query[z, b] = into[b * 192 + z * 24 : b * 192 + z * 24 + 24].astype(BF)
        for c in range(2):
            for j in range(2):
                for k in range(2):
                    outs[c, z, j * 2 + k] = sums[
                        j * 192 + z * 24 : j * 192 + z * 24 + 24,
                        c * 768 + k * 384 : c * 768 + (k + 1) * 384,
                    ].astype(BF)


def weight_grads_kernel(core, grad_kv, from_other, weight, normed, small, gain, column, query, outs,
                        keep, give, back_kv):
    back_kv[...] = (grad_kv[...] + from_other[...].astype(F32)).astype(BF)
    into = dot_cols(normed[...], back_kv[...])
    late = jnp.sum(into * weight[:, GROUP * HEAD :].astype(F32), axis=1, keepdims=True)
    lane = lax.broadcasted_iota(jnp.int32, (D, 128), 1)
    side = jnp.where(lane == 9, (column[...] + late) / gain[...], small[...])

    def put(first, second):
        first[:, :8] = query[...]
        first[:, 8:] = outs[0]
        second[:, 8:] = outs[1]
        for z in range(8):
            for b in range(8):
                rows = slice(b * 192 + z * 24, b * 192 + z * 24 + 24)
                second[z, b] = jnp.concatenate([into[rows], side[rows]], axis=1).astype(BF)

    @pl.when(core[0] == 0)
    def _():
        put(keep, give)

    @pl.when(core[0] == 1)
    def _():
        put(give, keep)


def input_back_kernel(core, query, kv, weight, own, below, above, far_up, far_down, both):
    both[:, : GROUP * HEAD] = query[...]
    both[:, GROUP * HEAD :] = kv[...]
    back = dot_rows(both[...], weight[...]).astype(BF)
    for (at, size), piece in zip(PIECES, (own, below, above, far_up, far_down)):
        piece[...] = back[at : at + size]


def settle_experts_kernel(half, whole, expert_in, shared_in, expert_out, shared_out):
    low = [whole[0, 0, e // 4, e % 4, :, :896].astype(F32) for e in range(8)]
    high = [whole[0, 1, e // 4, e % 4, :, :896].astype(F32) for e in range(8)]
    expert_in[:, :, :896] = jnp.transpose(jnp.stack(low), (1, 0, 2))
    expert_in[:, :, 896:] = jnp.transpose(jnp.stack([h[:, :128] for h in high]), (1, 0, 2))
    for e in range(8):
        shared_in[:, e * 128 : (e + 1) * 128] = high[e][:, 128:256]
        shared_in[:, FS + e * 128 : FS + (e + 1) * 128] = high[e][:, 256:384]
        for k in range(3):
            expert_out[e, :, k * 512 : (k + 1) * 512] = high[e][k * 8 : (k + 1) * 8, 384:]
    for y in range(2):
        for j in range(4):
            side = whole[0, y, half[0], j, :, 896:].astype(F32)
            for k in range(3):
                lanes = j * 384 + k * 128
                shared_out[y * 8 : (y + 1) * 8, lanes : lanes + 128] = side[k * 8 : (k + 1) * 8]


def settle_experts(half, whole):
    f32 = lambda *s: jax.ShapeDtypeStruct(s, F32)
    return pl.pallas_call(
        settle_experts_kernel,
        out_shape=(f32(192, EXPERTS, 1024), f32(192, 2 * FS), f32(8, 64, D), f32(128, D)),
        grid_spec=pltpu.PrefetchScalarGridSpec(
            num_scalar_prefetch=1,
            grid=(8,),
            in_specs=[pl.BlockSpec((1, 2, 2, 4, 24, 1024), lambda z, *_: (z,) + (0,) * 5)],
            out_specs=(
                pl.BlockSpec((24, EXPERTS, 1024), lambda z, *_: (z, 0, 0)),
                pl.BlockSpec((24, 2 * FS), lambda z, *_: (z, 0)),
                pl.BlockSpec((8, 8, D), lambda z, *_: (0, z, 0)),
                pl.BlockSpec((16, D), lambda z, *_: (z, 0)),
            ),
        ),
        compiler_params=pltpu.CompilerParams(vmem_limit_bytes=56 << 20),
        cost_estimate=pl.CostEstimate(flops=0, bytes_accessed=19 << 20, transcendentals=0),
    )(half, whole)


def piece_kernel(place, same, below, above, across, side, piece):
    for ref, distance in ((same, 0), (below, 3), (above, 1), (across, 2)):
        piece[lax.rem(place[0] + distance, 4), :, :896] = ref[...]
    piece[:, :, 896:] = side[...]


def settle_kernel(core, mine, other, query, key, value, small, outs):
    def put(first, second):
        for z in range(8):
            rows = slice(z * 24, (z + 1) * 24)
            sums = jnp.zeros((24, 128), F32)
            for k, head in enumerate(KEY_HEAD):
                query[rows, head * 384 : (head + 1) * 384] = first[z, k].astype(F32)
                key[rows, head * 128 : (head + 1) * 128] = second[z, k, :, :128].astype(F32)
                value[rows, head * 128 : (head + 1) * 128] = second[z, k, :, 128:256].astype(F32)
                sums += second[z, k, :, 256:].astype(F32)
            small[rows] = sums
            for k in range(2):
                outs[rows, k * 384 : (k + 1) * 384] = first[z, 4 + k].astype(F32)
                outs[rows, (2 + k) * 384 : (3 + k) * 384] = second[z, 4 + k].astype(F32)

    @pl.when(core[0] == 0)
    def _():
        put(mine, other)

    @pl.when(core[0] == 1)
    def _():
        put(other, mine)


def shards(
    tokens,
    segment_ids,
    routes,
    gain_attn,
    w_query,
    w_key,
    w_value,
    w_out,
    gain_ffn,
    w_router,
    w_shared_in,
    w_shared_out,
    w_expert_in,
    w_expert_out,
    cotangent,
):
    level, core, half, place = (
        lax.axis_index(a).astype(jnp.uint32) for a in ("z", "core", "yhi", "x")
    )
    rows = tokens.shape[0]
    zero = jnp.uint32(0)

    member = half * 4 + place
    key_head = jnp.where((place == 1) | (place == 2), 3 - place, place)

    tokens_x = spread_x(tokens)
    at_core = core.reshape(1).astype(jnp.int32)
    small = jnp.concatenate([gain_attn[None], gain_ffn[None], w_router.T], axis=0)
    small = jnp.pad(small, ((0, 6), (0, 448)))
    (slots,) = on_chip(
        pack_kernel, at_core, (w_query, w_key, w_value, small), (out(8, 112, 640),)
    )
    got = exchange(slots, FSDP)
    small = got[:, 96:106, :192].transpose(1, 0, 2).reshape(10, D)
    gain_one = small[:1].astype(F32)
    gain_two = small[1:2].astype(F32)
    router = small[2:]

    w_out_late, *_ = lax.optimization_barrier((w_out, *tokens_x[1:3]))
    out_mine = lax.ppermute(
        w_out_late,
        ("core", "yhi", "x"),
        [(s * 8 + b, (b % 2) * 8 + s * 4 + KEY_HEAD[b // 2]) for s in range(2) for b in range(8)],
    )

    qkv_other = swap_core(after(got[:, :96], *tokens_x[3:]))
    turn, flip = level & 3, level >> 2
    first, second = core * 4 + ((place - turn) & 3), core * 4 + ((place - turn - 2) & 3)
    halves = (
        lax.dynamic_slice(w_expert_in, (zero, first, zero), (192, 1, 896)).reshape(192, 896),
        jnp.concatenate(
            [
                lax.dynamic_slice(w_expert_in, (zero, second, zero + 896), (192, 1, 128)).reshape(
                    192, 128
                ),
                lax.dynamic_slice(w_shared_in, (zero, second * 128), (192, 128)),
                lax.dynamic_slice(w_shared_in, (zero, second * 128 + FS), (192, 128)),
                lax.dynamic_slice(w_expert_out, (second, zero, zero), (1, 64, D))
                .reshape(64, 3, 512)
                .transpose(1, 0, 2)
                .reshape(192, 512),
            ],
            axis=1,
        ),
    )
    halves = after_all(halves, slots)
    halves = [
        lax.ppermute(
            part,
            ("z", *FSDP),
            [
                (z * 8 + h * 4 + x, z * 8 + (h ^ (z >> 2) ^ k) * 4 + ((x - z - 2 * k) & 3))
                for z in range(8)
                for h in range(2)
                for x in range(4)
            ],
        )
        for k, part in enumerate(halves)
    ]
    block = after(jnp.concatenate(halves, axis=1), got, *tokens_x[3:])
    blocks = lax.all_gather(block, "z")
    inputs = tokens.astype(F32)
    normed_one, kv, w_qkv = on_chip(
        keys_kernel,
        at_core,
        (*tokens_x, gain_one, got, qkv_other),
        (out(512, D), out(512, 256), out(D, 640)),
        flops=2 * 512 * D * 256,
    )
    kv_other = lax.ppermute(kv, "yhi", [(0, 1)])
    (query,) = on_chip(
        query_kernel, at_core, (normed_one, w_qkv, kv), (out(512, 384),), flops=2 * 512 * D * 384
    )
    grad_late = after(cotangent, kv)
    grad_below, grad_above = up_x(grad_late), down_x(grad_late)
    out_other = swap_core(after(out_mine, kv_other, query))
    starts = [((place + k) & 3) * 128 for k in (0, 3, 1, 2)]
    pos = jnp.concatenate([s.astype(jnp.int32) + jnp.arange(128, dtype=jnp.int32) for s in starts])
    seg_own = jnp.concatenate(
        [lax.dynamic_slice_in_dim(segment_ids, half * 512 + s, 128) for s in starts]
    )
    seg_other = jnp.concatenate([lax.dynamic_slice_in_dim(segment_ids, s, 128) for s in starts])
    pos_other = jnp.where(half == 1, pos - 512, 1 << 20)
    places = (
        pos[:, None],
        seg_own[:, None],
        jnp.concatenate([pos, pos_other])[None],
        jnp.concatenate([seg_own, seg_other])[None],
    )
    part = [out(size, D) for _, size in PIECES]
    attended, logs = on_chip(
        attend_kernel,
        at_core,
        (query, kv, kv_other, *places),
        (out(512, 384), out(512, 128, dtype=F32)),
        flops=2 * 512 * 384 * 2048,
        exps=3 * 512 * 1024,
    )
    hidden_part = on_chip(
        output_kernel,
        at_core,
        (attended, out_mine, out_other),
        part,
        scratch=[pltpu.VMEM((384, D), BF)],
        flops=2 * 512 * 384 * D,
    )
    far_up, far_down = after_all((grad_below[:64], grad_above[64:]), hidden_part[0])
    grad_x = (cotangent, grad_below, grad_above, up_x(far_up), down_x(far_down))
    shared_other = lax.ppermute(after(w_shared_out, attended), ("core", "yhi"), [(0, 1), (3, 2)])
    grad_own = jnp.concatenate(grad_x, axis=0)
    grad_other = swap_core(grad_own)
    hidden = inputs + collect_x(hidden_part)

    unit_two, factor_two = normalize(hidden)
    normed_two = (unit_two * gain_two).astype(BF)
    logits = dot_rows(normed_two, router)
    chosen = jnp.sum(
        (routes[:, :, None] == jnp.arange(EXPERTS, dtype=jnp.int32)[None, None, :]).astype(F32),
        axis=1,
    )
    weighted = chosen * jnp.exp(logits)
    gates = weighted / jnp.sum(weighted, axis=-1, keepdims=True)
    packed = jnp.concatenate(
        [normed_two, *pair_of_float(gates), jnp.zeros((rows, 112), BF)], axis=1
    )
    packed = spread_x(after(packed, *grad_x[3:]))
    packed = (*packed, *(swap_core(p) for p in packed))

    scalars = jnp.stack([member, core * 4 + place, (core == half).astype(jnp.uint32)])
    back_own, back_other, mixed, grad_pre, normed_all, w_down = expert_pass(
        scalars.astype(jnp.int32), packed, grad_own, grad_other, blocks, w_shared_out, shared_other
    )
    back_other = swap_core(back_other)
    back_part = [plus(o, s) for o, s in zip(pieces_of(back_own), pieces_of(back_other))]
    normed_all, _, _ = lax.optimization_barrier((normed_all, back_part[3], back_part[4]))
    flat = expert_grads(normed_all, grad_pre, mixed, grad_own, grad_other)
    back_sum, flat_ffn = collect_x(back_part, flat)

    grad_gates = back_sum[:, D : D + 8] + back_sum[:, D + 8 : D + 16]
    grad_logits = (
        gates * (grad_gates - jnp.sum(gates * grad_gates, axis=-1, keepdims=True))
    ).astype(BF)
    grad_normed_two = back_sum[:, :D] + dot(grad_logits, router)
    grad_router = dot_cols(normed_two, jnp.pad(grad_logits, ((0, 0), (0, 120))))
    grad_gain_ffn = jnp.sum(grad_normed_two * unit_two, axis=0, keepdims=True)
    grad_hidden = cotangent.astype(F32) + norm_back(
        grad_normed_two, unit_two, factor_two, gain_two
    )
    grad_hidden_low = grad_hidden.astype(BF)
    hidden_low = spread_x(grad_hidden_low)
    result_part = dot(after(mixed, grad_hidden_low), w_down).astype(BF)
    hidden_low = (after(hidden_low[0], result_part), *hidden_low[1:])

    grad_low, grad_query, grad_kv, to_other = on_chip(
        attend_back_kernel,
        at_core,
        (*hidden_low, query, kv, kv_other, *places, out_mine, out_other, logs),
        (out(512, D), out(512, 384), out(512, 256, dtype=F32), out(512, 256)),
        scratch=[pltpu.VMEM((384, D), BF)],
        flops=2 * 512 * 384 * 6656,
        exps=3 * 512 * 1024,
    )
    from_other = lax.ppermute(to_other, "yhi", [(1, 0)])
    result_other = swap_core(after(result_part[512:], to_other))
    from_other, result_other = lax.optimization_barrier((from_other, result_other))
    small = grad_router + jnp.pad(grad_gain_ffn.T, ((0, 0), (8, 119)))
    query_sums, outs_sums, column = on_chip(
        early_grads_kernel,
        at_core,
        (grad_query, w_qkv, normed_one, attended, grad_low),
        (out(8, 8, 24, 384), out(2, 8, 4, 24, 384), out(D, 1, dtype=F32)),
        flops=2 * 512 * D * 768,
    )
    keep, give, back_kv = on_chip(
        weight_grads_kernel,
        at_core,
        (
            grad_kv,
            from_other,
            w_qkv,
            normed_one,
            small,
            gain_one.reshape(D, 1),
            column,
            query_sums,
            outs_sums,
        ),
        (out(8, 12, 24, 384), out(8, 12, 24, 384), out(512, 256)),
        flops=2 * 512 * D * 256,
    )

    flat = plus(keep, swap_core(give))
    flat_sent = flat
    flat = exchange(flat, "z")
    ffn = lax.psum_scatter(flat_ffn, "z", scatter_dimension=0, tiled=True)[0]
    ffn = after(ffn, flat_sent)
    side = ffn[..., 1792:].reshape(4, 2, 24, 128)
    main = ffn[..., :1792].reshape(2, 4, 24, 1792)
    both = [
        jnp.concatenate([m[..., :896], side[:, 0], m[..., 896:], side[:, 1]], axis=-1)
        for m in (main[0], main[1])
    ]
    keep = jnp.where(half == 0, both[0], both[1])
    away = jnp.where(half == 0, both[1], both[0])
    ffn = plus(keep, lax.ppermute(away, "yhi", [(0, 1), (1, 0)]))
    here = lax.axis_index("ylo")
    keep = jnp.where(here == 0, ffn[..., :1024], ffn[..., 1024:])
    away = jnp.where(here == 0, ffn[..., 1024:], ffn[..., :1024])
    ffn = plus(keep, lax.ppermute(away, "ylo", [(0, 1), (1, 0)]))
    to = [
        lax.dynamic_index_in_dim(ffn[..., :896], (place + k) & 3, 0, False) for k in (0, 1, 3, 2)
    ]
    across = lax.ppermute(to[3], "x", [(i, (i + 2) % 4) for i in range(4)])
    (piece,) = on_chip(
        piece_kernel,
        place.reshape(1).astype(jnp.int32),
        (to[0], up_x(to[1]), down_x(to[2]), across, ffn[..., 896:]),
        (out(4, 24, 1024),),
    )
    whole = lax.all_gather(after(piece, flat), REP).reshape(8, 2, 2, 4, 24, 1024)
    flat = jnp.sum(flat.astype(F32), axis=0).astype(BF)
    outs = lax.dynamic_update_slice(
        jnp.zeros((8, 2, 24, 384), BF), flat[8:].reshape(2, 2, 24, 384), (2 * key_head, *(jnp.uint32(0),) * 3)
    )
    flat = jnp.concatenate([flat[:8, None], outs], axis=1)
    flat = jnp.concatenate([flat, flat], axis=0)
    result_part = [
        plus(o, s)
        for o, s in zip(pieces_of(result_part[:512]), pieces_of(after(result_other, flat)))
    ]
    back_one = on_chip(
        input_back_kernel,
        at_core,
        (after(grad_query, flat), back_kv, w_qkv),
        part,
        scratch=[pltpu.VMEM((512, 640), BF)],
        flops=2 * 512 * D * 640,
    )
    got = exchange(flat, PLANE).reshape(4, 4, 3, 24, 384)
    got = jnp.sum(got.astype(F32), axis=0)
    mine = jnp.concatenate([got[:, 0], jnp.sum(got[:, 1:], axis=0)], axis=0).astype(BF)
    result = (hidden + collect_x(result_part, gate=got)).astype(BF)
    mine = spread_z(mine, level)
    back_one = collect_x(back_one, gate=mine)
    sum_query, sum_key, sum_value, small, sum_out = on_chip(
        settle_kernel,
        at_core,
        (mine, swap_core(mine)),
        (
            out(192, D, dtype=F32),
            out(192, 512, dtype=F32),
            out(192, 512, dtype=F32),
            out(192, 128, dtype=F32),
            out(192, D, dtype=F32),
        ),
    )

    unit_own, factor_own = normalize(inputs)
    grad_input = (grad_hidden + norm_back(back_one, unit_own, factor_own, gain_one)).astype(BF)

    at_half = half.reshape(1).astype(jnp.int32)
    sum_expert_in, sum_shared_in, sum_expert_out, sum_shared_out = settle_experts(
        at_half, after(whole, sum_query, result)
    )

    return (
        result,
        grad_input,
        small[:, 9],
        sum_query,
        sum_key,
        sum_value,
        sum_out,
        small[:, 8],
        small[:, :8],
        sum_shared_in,
        sum_shared_out,
        sum_expert_in,
        sum_expert_out,
    )


def solution(mesh):
    fine = Mesh(mesh.devices.reshape(SIZES), AXES)
    tokens = P((*REP, *FSDP), None)
    first = P(FSDP, None)
    return jax.shard_map(
        shards,
        mesh=fine,
        in_specs=(
            tokens,
            P(REP),
            tokens,
            P(FSDP),
            first,
            first,
            first,
            first,
            P(FSDP),
            first,
            first,
            first,
            P(FSDP, None, None),
            P(None, FSDP, None),
            tokens,
        ),
        out_specs=(
            tokens,
            tokens,
            P(FSDP),
            first,
            first,
            first,
            first,
            P(FSDP),
            first,
            first,
            first,
            P(FSDP, None, None),
            P(None, FSDP, None),
        ),
        check_vma=False,
    )
```

```python
import math

import jax
import jax.numpy as jnp
from jax import lax
from jax.experimental import pallas as pl
from jax.experimental.pallas import tpu as pltpu
from jax.sharding import Mesh, PartitionSpec as P

HEADS = 12
KV_HEADS = 4
HEAD = 128
GROUP = HEADS // KV_HEADS
D = 1536
FE = 512
FS = 1024
EXPERTS = 8
EPS = 1e-05
SCALE = 1.0 / math.sqrt(HEAD)

AXES = ("z", "ylo", "core", "yhi", "x")
SIZES = (8, 2, 2, 2, 4)
REP = ("z", "ylo", "core")
FSDP = ("yhi", "x")
PLANE = ("ylo", "yhi", "x")
KEY_HEAD = (0, 2, 1, 3)
BF = jnp.bfloat16
F32 = jnp.float32


def dot(left, right):
    return jnp.dot(left, right, preferred_element_type=F32)


def dot_rows(left, right):
    return lax.dot_general(left, right, (((1,), (1,)), ((), ())), preferred_element_type=F32)


def dot_cols(left, right):
    return lax.dot_general(left, right, (((0,), (0,)), ((), ())), preferred_element_type=F32)


def exchange(blocks, axes):
    return lax.all_to_all(blocks, axes, 0, 0, tiled=True)


def up_x(rows):
    return lax.ppermute(rows, "x", [(i, (i + 1) % 4) for i in range(4)])


def down_x(rows):
    return lax.ppermute(rows, "x", [(i, (i + 3) % 4) for i in range(4)])


def spread_x(rows):
    cut = rows.shape[0] // 2
    below, above = up_x(rows), down_x(rows)
    return rows, below, above, up_x(below[:cut]), down_x(above[cut:])


def pieces_of(rows):
    return tuple(rows[at : at + size] for at, size in PIECES)


def collect_x(pieces, beside=None, gate=None):
    above, below = near_pieces(pieces, far_pieces(pieces))
    if gate is not None:
        above, below = after_all((above, below), gate)
    if beside is not None:
        above, below, beside = lax.optimization_barrier((above, below, beside))
    total = near_sum(pieces[0], up_x(above), down_x(below))
    return total if beside is None else (total, beside)


def far_pieces(pieces):
    return up_x(pieces[3]), down_x(pieces[4])


def near_pieces(pieces, far):
    _, below, above, *_ = pieces
    cut = far[0].shape[0]
    above = jnp.concatenate([plus(above[:cut], far[0]), above[cut:]], axis=0)
    below = jnp.concatenate([below[:cut], plus(below[cut:], far[1])], axis=0)
    return above, below


def near_sum(own, below, above):
    return own.astype(F32) + below.astype(F32) + above.astype(F32)


def plus(left, right):
    return (left.astype(F32) + right.astype(F32)).astype(BF)


def spread_z(rows, level):
    up = [(i, (i + 1) % 8) for i in range(8)]
    down = [(i, (i + 7) % 8) for i in range(8)]
    cut = rows.shape[0] // 2
    whole = jnp.zeros((8, *rows.shape), rows.dtype)
    rest = (jnp.uint32(0),) * (rows.ndim - 1)

    level = level.astype(jnp.int32)

    def put(whole, block, distance, start=0):
        return lax.dynamic_update_slice(
            whole,
            block[None],
            ((level + distance + 8 & 7).astype(jnp.uint32), jnp.uint32(start), *rest)
        )

    whole = put(whole, rows, 0)
    below = above = rows
    for k in (1, 2, 3):
        below, above = lax.ppermute(below, "z", up), lax.ppermute(above, "z", down)
        below, above = lax.optimization_barrier((below, above))
        whole = put(put(whole, below, -k), above, k)
    whole = put(whole, lax.ppermute(below[:cut], "z", up), 4)
    return put(whole, lax.ppermute(above[cut:], "z", down), 4, cut)


def after(value, *others):
    return lax.optimization_barrier((value, *others))[0]


def after_all(values, *others):
    return lax.optimization_barrier((*values, *others))[: len(values)]


def swap_core(rows):
    return lax.ppermute(rows, "core", [(0, 1), (1, 0)])


def pair_of_float(values):
    high = values.astype(BF)
    return high, (values - high.astype(F32)).astype(BF)


def normalize(values):
    factor = lax.rsqrt(jnp.mean(values * values, axis=-1, keepdims=True) + EPS)
    return values * factor, factor


def norm_back(grad_normed, unit, factor, gain):
    scaled = grad_normed * gain
    inner = jnp.mean(scaled * unit, axis=-1, keepdims=True)
    return factor * (scaled - unit * inner)


def silu_slope(values, sig):
    return sig * (1.0 + values * (1.0 - sig))


def expert_kernel(member, own, below, above, far_up, far_down, own_o, below_o, above_o, far_up_o,
                  far_down_o, grad_own, grad_other, blocks, shared_mine, shared_other, back_own, back_other, mixed, grad_pre, normed, w_down,
                  w_in, rows):
    step = pl.program_id(0)

    @pl.when(step == 0)
    def _():
        for b in range(8):
            flip = (b >> 2) ^ (member[0] >> 2)
            first = flip * 4 + ((b - member[0]) & 3)
            second = (1 - flip) * 4 + ((b - member[0] - 2) & 3)
            w_in[b * 192 : (b + 1) * 192, :896] = blocks[first, :, :896]
            w_in[b * 192 : (b + 1) * 192, 896:] = blocks[second, :, 896:1280]
            for k in range(3):
                w_down[b * 64 : (b + 1) * 64, k * 512 : (k + 1) * 512] = blocks[
                    second, k * 64 : (k + 1) * 64, 1280:
                ]

        @pl.when(member[2] == 0)
        def _():
            w_down[FE:] = shared_other[...]

        @pl.when(member[2] != 0)
        def _():
            w_down[FE:] = shared_mine[...]

        at = 0
        for piece in (own, below, above, far_up, far_down, own_o, below_o, above_o, far_up_o,
                      far_down_o):
            rows[at : at + piece.shape[0]] = piece[...]
            at += piece.shape[0]

    part = pl.ds(pl.multiple_of(step * 256, 256), 256)
    x = rows[part, :D]
    lane = lax.broadcasted_iota(jnp.int32, (256, 128), 1)
    expert = member[1]
    high, low = lane == expert, lane == expert + 8
    gate = jnp.sum(
        jnp.where(high | low, rows[part, D:].astype(F32), 0.0), axis=1, keepdims=True
    )
    back_down = dot_rows(jnp.where(step < 2, grad_own[...], grad_other[...]), w_down[...])
    pre = dot(x, w_in[...])
    gate_part, up_part = pre[:, :FE], pre[:, FE : 2 * FE]
    shared_gate, shared_up = pre[:, 2 * FE : 2 * FE + 128], pre[:, 2 * FE + 128 :]
    gate_sig = jax.nn.sigmoid(gate_part)
    gate_act = gate_part * gate_sig
    activ = gate_act * up_part
    shared_sig = jax.nn.sigmoid(shared_gate)
    shared_silu = shared_gate * shared_sig
    grad_mixed, grad_shared = back_down[:, :FE], back_down[:, FE:]
    grad_gate = jnp.sum(grad_mixed * activ, axis=1, keepdims=True)
    grad_activ = grad_mixed * gate
    mixed[:, :FE] = (gate * activ).astype(BF)
    mixed[:, FE:] = (shared_silu * shared_up).astype(BF)
    grad_pre[:, :FE] = (grad_activ * up_part * silu_slope(gate_part, gate_sig)).astype(BF)
    grad_pre[:, FE : 2 * FE] = (grad_activ * gate_act).astype(BF)
    grad_pre[:, 2 * FE : 2 * FE + 128] = (
        grad_shared * shared_up * silu_slope(shared_gate, shared_sig)
    ).astype(BF)
    grad_pre[:, 2 * FE + 128 :] = (grad_shared * shared_silu).astype(BF)
    normed[...] = x
    back = dot_rows(grad_pre[...], w_in[...]).astype(BF)
    top = grad_gate.astype(BF).astype(F32)
    tail = jnp.where(high, top, jnp.where(low, grad_gate - top, 0.0)).astype(BF)

    @pl.when(step < 2)
    def _():
        back_own[:, :D], back_own[:, D:] = back, tail

    @pl.when(step >= 2)
    def _():
        back_other[:, :D], back_other[:, D:] = back, tail


def lower_chunk(n):
    return pl.BlockSpec((256, n), lambda i, *_: (jnp.minimum(i, 1), 0))


def upper_chunk(n):
    return pl.BlockSpec((256, n), lambda i, *_: (jnp.maximum(i - 2, 0), 0))


def expert_pass(scalars, pieces, grad_own, grad_other, blocks, shared_mine, shared_other):
    whole = lambda a: pl.BlockSpec(a.shape, lambda i, *_, n=a.ndim: (0,) * n)
    chunk = lambda n: pl.BlockSpec((256, n), lambda i, *_: (i, 0))
    shape = lambda n, rows=1024: jax.ShapeDtypeStruct((rows, n), BF)
    return pl.pallas_call(
        expert_kernel,
        out_shape=(shape(1664, 512), shape(1664, 512), shape(640), shape(1280), shape(D), shape(D, 640)),
        grid_spec=pltpu.PrefetchScalarGridSpec(
            num_scalar_prefetch=1,
            grid=(4,),
            in_specs=[
                *(whole(p) for p in pieces),
                lower_chunk(D),
                upper_chunk(D),
                whole(blocks),
                whole(shared_mine),
                whole(shared_other),
            ],
            out_specs=(
                lower_chunk(1664),
                upper_chunk(1664),
                chunk(640),
                chunk(1280),
                chunk(D),
                pl.BlockSpec((640, D), lambda i, *_: (0, 0)),
            ),
            scratch_shapes=[
                pltpu.VMEM((D, 1280), BF),
                pltpu.VMEM((1024, 1664), BF),
            ],
        ),
        compiler_params=pltpu.CompilerParams(vmem_limit_bytes=56 << 20),
        cost_estimate=pl.CostEstimate(
            flops=2 * 1024 * D * 3200, bytes_accessed=30 << 20, transcendentals=1024 * 640
        ),
    )(scalars, *pieces, grad_own, grad_other, blocks, shared_mine, shared_other)


def expert_grad_kernel(normed, grad_pre, mixed, shared, own, other, own_cols, other_cols, out):
    into = dot_cols(normed[...], grad_pre[...])
    down = dot_cols(mixed[:512], own[...]) + dot_cols(mixed[512:], other[...])
    side = dot_cols(shared[:512], own_cols[...]) + dot_cols(shared[512:], other_cols[...])
    for b in range(2):
        for z in range(8):
            at = b * 64 + z * 8
            folded = jnp.concatenate(
                [down[at : at + 8, k * 512 : (k + 1) * 512] for k in range(3)], axis=0
            )
            mine = jnp.concatenate(
                [side[z * 16 + b * 8 : z * 16 + b * 8 + 8, k * 128 : (k + 1) * 128] for k in range(3)],
                axis=0,
            )
            out[z, b] = jnp.concatenate(
                [
                    into[b * 192 + z * 24 : b * 192 + z * 24 + 24],
                    folded,
                    mine,
                ],
                axis=1,
            ).astype(BF)


def expert_grads(normed, grad_pre, mixed, grad_own, grad_other):
    return pl.pallas_call(
        expert_grad_kernel,
        out_shape=jax.ShapeDtypeStruct((8, 8, 24, 1920), BF),
        grid=(4,),
        in_specs=[
            pl.BlockSpec((1024, 384), lambda j: (0, j)),
            pl.BlockSpec((1024, 1280), lambda j: (0, 0)),
            pl.BlockSpec((1024, 128), lambda j: (0, j)),
            pl.BlockSpec((1024, 128), lambda j: (0, 4)),
            pl.BlockSpec((512, D), lambda j: (0, 0)),
            pl.BlockSpec((512, D), lambda j: (0, 0)),
            pl.BlockSpec((512, 384), lambda j: (0, j)),
            pl.BlockSpec((512, 384), lambda j: (0, j)),
        ],
        out_specs=pl.BlockSpec((8, 2, 24, 1920), lambda j: (0, j, 0, 0)),
        compiler_params=pltpu.CompilerParams(vmem_limit_bytes=56 << 20),
        cost_estimate=pl.CostEstimate(
            flops=2 * 1024 * D * 1920, bytes_accessed=22 << 20, transcendentals=0
        ),
    )(normed, grad_pre, mixed, mixed, grad_own, grad_other, grad_own, grad_other)


def full(a):
    return pl.BlockSpec(a.shape, lambda *_, n=len(a.shape): (0,) * n)


def on_chip(kernel, scalars, args, outs, scratch=(), flops=0, exps=0):
    size = sum(math.prod(a.shape) * a.dtype.itemsize for a in (*args, *outs))
    return pl.pallas_call(
        kernel,
        out_shape=tuple(outs),
        grid_spec=pltpu.PrefetchScalarGridSpec(
            num_scalar_prefetch=1,
            grid=(1,),
            in_specs=[full(a) for a in args],
            out_specs=tuple(full(a) for a in outs),
            scratch_shapes=list(scratch),
        ),
        compiler_params=pltpu.CompilerParams(vmem_limit_bytes=56 << 20),
        cost_estimate=pl.CostEstimate(flops=flops, bytes_accessed=size, transcendentals=exps),
    )(scalars, *args)


def out(*shape, dtype=BF):
    return jax.ShapeDtypeStruct(shape, dtype)


PIECES = ((0, 128), (128, 128), (256, 128), (384, 64), (448, 64))


def pack_kernel(core, query, key, value, small, slots):
    rows = pl.ds(pl.multiple_of(core[0] * 96, 32), 96)
    for k, head in enumerate(KEY_HEAD):
        for slot in (k, k + 4):
            slots[slot, :96, :384] = query[rows, head * 384 : (head + 1) * 384]
            slots[slot, :96, 384:512] = key[rows, head * 128 : (head + 1) * 128]
            slots[slot, :96, 512:] = value[rows, head * 128 : (head + 1) * 128]
            slots[slot, 96:] = small[...]


def keys_kernel(core, own, below, above, far_up, far_down, gain, got, other, normed, kv, weight):
    for b in range(8):
        first = pl.multiple_of(b * 192 + core[0] * 96, 32)
        second = pl.multiple_of(b * 192 + (1 - core[0]) * 96, 32)
        weight[pl.ds(first, 96)] = got[b, :96]
        weight[pl.ds(second, 96)] = other[b]
    for (at, size), piece in zip(PIECES, (own, below, above, far_up, far_down)):
        unit, _ = normalize(piece[...].astype(F32))
        normed[at : at + size] = (unit * gain[...]).astype(BF)
    kv[...] = dot(normed[...], weight[:, GROUP * HEAD :]).astype(BF)


def query_kernel(core, normed, weight, kv, query):
    query[...] = dot(normed[...], weight[:, : GROUP * HEAD]).astype(BF)


def mask_of(query_at, query_seg, key_at, key_seg):
    return (query_at == key_at) | (
        (key_at < query_at) & (query_seg == key_seg) & (key_seg != 0)
    )


def attend_kernel(core, query, kv, kv_other, qat, qseg, kat, kseg, attended, logs):
    allowed = mask_of(qat[...], qseg[...], kat[...], kseg[...])
    keys = jnp.concatenate([kv[:, :HEAD], kv_other[:, :HEAD]], axis=0)
    values = jnp.concatenate([kv[:, HEAD:], kv_other[:, HEAD:]], axis=0)
    lane = lax.broadcasted_iota(jnp.int32, (512, 128), 1)
    kept = jnp.zeros((512, 128), F32)
    for g in range(GROUP):
        scores = dot_rows(query[:, g * HEAD : (g + 1) * HEAD], keys) * SCALE
        scores = jnp.where(allowed, scores, -1e30)
        top = jnp.max(scores, axis=1, keepdims=True)
        expo = jnp.exp(scores - top)
        total = jnp.sum(expo, axis=1, keepdims=True)
        kept = jnp.where(lane == g, top + jnp.log(total), kept)
        attended[:, g * HEAD : (g + 1) * HEAD] = dot((expo / total).astype(BF), values).astype(BF)
    logs[...] = kept


def output_kernel(core, attended, mine, other, own, below, above, far_up, far_down, weight):
    for c in range(2):
        @pl.when(core[0] == c)
        def _():
            weight[c * 192 : (c + 1) * 192] = mine[...]
            weight[(1 - c) * 192 : (2 - c) * 192] = other[...]
    whole = dot(attended[...], weight[...]).astype(BF)
    for (at, size), piece in zip(PIECES, (own, below, above, far_up, far_down)):
        piece[...] = whole[at : at + size]


def attend_back_kernel(core, own, below, above, far_up, far_down, query, kv, kv_other, qat, qseg, kat, kseg,
                       mine, other, logs, grad, grad_query, grad_own, grad_other, weight):
    for c in range(2):
        @pl.when(core[0] == c)
        def _():
            weight[c * 192 : (c + 1) * 192] = mine[...]
            weight[(1 - c) * 192 : (2 - c) * 192] = other[...]
    for (at, size), piece in zip(PIECES, (own, below, above, far_up, far_down)):
        grad[at : at + size] = piece[...]
    grad_att = dot_rows(grad[...], weight[...]).astype(BF)
    allowed = mask_of(qat[...], qseg[...], kat[...], kseg[...])
    keys = jnp.concatenate([kv[:, :HEAD], kv_other[:, :HEAD]], axis=0)
    values = jnp.concatenate([kv[:, HEAD:], kv_other[:, HEAD:]], axis=0)
    grad_keys = jnp.zeros((1024, HEAD), F32)
    grad_values = jnp.zeros((1024, HEAD), F32)
    for g in range(GROUP):
        queries = query[:, g * HEAD : (g + 1) * HEAD]
        heads = grad_att[:, g * HEAD : (g + 1) * HEAD]
        scores = jnp.where(allowed, dot_rows(queries, keys) * SCALE, -1e30)
        probs = jnp.exp(scores - logs[:, g : g + 1])
        grad_probs = dot_rows(heads, values)
        inner = jnp.sum(probs * grad_probs, axis=1, keepdims=True)
        grad_scores = (probs * (grad_probs - inner)).astype(BF)
        grad_query[:, g * HEAD : (g + 1) * HEAD] = (dot(grad_scores, keys) * SCALE).astype(BF)
        grad_keys += dot_cols(grad_scores, queries)
        grad_values += dot_cols(probs.astype(BF), heads)
    grad_keys = grad_keys * SCALE
    grad_own[:, :HEAD] = grad_keys[:512]
    grad_own[:, HEAD:] = grad_values[:512]
    grad_other[:, :HEAD] = grad_keys[512:].astype(BF)
    grad_other[:, HEAD:] = grad_values[512:].astype(BF)


def early_grads_kernel(core, grad_query, weight, normed, attended, grad, query, outs, column):
    into = dot_cols(normed[...], grad_query[...])
    column[...] = jnp.sum(into * weight[:, : GROUP * HEAD].astype(F32), axis=1, keepdims=True)
    sums = dot_cols(attended[...], grad[...])
    for z in range(8):
        for b in range(8):
            query[z, b] = into[b * 192 + z * 24 : b * 192 + z * 24 + 24].astype(BF)
        for c in range(2):
            for j in range(2):
                for k in range(2):
                    outs[c, z, j * 2 + k] = sums[
                        j * 192 + z * 24 : j * 192 + z * 24 + 24,
                        c * 768 + k * 384 : c * 768 + (k + 1) * 384,
                    ].astype(BF)


def weight_grads_kernel(core, grad_kv, from_other, weight, normed, small, gain, column, query, outs,
                        keep, give, back_kv):
    back_kv[...] = (grad_kv[...] + from_other[...].astype(F32)).astype(BF)
    into = dot_cols(normed[...], back_kv[...])
    late = jnp.sum(into * weight[:, GROUP * HEAD :].astype(F32), axis=1, keepdims=True)
    lane = lax.broadcasted_iota(jnp.int32, (D, 128), 1)
    side = jnp.where(lane == 9, (column[...] + late) / gain[...], small[...])

    def put(first, second):
        first[:, :8] = query[...]
        first[:, 8:] = outs[0]
        second[:, 8:] = outs[1]
        for z in range(8):
            for b in range(8):
                rows = slice(b * 192 + z * 24, b * 192 + z * 24 + 24)
                second[z, b] = jnp.concatenate([into[rows], side[rows]], axis=1).astype(BF)

    @pl.when(core[0] == 0)
    def _():
        put(keep, give)

    @pl.when(core[0] == 1)
    def _():
        put(give, keep)


def input_back_kernel(core, query, kv, weight, own, below, above, far_up, far_down, both):
    both[:, : GROUP * HEAD] = query[...]
    both[:, GROUP * HEAD :] = kv[...]
    back = dot_rows(both[...], weight[...]).astype(BF)
    for (at, size), piece in zip(PIECES, (own, below, above, far_up, far_down)):
        piece[...] = back[at : at + size]


def settle_experts_kernel(half, whole, expert_in, shared_in, expert_out, shared_out):
    low = [whole[0, 0, e // 4, e % 4, :, :896].astype(F32) for e in range(8)]
    high = [whole[0, 1, e // 4, e % 4, :, :896].astype(F32) for e in range(8)]
    expert_in[:, :, :896] = jnp.transpose(jnp.stack(low), (1, 0, 2))
    expert_in[:, :, 896:] = jnp.transpose(jnp.stack([h[:, :128] for h in high]), (1, 0, 2))
    for e in range(8):
        shared_in[:, e * 128 : (e + 1) * 128] = high[e][:, 128:256]
        shared_in[:, FS + e * 128 : FS + (e + 1) * 128] = high[e][:, 256:384]
        for k in range(3):
            expert_out[e, :, k * 512 : (k + 1) * 512] = high[e][k * 8 : (k + 1) * 8, 384:]
    for y in range(2):
        for j in range(4):
            side = whole[0, y, half[0], j, :, 896:].astype(F32)
            for k in range(3):
                lanes = j * 384 + k * 128
                shared_out[y * 8 : (y + 1) * 8, lanes : lanes + 128] = side[k * 8 : (k + 1) * 8]


def settle_experts(half, whole):
    f32 = lambda *s: jax.ShapeDtypeStruct(s, F32)
    return pl.pallas_call(
        settle_experts_kernel,
        out_shape=(f32(192, EXPERTS, 1024), f32(192, 2 * FS), f32(8, 64, D), f32(128, D)),
        grid_spec=pltpu.PrefetchScalarGridSpec(
            num_scalar_prefetch=1,
            grid=(8,),
            in_specs=[pl.BlockSpec((1, 2, 2, 4, 24, 1024), lambda z, *_: (z,) + (0,) * 5)],
            out_specs=(
                pl.BlockSpec((24, EXPERTS, 1024), lambda z, *_: (z, 0, 0)),
                pl.BlockSpec((24, 2 * FS), lambda z, *_: (z, 0)),
                pl.BlockSpec((8, 8, D), lambda z, *_: (0, z, 0)),
                pl.BlockSpec((16, D), lambda z, *_: (z, 0)),
            ),
        ),
        compiler_params=pltpu.CompilerParams(vmem_limit_bytes=56 << 20),
        cost_estimate=pl.CostEstimate(flops=0, bytes_accessed=19 << 20, transcendentals=0),
    )(half, whole)


def piece_kernel(place, same, below, above, across, side, piece):
    for ref, distance in ((same, 0), (below, 3), (above, 1), (across, 2)):
        piece[lax.rem(place[0] + distance, 4), :, :896] = ref[...]
    piece[:, :, 896:] = side[...]


def settle_kernel(core, mine, other, query, key, value, router, gains, outs, small):
    small[192:] = jnp.zeros((64, 128), F32)

    def put(first, second):
        for z in range(8):
            rows = slice(z * 24, (z + 1) * 24)
            sums = jnp.zeros((24, 128), F32)
            for k, head in enumerate(KEY_HEAD):
                query[rows, head * 384 : (head + 1) * 384] = first[z, k].astype(F32)
                key[rows, head * 128 : (head + 1) * 128] = second[z, k, :, :128].astype(F32)
                value[rows, head * 128 : (head + 1) * 128] = second[z, k, :, 128:256].astype(F32)
                sums += second[z, k, :, 256:].astype(F32)
            router[rows] = sums[:, :8]
            small[rows] = sums
            for k in range(2):
                outs[rows, k * 384 : (k + 1) * 384] = first[z, 4 + k].astype(F32)
                outs[rows, (2 + k) * 384 : (3 + k) * 384] = second[z, 4 + k].astype(F32)

    @pl.when(core[0] == 0)
    def _():
        put(mine, other)

    @pl.when(core[0] == 1)
    def _():
        put(other, mine)

    gains[...] = small[...].T[8:16, :192]


def shards(
    tokens,
    segment_ids,
    routes,
    gain_attn,
    w_query,
    w_key,
    w_value,
    w_out,
    gain_ffn,
    w_router,
    w_shared_in,
    w_shared_out,
    w_expert_in,
    w_expert_out,
    cotangent,
):
    level, core, half, place = (
        lax.axis_index(a).astype(jnp.uint32) for a in ("z", "core", "yhi", "x")
    )
    rows = tokens.shape[0]
    zero = jnp.uint32(0)

    member = half * 4 + place
    key_head = jnp.where((place == 1) | (place == 2), 3 - place, place)

    tokens_x = spread_x(tokens)
    at_core = core.reshape(1).astype(jnp.int32)
    small = jnp.concatenate([gain_attn[None], gain_ffn[None], w_router.T], axis=0)
    small = jnp.pad(small, ((0, 6), (0, 448)))
    (slots,) = on_chip(
        pack_kernel, at_core, (w_query, w_key, w_value, small), (out(8, 112, 640),)
    )
    got = exchange(slots, FSDP)
    small = got[:, 96:106, :192].transpose(1, 0, 2).reshape(10, D)
    gain_one = small[:1].astype(F32)
    gain_two = small[1:2].astype(F32)
    router = small[2:]

    w_out_late, *_ = lax.optimization_barrier((w_out, *tokens_x[1:3]))
    out_mine = lax.ppermute(
        w_out_late,
        ("core", "yhi", "x"),
        [(s * 8 + b, (b % 2) * 8 + s * 4 + KEY_HEAD[b // 2]) for s in range(2) for b in range(8)],
    )

    qkv_other = swap_core(after(got[:, :96], *tokens_x[3:]))
    turn, flip = level & 3, level >> 2
    first, second = core * 4 + ((place - turn) & 3), core * 4 + ((place - turn - 2) & 3)
    halves = (
        lax.dynamic_slice(w_expert_in, (zero, first, zero), (192, 1, 896)).reshape(192, 896),
        jnp.concatenate(
            [
                lax.dynamic_slice(w_expert_in, (zero, second, zero + 896), (192, 1, 128)).reshape(
                    192, 128
                ),
                lax.dynamic_slice(w_shared_in, (zero, second * 128), (192, 128)),
                lax.dynamic_slice(w_shared_in, (zero, second * 128 + FS), (192, 128)),
                lax.dynamic_slice(w_expert_out, (second, zero, zero), (1, 64, D))
                .reshape(64, 3, 512)
                .transpose(1, 0, 2)
                .reshape(192, 512),
            ],
            axis=1,
        ),
    )
    halves = after_all(halves, slots)
    halves = [
        lax.ppermute(
            part,
            ("z", *FSDP),
            [
                (z * 8 + h * 4 + x, z * 8 + (h ^ (z >> 2) ^ k) * 4 + ((x - z - 2 * k) & 3))
                for z in range(8)
                for h in range(2)
                for x in range(4)
            ],
        )
        for k, part in enumerate(halves)
    ]
    block = after(jnp.concatenate(halves, axis=1), got, *tokens_x[3:])
    blocks = lax.all_gather(block, "z")
    inputs = tokens.astype(F32)
    normed_one, kv, w_qkv = on_chip(
        keys_kernel,
        at_core,
        (*tokens_x, gain_one, got, qkv_other),
        (out(512, D), out(512, 256), out(D, 640)),
        flops=2 * 512 * D * 256,
    )
    kv_other = lax.ppermute(kv, "yhi", [(0, 1)])
    (query,) = on_chip(
        query_kernel, at_core, (normed_one, w_qkv, kv), (out(512, 384),), flops=2 * 512 * D * 384
    )
    grad_late = after(cotangent, kv)
    grad_below, grad_above = up_x(grad_late), down_x(grad_late)
    out_other = swap_core(after(out_mine, kv_other, query))
    starts = [((place + k) & 3) * 128 for k in (0, 3, 1, 2)]
    pos = jnp.concatenate([s.astype(jnp.int32) + jnp.arange(128, dtype=jnp.int32) for s in starts])
    seg_own = jnp.concatenate(
        [lax.dynamic_slice_in_dim(segment_ids, half * 512 + s, 128) for s in starts]
    )
    seg_other = jnp.concatenate([lax.dynamic_slice_in_dim(segment_ids, s, 128) for s in starts])
    pos_other = jnp.where(half == 1, pos - 512, 1 << 20)
    places = (
        pos[:, None],
        seg_own[:, None],
        jnp.concatenate([pos, pos_other])[None],
        jnp.concatenate([seg_own, seg_other])[None],
    )
    part = [out(size, D) for _, size in PIECES]
    attended, logs = on_chip(
        attend_kernel,
        at_core,
        (query, kv, kv_other, *places),
        (out(512, 384), out(512, 128, dtype=F32)),
        flops=2 * 512 * 384 * 2048,
        exps=3 * 512 * 1024,
    )
    hidden_part = on_chip(
        output_kernel,
        at_core,
        (attended, out_mine, out_other),
        part,
        scratch=[pltpu.VMEM((384, D), BF)],
        flops=2 * 512 * 384 * D,
    )
    hidden_near = near_pieces(hidden_part, far_pieces(hidden_part))
    far_up, far_down = after_all((grad_below[:64], grad_above[64:]), *hidden_near)
    grad_x = (cotangent, grad_below, grad_above, up_x(far_up), down_x(far_down))
    shared_other = lax.ppermute(after(w_shared_out, attended), ("core", "yhi"), [(0, 1), (3, 2)])
    grad_own = jnp.concatenate(grad_x, axis=0)
    grad_other = swap_core(grad_own)
    above, below = hidden_near
    hidden = inputs + near_sum(hidden_part[0], up_x(above), down_x(below))

    unit_two, factor_two = normalize(hidden)
    normed_two = (unit_two * gain_two).astype(BF)
    logits = dot_rows(normed_two, router)
    chosen = jnp.sum(
        (routes[:, :, None] == jnp.arange(EXPERTS, dtype=jnp.int32)[None, None, :]).astype(F32),
        axis=1,
    )
    weighted = chosen * jnp.exp(logits)
    gates = weighted / jnp.sum(weighted, axis=-1, keepdims=True)
    packed = jnp.concatenate(
        [normed_two, *pair_of_float(gates), jnp.zeros((rows, 112), BF)], axis=1
    )
    packed = spread_x(after(packed, *grad_x[3:]))
    packed = (*packed, *(swap_core(p) for p in packed))

    scalars = jnp.stack([member, core * 4 + place, (core == half).astype(jnp.uint32)])
    back_own, back_other, mixed, grad_pre, normed_all, w_down = expert_pass(
        scalars.astype(jnp.int32), packed, grad_own, grad_other, blocks, w_shared_out, shared_other
    )
    back_other = swap_core(back_other)
    back_part = [plus(o, s) for o, s in zip(pieces_of(back_own), pieces_of(back_other))]
    normed_all, _, _ = lax.optimization_barrier((normed_all, back_part[3], back_part[4]))
    flat = expert_grads(normed_all, grad_pre, mixed, grad_own, grad_other)
    back_sum, flat_ffn = collect_x(back_part, flat)

    grad_gates = back_sum[:, D : D + 8] + back_sum[:, D + 8 : D + 16]
    grad_logits = (
        gates * (grad_gates - jnp.sum(gates * grad_gates, axis=-1, keepdims=True))
    ).astype(BF)
    grad_normed_two = back_sum[:, :D] + dot(grad_logits, router)
    grad_router = dot_cols(normed_two, jnp.pad(grad_logits, ((0, 0), (0, 120))))
    grad_gain_ffn = jnp.sum(grad_normed_two * unit_two, axis=0, keepdims=True)
    grad_hidden = cotangent.astype(F32) + norm_back(
        grad_normed_two, unit_two, factor_two, gain_two
    )
    grad_hidden_low = grad_hidden.astype(BF)
    hidden_low = spread_x(grad_hidden_low)
    result_part = dot(after(mixed, grad_hidden_low), w_down).astype(BF)
    hidden_low = (after(hidden_low[0], result_part), *hidden_low[1:])

    grad_low, grad_query, grad_kv, to_other = on_chip(
        attend_back_kernel,
        at_core,
        (*hidden_low, query, kv, kv_other, *places, out_mine, out_other, logs),
        (out(512, D), out(512, 384), out(512, 256, dtype=F32), out(512, 256)),
        scratch=[pltpu.VMEM((384, D), BF)],
        flops=2 * 512 * 384 * 6656,
        exps=3 * 512 * 1024,
    )
    from_other = lax.ppermute(to_other, "yhi", [(1, 0)])
    small = grad_router + jnp.pad(grad_gain_ffn.T, ((0, 0), (8, 119)))
    query_sums, outs_sums, column = on_chip(
        early_grads_kernel,
        at_core,
        (grad_query, w_qkv, normed_one, attended, grad_low),
        (out(8, 8, 24, 384), out(2, 8, 4, 24, 384), out(D, 1, dtype=F32)),
        flops=2 * 512 * D * 768,
    )
    keep, give, back_kv = on_chip(
        weight_grads_kernel,
        at_core,
        (
            grad_kv,
            from_other,
            w_qkv,
            normed_one,
            small,
            gain_one.reshape(D, 1),
            column,
            query_sums,
            outs_sums,
        ),
        (out(8, 12, 24, 384), out(8, 12, 24, 384), out(512, 256)),
        flops=2 * 512 * D * 256,
    )

    flat = plus(keep, swap_core(give))
    flat_sent = flat
    result_other = swap_core(after(result_part[512:], flat_sent))
    flat = exchange(flat, "z")
    ffn = lax.psum_scatter(flat_ffn, "z", scatter_dimension=0, tiled=True)[0]
    ffn = after(ffn, flat_sent)
    side = ffn[..., 1792:].reshape(4, 2, 24, 128)
    main = ffn[..., :1792].reshape(2, 4, 24, 1792)
    both = [
        jnp.concatenate([m[..., :896], side[:, 0], m[..., 896:], side[:, 1]], axis=-1)
        for m in (main[0], main[1])
    ]
    keep = jnp.where(half == 0, both[0], both[1])
    away = jnp.where(half == 0, both[1], both[0])
    ffn = plus(keep, lax.ppermute(away, "yhi", [(0, 1), (1, 0)]))
    here = lax.axis_index("ylo")
    keep = jnp.where(here == 0, ffn[..., :1024], ffn[..., 1024:])
    away = jnp.where(here == 0, ffn[..., 1024:], ffn[..., :1024])
    ffn = plus(keep, lax.ppermute(away, "ylo", [(0, 1), (1, 0)]))
    to = [
        lax.dynamic_index_in_dim(ffn[..., :896], (place + k) & 3, 0, False) for k in (0, 1, 3, 2)
    ]
    across = lax.ppermute(to[3], "x", [(i, (i + 2) % 4) for i in range(4)])
    (piece,) = on_chip(
        piece_kernel,
        place.reshape(1).astype(jnp.int32),
        (to[0], up_x(to[1]), down_x(to[2]), across, ffn[..., 896:]),
        (out(4, 24, 1024),),
    )
    whole = lax.all_gather(after(piece, flat, result_other), REP).reshape(8, 2, 2, 4, 24, 1024)
    flat = jnp.sum(flat.astype(F32), axis=0).astype(BF)
    outs = lax.dynamic_update_slice(
        jnp.zeros((8, 2, 24, 384), BF), flat[8:].reshape(2, 2, 24, 384), (2 * key_head, *(jnp.uint32(0),) * 3)
    )
    flat = jnp.concatenate([flat[:8, None], outs], axis=1)
    flat = jnp.concatenate([flat, flat], axis=0)
    result_part = [
        plus(o, s)
        for o, s in zip(pieces_of(result_part[:512]), pieces_of(after(result_other, flat)))
    ]
    back_one = on_chip(
        input_back_kernel,
        at_core,
        (after(grad_query, flat), back_kv, w_qkv),
        part,
        scratch=[pltpu.VMEM((512, 640), BF)],
        flops=2 * 512 * D * 640,
    )
    got = exchange(flat, PLANE).reshape(4, 4, 3, 24, 384)
    got = jnp.sum(got.astype(F32), axis=0)
    mine = jnp.concatenate([got[:, 0], jnp.sum(got[:, 1:], axis=0)], axis=0).astype(BF)
    result = (hidden + collect_x(result_part, gate=got)).astype(BF)
    mine = spread_z(mine, level)
    above, below = after_all(near_pieces(back_one, far_pieces(back_one)), mine)
    back_near = up_x(above), down_x(below)
    sum_query, sum_key, sum_value, sum_router, sum_gains, sum_out = on_chip(
        settle_kernel,
        at_core,
        (mine, swap_core(mine)),
        (
            out(192, D, dtype=F32),
            out(192, 512, dtype=F32),
            out(192, 512, dtype=F32),
            out(192, EXPERTS, dtype=F32),
            out(8, 192, dtype=F32),
            out(192, D, dtype=F32),
        ),
        scratch=[pltpu.VMEM((256, 128), F32)],
    )

    at_half = half.reshape(1).astype(jnp.int32)
    sum_expert_in, sum_shared_in, sum_expert_out, sum_shared_out = settle_experts(
        at_half, after(whole, sum_query, result)
    )

    back_one = near_sum(back_one[0], *after_all(back_near, sum_expert_in))
    unit_own, factor_own = normalize(inputs)
    grad_input = (grad_hidden + norm_back(back_one, unit_own, factor_own, gain_one)).astype(BF)

    return (
        result,
        grad_input,
        sum_gains[1],
        sum_query,
        sum_key,
        sum_value,
        sum_out,
        sum_gains[0],
        sum_router,
        sum_shared_in,
        sum_shared_out,
        sum_expert_in,
        sum_expert_out,
    )


def solution(mesh):
    fine = Mesh(mesh.devices.reshape(SIZES), AXES)
    tokens = P((*REP, *FSDP), None)
    first = P(FSDP, None)
    return jax.shard_map(
        shards,
        mesh=fine,
        in_specs=(
            tokens,
            P(REP),
            tokens,
            P(FSDP),
            first,
            first,
            first,
            first,
            P(FSDP),
            first,
            first,
            first,
            P(FSDP, None, None),
            P(None, FSDP, None),
            tokens,
        ),
        out_specs=(
            tokens,
            tokens,
            P(FSDP),
            first,
            first,
            first,
            first,
            P(FSDP),
            first,
            first,
            first,
            P(FSDP, None, None),
            P(None, FSDP, None),
        ),
        check_vma=False,
    )
```

```python
import math

import jax
import jax.numpy as jnp
from jax import lax
from jax.experimental import pallas as pl
from jax.experimental.pallas import tpu as pltpu
from jax.sharding import Mesh, PartitionSpec as P

HEADS = 12
KV_HEADS = 4
HEAD = 128
GROUP = HEADS // KV_HEADS
D = 1536
FE = 512
FS = 1024
EXPERTS = 8
EPS = 1e-05
SCALE = 1.0 / math.sqrt(HEAD)

AXES = ("z", "ylo", "core", "yhi", "x")
SIZES = (8, 2, 2, 2, 4)
REP = ("z", "ylo", "core")
FSDP = ("yhi", "x")
PLANE = ("ylo", "yhi", "x")
KEY_HEAD = (0, 2, 1, 3)
BF = jnp.bfloat16
F32 = jnp.float32


def dot(left, right):
    return jnp.dot(left, right, preferred_element_type=F32)


def dot_rows(left, right):
    return lax.dot_general(left, right, (((1,), (1,)), ((), ())), preferred_element_type=F32)


def dot_cols(left, right):
    return lax.dot_general(left, right, (((0,), (0,)), ((), ())), preferred_element_type=F32)


def exchange(blocks, axes):
    return lax.all_to_all(blocks, axes, 0, 0, tiled=True)


def up_x(rows):
    return lax.ppermute(rows, "x", [(i, (i + 1) % 4) for i in range(4)])


def down_x(rows):
    return lax.ppermute(rows, "x", [(i, (i + 3) % 4) for i in range(4)])


def spread_x(rows):
    cut = rows.shape[0] // 2
    below, above = up_x(rows), down_x(rows)
    return rows, below, above, up_x(below[:cut]), down_x(above[cut:])


def pieces_of(rows):
    return tuple(rows[at : at + size] for at, size in PIECES)


def collect_x(pieces, beside=None, gate=None):
    above, below = near_pieces(pieces, far_pieces(pieces))
    if gate is not None:
        above, below = after_all((above, below), gate)
    if beside is not None:
        above, below, beside = lax.optimization_barrier((above, below, beside))
    total = near_sum(pieces[0], up_x(above), down_x(below))
    return total if beside is None else (total, beside)


def far_pieces(pieces):
    return up_x(pieces[3]), down_x(pieces[4])


def near_pieces(pieces, far):
    _, below, above, *_ = pieces
    cut = far[0].shape[0]
    above = jnp.concatenate([plus(above[:cut], far[0]), above[cut:]], axis=0)
    below = jnp.concatenate([below[:cut], plus(below[cut:], far[1])], axis=0)
    return above, below


def near_sum(own, below, above):
    return own.astype(F32) + below.astype(F32) + above.astype(F32)


def plus(left, right):
    return (left.astype(F32) + right.astype(F32)).astype(BF)


def spread_z(rows, level):
    up = [(i, (i + 1) % 8) for i in range(8)]
    down = [(i, (i + 7) % 8) for i in range(8)]
    cut = rows.shape[0] // 2
    whole = jnp.zeros((8, *rows.shape), rows.dtype)
    rest = (jnp.uint32(0),) * (rows.ndim - 1)

    level = level.astype(jnp.int32)

    def put(whole, block, distance, start=0):
        return lax.dynamic_update_slice(
            whole,
            block[None],
            ((level + distance + 8 & 7).astype(jnp.uint32), jnp.uint32(start), *rest)
        )

    whole = put(whole, rows, 0)
    below = above = rows
    for k in (1, 2, 3):
        below, above = lax.ppermute(below, "z", up), lax.ppermute(above, "z", down)
        below, above = lax.optimization_barrier((below, above))
        whole = put(put(whole, below, -k), above, k)
    whole = put(whole, lax.ppermute(below[:cut], "z", up), 4)
    return put(whole, lax.ppermute(above[cut:], "z", down), 4, cut)


def after(value, *others):
    return lax.optimization_barrier((value, *others))[0]


def after_all(values, *others):
    return lax.optimization_barrier((*values, *others))[: len(values)]


def swap_core(rows):
    return lax.ppermute(rows, "core", [(0, 1), (1, 0)])


def pair_of_float(values):
    high = values.astype(BF)
    return high, (values - high.astype(F32)).astype(BF)


def normalize(values):
    factor = lax.rsqrt(jnp.mean(values * values, axis=-1, keepdims=True) + EPS)
    return values * factor, factor


def norm_back(grad_normed, unit, factor, gain):
    scaled = grad_normed * gain
    inner = jnp.mean(scaled * unit, axis=-1, keepdims=True)
    return factor * (scaled - unit * inner)


def silu_slope(values, sig):
    return sig * (1.0 + values * (1.0 - sig))


def expert_kernel(member, own, below, above, far_up, far_down, own_o, below_o, above_o, far_up_o,
                  far_down_o, grad_own, grad_other, blocks, shared_mine, shared_other, back_own, back_other, mixed, grad_pre, normed, w_down,
                  w_in, rows):
    step = pl.program_id(0)

    @pl.when(step == 0)
    def _():
        for b in range(8):
            flip = (b >> 2) ^ (member[0] >> 2)
            first = flip * 4 + ((b - member[0]) & 3)
            second = (1 - flip) * 4 + ((b - member[0] - 2) & 3)
            w_in[b * 192 : (b + 1) * 192, :896] = blocks[first, :, :896]
            w_in[b * 192 : (b + 1) * 192, 896:] = blocks[second, :, 896:1280]
            for k in range(3):
                w_down[b * 64 : (b + 1) * 64, k * 512 : (k + 1) * 512] = blocks[
                    second, k * 64 : (k + 1) * 64, 1280:
                ]

        @pl.when(member[2] == 0)
        def _():
            w_down[FE:] = shared_other[...]

        @pl.when(member[2] != 0)
        def _():
            w_down[FE:] = shared_mine[...]

        at = 0
        for piece in (own, below, above, far_up, far_down, own_o, below_o, above_o, far_up_o,
                      far_down_o):
            rows[at : at + piece.shape[0]] = piece[...]
            at += piece.shape[0]

    part = pl.ds(pl.multiple_of(step * 256, 256), 256)
    x = rows[part, :D]
    lane = lax.broadcasted_iota(jnp.int32, (256, 128), 1)
    expert = member[1]
    high, low = lane == expert, lane == expert + 8
    gate = jnp.sum(
        jnp.where(high | low, rows[part, D:].astype(F32), 0.0), axis=1, keepdims=True
    )
    back_down = dot_rows(jnp.where(step < 2, grad_own[...], grad_other[...]), w_down[...])
    pre = dot(x, w_in[...])
    gate_part, up_part = pre[:, :FE], pre[:, FE : 2 * FE]
    shared_gate, shared_up = pre[:, 2 * FE : 2 * FE + 128], pre[:, 2 * FE + 128 :]
    gate_sig = jax.nn.sigmoid(gate_part)
    gate_act = gate_part * gate_sig
    activ = gate_act * up_part
    shared_sig = jax.nn.sigmoid(shared_gate)
    shared_silu = shared_gate * shared_sig
    grad_mixed, grad_shared = back_down[:, :FE], back_down[:, FE:]
    grad_gate = jnp.sum(grad_mixed * activ, axis=1, keepdims=True)
    grad_activ = grad_mixed * gate
    mixed[:, :FE] = (gate * activ).astype(BF)
    mixed[:, FE:] = (shared_silu * shared_up).astype(BF)
    grad_pre[:, :FE] = (grad_activ * up_part * silu_slope(gate_part, gate_sig)).astype(BF)
    grad_pre[:, FE : 2 * FE] = (grad_activ * gate_act).astype(BF)
    grad_pre[:, 2 * FE : 2 * FE + 128] = (
        grad_shared * shared_up * silu_slope(shared_gate, shared_sig)
    ).astype(BF)
    grad_pre[:, 2 * FE + 128 :] = (grad_shared * shared_silu).astype(BF)
    normed[...] = x
    back = dot_rows(grad_pre[...], w_in[...]).astype(BF)
    top = grad_gate.astype(BF).astype(F32)
    tail = jnp.where(high, top, jnp.where(low, grad_gate - top, 0.0)).astype(BF)

    @pl.when(step < 2)
    def _():
        back_own[:, :D], back_own[:, D:] = back, tail

    @pl.when(step >= 2)
    def _():
        back_other[:, :D], back_other[:, D:] = back, tail


def lower_chunk(n):
    return pl.BlockSpec((256, n), lambda i, *_: (jnp.minimum(i, 1), 0))


def upper_chunk(n):
    return pl.BlockSpec((256, n), lambda i, *_: (jnp.maximum(i - 2, 0), 0))


def expert_pass(scalars, pieces, grad_own, grad_other, blocks, shared_mine, shared_other):
    whole = lambda a: pl.BlockSpec(a.shape, lambda i, *_, n=a.ndim: (0,) * n)
    chunk = lambda n: pl.BlockSpec((256, n), lambda i, *_: (i, 0))
    shape = lambda n, rows=1024: jax.ShapeDtypeStruct((rows, n), BF)
    return pl.pallas_call(
        expert_kernel,
        out_shape=(shape(1664, 512), shape(1664, 512), shape(640), shape(1280), shape(D), shape(D, 640)),
        grid_spec=pltpu.PrefetchScalarGridSpec(
            num_scalar_prefetch=1,
            grid=(4,),
            in_specs=[
                *(whole(p) for p in pieces),
                lower_chunk(D),
                upper_chunk(D),
                whole(blocks),
                whole(shared_mine),
                whole(shared_other),
            ],
            out_specs=(
                lower_chunk(1664),
                upper_chunk(1664),
                chunk(640),
                chunk(1280),
                chunk(D),
                pl.BlockSpec((640, D), lambda i, *_: (0, 0)),
            ),
            scratch_shapes=[
                pltpu.VMEM((D, 1280), BF),
                pltpu.VMEM((1024, 1664), BF),
            ],
        ),
        compiler_params=pltpu.CompilerParams(vmem_limit_bytes=56 << 20),
        cost_estimate=pl.CostEstimate(
            flops=2 * 1024 * D * 3200, bytes_accessed=30 << 20, transcendentals=1024 * 640
        ),
    )(scalars, *pieces, grad_own, grad_other, blocks, shared_mine, shared_other)


def expert_grad_kernel(normed, grad_pre, mixed, shared, own, other, own_cols, other_cols, out):
    into = dot_cols(normed[...], grad_pre[...])
    down = dot_cols(mixed[:512], own[...]) + dot_cols(mixed[512:], other[...])
    side = dot_cols(shared[:512], own_cols[...]) + dot_cols(shared[512:], other_cols[...])
    for b in range(2):
        for z in range(8):
            at = b * 64 + z * 8
            folded = jnp.concatenate(
                [down[at : at + 8, k * 512 : (k + 1) * 512] for k in range(3)], axis=0
            )
            mine = jnp.concatenate(
                [side[z * 16 + b * 8 : z * 16 + b * 8 + 8, k * 128 : (k + 1) * 128] for k in range(3)],
                axis=0,
            )
            out[z, b] = jnp.concatenate(
                [
                    into[b * 192 + z * 24 : b * 192 + z * 24 + 24],
                    folded,
                    mine,
                ],
                axis=1,
            ).astype(BF)


def expert_grads(normed, grad_pre, mixed, grad_own, grad_other):
    return pl.pallas_call(
        expert_grad_kernel,
        out_shape=jax.ShapeDtypeStruct((8, 8, 24, 1920), BF),
        grid=(4,),
        in_specs=[
            pl.BlockSpec((1024, 384), lambda j: (0, j)),
            pl.BlockSpec((1024, 1280), lambda j: (0, 0)),
            pl.BlockSpec((1024, 128), lambda j: (0, j)),
            pl.BlockSpec((1024, 128), lambda j: (0, 4)),
            pl.BlockSpec((512, D), lambda j: (0, 0)),
            pl.BlockSpec((512, D), lambda j: (0, 0)),
            pl.BlockSpec((512, 384), lambda j: (0, j)),
            pl.BlockSpec((512, 384), lambda j: (0, j)),
        ],
        out_specs=pl.BlockSpec((8, 2, 24, 1920), lambda j: (0, j, 0, 0)),
        compiler_params=pltpu.CompilerParams(vmem_limit_bytes=56 << 20),
        cost_estimate=pl.CostEstimate(
            flops=2 * 1024 * D * 1920, bytes_accessed=22 << 20, transcendentals=0
        ),
    )(normed, grad_pre, mixed, mixed, grad_own, grad_other, grad_own, grad_other)


def full(a):
    return pl.BlockSpec(a.shape, lambda *_, n=len(a.shape): (0,) * n)


def on_chip(kernel, scalars, args, outs, scratch=(), flops=0, exps=0):
    size = sum(math.prod(a.shape) * a.dtype.itemsize for a in (*args, *outs))
    return pl.pallas_call(
        kernel,
        out_shape=tuple(outs),
        grid_spec=pltpu.PrefetchScalarGridSpec(
            num_scalar_prefetch=1,
            grid=(1,),
            in_specs=[full(a) for a in args],
            out_specs=tuple(full(a) for a in outs),
            scratch_shapes=list(scratch),
        ),
        compiler_params=pltpu.CompilerParams(vmem_limit_bytes=56 << 20),
        cost_estimate=pl.CostEstimate(flops=flops, bytes_accessed=size, transcendentals=exps),
    )(scalars, *args)


def out(*shape, dtype=BF):
    return jax.ShapeDtypeStruct(shape, dtype)


PIECES = ((0, 128), (128, 128), (256, 128), (384, 64), (448, 64))


def pack_kernel(core, query, key, value, small, slots):
    rows = pl.ds(pl.multiple_of(core[0] * 96, 32), 96)
    for k, head in enumerate(KEY_HEAD):
        for slot in (k, k + 4):
            slots[slot, :96, :384] = query[rows, head * 384 : (head + 1) * 384]
            slots[slot, :96, 384:512] = key[rows, head * 128 : (head + 1) * 128]
            slots[slot, :96, 512:] = value[rows, head * 128 : (head + 1) * 128]
            slots[slot, 96:] = small[...]


def keys_kernel(core, own, below, above, far_up, far_down, gain, got, other, normed, kv, weight):
    for b in range(8):
        first = pl.multiple_of(b * 192 + core[0] * 96, 32)
        second = pl.multiple_of(b * 192 + (1 - core[0]) * 96, 32)
        weight[pl.ds(first, 96)] = got[b, :96]
        weight[pl.ds(second, 96)] = other[b, :96]
    for (at, size), piece in zip(PIECES, (own, below, above, far_up, far_down)):
        unit, _ = normalize(piece[...].astype(F32))
        normed[at : at + size] = (unit * gain[...]).astype(BF)
    kv[...] = dot(normed[...], weight[:, GROUP * HEAD :]).astype(BF)


def query_kernel(core, normed, weight, kv, query):
    query[...] = dot(normed[...], weight[:, : GROUP * HEAD]).astype(BF)


def mask_of(scalars, segments):
    def place_of(i):
        shift = jnp.where(i < 384, scalars[4] - 256, scalars[5] - 384)
        return i + jnp.where(i < 128, scalars[2], jnp.where(i < 256, scalars[3] - 128, shift))

    query_at = place_of(lax.broadcasted_iota(jnp.int32, (512, 1), 0))
    lane = lax.broadcasted_iota(jnp.int32, (1, 512), 1)
    own_at = place_of(lane)
    other_at = jnp.where(scalars[1] == 1, own_at - 512, 1 << 20)
    key_at = jnp.concatenate([own_at, other_at], axis=1)
    key_seg = segments[...]
    query_seg = jnp.broadcast_to(key_seg[:, :512], (8, 512)).T[:, :1]
    return (query_at == key_at) | (
        (key_at < query_at) & (query_seg == key_seg) & (key_seg != 0.0)
    )


def attend_kernel(core, query, kv, kv_other, segments, attended, logs):
    allowed = mask_of(core, segments)
    keys = jnp.concatenate([kv[:, :HEAD], kv_other[:, :HEAD]], axis=0)
    values = jnp.concatenate([kv[:, HEAD:], kv_other[:, HEAD:]], axis=0)
    lane = lax.broadcasted_iota(jnp.int32, (512, 128), 1)
    kept = jnp.zeros((512, 128), F32)
    for g in range(GROUP):
        scores = dot_rows(query[:, g * HEAD : (g + 1) * HEAD], keys) * SCALE
        scores = jnp.where(allowed, scores, -1e30)
        top = jnp.max(scores, axis=1, keepdims=True)
        expo = jnp.exp(scores - top)
        total = jnp.sum(expo, axis=1, keepdims=True)
        kept = jnp.where(lane == g, top + jnp.log(total), kept)
        attended[:, g * HEAD : (g + 1) * HEAD] = dot((expo / total).astype(BF), values).astype(BF)
    logs[...] = kept


def output_kernel(core, attended, mine, other, own, below, above, far_up, far_down, weight):
    for c in range(2):
        @pl.when(core[0] == c)
        def _():
            weight[c * 192 : (c + 1) * 192] = mine[...]
            weight[(1 - c) * 192 : (2 - c) * 192] = other[...]
    whole = dot(attended[...], weight[...]).astype(BF)
    for (at, size), piece in zip(PIECES, (own, below, above, far_up, far_down)):
        piece[...] = whole[at : at + size]


def attend_back_kernel(core, own, below, above, far_up, far_down, query, kv, kv_other, segments,
                       mine, other, logs, grad, grad_query, grad_own, grad_other, weight):
    for c in range(2):
        @pl.when(core[0] == c)
        def _():
            weight[c * 192 : (c + 1) * 192] = mine[...]
            weight[(1 - c) * 192 : (2 - c) * 192] = other[...]
    for (at, size), piece in zip(PIECES, (own, below, above, far_up, far_down)):
        grad[at : at + size] = piece[...]
    grad_att = dot_rows(grad[...], weight[...]).astype(BF)
    allowed = mask_of(core, segments)
    keys = jnp.concatenate([kv[:, :HEAD], kv_other[:, :HEAD]], axis=0)
    values = jnp.concatenate([kv[:, HEAD:], kv_other[:, HEAD:]], axis=0)
    grad_keys = jnp.zeros((1024, HEAD), F32)
    grad_values = jnp.zeros((1024, HEAD), F32)
    for g in range(GROUP):
        queries = query[:, g * HEAD : (g + 1) * HEAD]
        heads = grad_att[:, g * HEAD : (g + 1) * HEAD]
        scores = jnp.where(allowed, dot_rows(queries, keys) * SCALE, -1e30)
        probs = jnp.exp(scores - logs[:, g : g + 1])
        grad_probs = dot_rows(heads, values)
        inner = jnp.sum(probs * grad_probs, axis=1, keepdims=True)
        grad_scores = (probs * (grad_probs - inner)).astype(BF)
        grad_query[:, g * HEAD : (g + 1) * HEAD] = (dot(grad_scores, keys) * SCALE).astype(BF)
        grad_keys += dot_cols(grad_scores, queries)
        grad_values += dot_cols(probs.astype(BF), heads)
    grad_keys = grad_keys * SCALE
    grad_own[:, :HEAD] = grad_keys[:512]
    grad_own[:, HEAD:] = grad_values[:512]
    grad_other[:, :HEAD] = grad_keys[512:].astype(BF)
    grad_other[:, HEAD:] = grad_values[512:].astype(BF)


def early_grads_kernel(core, grad_query, weight, normed, attended, grad, query, outs, column):
    into = dot_cols(normed[...], grad_query[...])
    column[...] = jnp.sum(into * weight[:, : GROUP * HEAD].astype(F32), axis=1, keepdims=True)
    sums = dot_cols(attended[...], grad[...])
    for z in range(8):
        for b in range(8):
            query[z, b] = into[b * 192 + z * 24 : b * 192 + z * 24 + 24].astype(BF)
        for c in range(2):
            for j in range(2):
                for k in range(2):
                    outs[c, z, j * 2 + k] = sums[
                        j * 192 + z * 24 : j * 192 + z * 24 + 24,
                        c * 768 + k * 384 : c * 768 + (k + 1) * 384,
                    ].astype(BF)


def weight_grads_kernel(core, grad_kv, from_other, weight, normed, small, gain, column, query, outs,
                        keep, give, back_kv):
    back_kv[...] = (grad_kv[...] + from_other[...].astype(F32)).astype(BF)
    into = dot_cols(normed[...], back_kv[...])
    late = jnp.sum(into * weight[:, GROUP * HEAD :].astype(F32), axis=1, keepdims=True)
    lane = lax.broadcasted_iota(jnp.int32, (D, 128), 1)
    side = jnp.where(lane == 9, (column[...] + late) / gain[...], small[...])

    def put(first, second):
        first[:, :8] = query[...]
        first[:, 8:] = outs[0]
        second[:, 8:] = outs[1]
        for z in range(8):
            for b in range(8):
                rows = slice(b * 192 + z * 24, b * 192 + z * 24 + 24)
                second[z, b] = jnp.concatenate([into[rows], side[rows]], axis=1).astype(BF)

    @pl.when(core[0] == 0)
    def _():
        put(keep, give)

    @pl.when(core[0] == 1)
    def _():
        put(give, keep)


def input_back_kernel(core, query, kv, weight, own, below, above, far_up, far_down, both):
    both[:, : GROUP * HEAD] = query[...]
    both[:, GROUP * HEAD :] = kv[...]
    back = dot_rows(both[...], weight[...]).astype(BF)
    for (at, size), piece in zip(PIECES, (own, below, above, far_up, far_down)):
        piece[...] = back[at : at + size]


def settle_experts_kernel(half, whole, expert_in, shared_in, expert_out, shared_out):
    low = [whole[0, 0, e // 4, e % 4, :, :896].astype(F32) for e in range(8)]
    high = [whole[0, 1, e // 4, e % 4, :, :896].astype(F32) for e in range(8)]
    expert_in[:, :, :896] = jnp.transpose(jnp.stack(low), (1, 0, 2))
    expert_in[:, :, 896:] = jnp.transpose(jnp.stack([h[:, :128] for h in high]), (1, 0, 2))
    for e in range(8):
        shared_in[:, e * 128 : (e + 1) * 128] = high[e][:, 128:256]
        shared_in[:, FS + e * 128 : FS + (e + 1) * 128] = high[e][:, 256:384]
        for k in range(3):
            expert_out[e, :, k * 512 : (k + 1) * 512] = high[e][k * 8 : (k + 1) * 8, 384:]
    for y in range(2):
        for j in range(4):
            side = whole[0, y, half[0], j, :, 896:].astype(F32)
            for k in range(3):
                lanes = j * 384 + k * 128
                shared_out[y * 8 : (y + 1) * 8, lanes : lanes + 128] = side[k * 8 : (k + 1) * 8]


def settle_experts(half, whole):
    f32 = lambda *s: jax.ShapeDtypeStruct(s, F32)
    return pl.pallas_call(
        settle_experts_kernel,
        out_shape=(f32(192, EXPERTS, 1024), f32(192, 2 * FS), f32(8, 64, D), f32(128, D)),
        grid_spec=pltpu.PrefetchScalarGridSpec(
            num_scalar_prefetch=1,
            grid=(8,),
            in_specs=[pl.BlockSpec((1, 2, 2, 4, 24, 1024), lambda z, *_: (z,) + (0,) * 5)],
            out_specs=(
                pl.BlockSpec((24, EXPERTS, 1024), lambda z, *_: (z, 0, 0)),
                pl.BlockSpec((24, 2 * FS), lambda z, *_: (z, 0)),
                pl.BlockSpec((8, 8, D), lambda z, *_: (0, z, 0)),
                pl.BlockSpec((16, D), lambda z, *_: (z, 0)),
            ),
        ),
        compiler_params=pltpu.CompilerParams(vmem_limit_bytes=56 << 20),
        cost_estimate=pl.CostEstimate(flops=0, bytes_accessed=19 << 20, transcendentals=0),
    )(half, whole)


def piece_kernel(place, same, below, above, across, side, piece):
    for ref, distance in ((same, 0), (below, 3), (above, 1), (across, 2)):
        piece[lax.rem(place[0] + distance, 4), :, :896] = ref[...]
    piece[:, :, 896:] = side[...]


def settle_kernel(core, mine, other, query, key, value, router, ffn, attn, outs, small):
    small[192:] = jnp.zeros((64, 128), F32)

    def put(first, second):
        for z in range(8):
            rows = slice(z * 24, (z + 1) * 24)
            sums = jnp.zeros((24, 128), F32)
            for k, head in enumerate(KEY_HEAD):
                query[rows, head * 384 : (head + 1) * 384] = first[z, k].astype(F32)
                key[rows, head * 128 : (head + 1) * 128] = second[z, k, :, :128].astype(F32)
                value[rows, head * 128 : (head + 1) * 128] = second[z, k, :, 128:256].astype(F32)
                sums += second[z, k, :, 256:].astype(F32)
            small[rows] = sums
            for k in range(2):
                outs[rows, k * 384 : (k + 1) * 384] = first[z, 4 + k].astype(F32)
                outs[rows, (2 + k) * 384 : (3 + k) * 384] = second[z, 4 + k].astype(F32)

    @pl.when(core[0] == 0)
    def _():
        put(mine, other)

    @pl.when(core[0] == 1)
    def _():
        put(other, mine)

    turned = small[...].T
    router[...] = turned[:8, :192]
    ffn[...] = turned[8:9, :192]
    attn[...] = turned[9:10, :192]


def shards(
    tokens,
    segment_ids,
    routes,
    gain_attn,
    w_query,
    w_key,
    w_value,
    w_out,
    gain_ffn,
    w_router,
    w_shared_in,
    w_shared_out,
    w_expert_in,
    w_expert_out,
    cotangent,
):
    level, core, half, place = (
        lax.axis_index(a).astype(jnp.uint32) for a in ("z", "core", "yhi", "x")
    )
    rows = tokens.shape[0]
    zero = jnp.uint32(0)

    member = half * 4 + place
    key_head = jnp.where((place == 1) | (place == 2), 3 - place, place)

    tokens_x = spread_x(tokens)
    at_core = core.reshape(1).astype(jnp.int32)
    small = jnp.concatenate([gain_attn[None], gain_ffn[None], w_router.T], axis=0)
    small = jnp.pad(small, ((0, 6), (0, 448)))
    (slots,) = on_chip(
        pack_kernel, at_core, (w_query, w_key, w_value, small), (out(8, 112, 640),)
    )
    got = exchange(slots, FSDP)
    small = got[:, 96:106, :192].transpose(1, 0, 2).reshape(10, D)
    gain_one = small[:1].astype(F32)
    gain_two = small[1:2].astype(F32)
    router = small[2:]

    w_out_late, *_ = lax.optimization_barrier((w_out, *tokens_x[1:3]))
    out_mine = lax.ppermute(
        w_out_late,
        ("core", "yhi", "x"),
        [(s * 8 + b, (b % 2) * 8 + s * 4 + KEY_HEAD[b // 2]) for s in range(2) for b in range(8)],
    )

    qkv_other = swap_core(after(got, *tokens_x[3:]))
    turn, flip = level & 3, level >> 2
    first, second = core * 4 + ((place - turn) & 3), core * 4 + ((place - turn - 2) & 3)
    halves = (
        lax.dynamic_slice(w_expert_in, (zero, first, zero), (192, 1, 896)).reshape(192, 896),
        jnp.concatenate(
            [
                lax.dynamic_slice(w_expert_in, (zero, second, zero + 896), (192, 1, 128)).reshape(
                    192, 128
                ),
                lax.dynamic_slice(w_shared_in, (zero, second * 128), (192, 128)),
                lax.dynamic_slice(w_shared_in, (zero, second * 128 + FS), (192, 128)),
                lax.dynamic_slice(w_expert_out, (second, zero, zero), (1, 64, D))
                .reshape(64, 3, 512)
                .transpose(1, 0, 2)
                .reshape(192, 512),
            ],
            axis=1,
        ),
    )
    halves = after_all(halves, slots)
    halves = [
        lax.ppermute(
            part,
            ("z", *FSDP),
            [
                (z * 8 + h * 4 + x, z * 8 + (h ^ (z >> 2) ^ k) * 4 + ((x - z - 2 * k) & 3))
                for z in range(8)
                for h in range(2)
                for x in range(4)
            ],
        )
        for k, part in enumerate(halves)
    ]
    block = after(jnp.concatenate(halves, axis=1), got, *tokens_x[3:])
    blocks = lax.all_gather(block, "z")
    inputs = tokens.astype(F32)
    normed_one, kv, w_qkv = on_chip(
        keys_kernel,
        at_core,
        (*tokens_x, gain_one, got, qkv_other),
        (out(512, D), out(512, 256), out(D, 640)),
        flops=2 * 512 * D * 256,
    )
    kv_other = lax.ppermute(kv, "yhi", [(0, 1)])
    (query,) = on_chip(
        query_kernel, at_core, (normed_one, w_qkv, kv), (out(512, 384),), flops=2 * 512 * D * 384
    )
    grad_late = after(cotangent, kv)
    grad_below, grad_above = up_x(grad_late), down_x(grad_late)
    out_other = swap_core(after(out_mine, kv_other, query))
    starts = [((place + k) & 3) * 128 for k in (0, 3, 1, 2)]
    segments = [lax.dynamic_slice_in_dim(segment_ids, half * 512 + s, 128) for s in starts]
    segments += [lax.dynamic_slice_in_dim(segment_ids, s, 128) for s in starts]
    segments = jnp.concatenate(segments)[None].astype(F32)
    at_block = jnp.stack([core, half, *starts]).astype(jnp.int32)
    part = [out(size, D) for _, size in PIECES]
    attended, logs = on_chip(
        attend_kernel,
        at_block,
        (query, kv, kv_other, segments),
        (out(512, 384), out(512, 128, dtype=F32)),
        flops=2 * 512 * 384 * 2048,
        exps=3 * 512 * 1024,
    )
    hidden_part = on_chip(
        output_kernel,
        at_core,
        (attended, out_mine, out_other),
        part,
        scratch=[pltpu.VMEM((384, D), BF)],
        flops=2 * 512 * 384 * D,
    )
    far_up, far_down = after_all((grad_below[:64], grad_above[64:]), hidden_part[0])
    hidden_near = near_pieces(hidden_part, far_pieces(hidden_part))
    grad_x = (cotangent, grad_below, grad_above, up_x(far_up), down_x(far_down))
    shared_other = lax.ppermute(after(w_shared_out, attended), ("core", "yhi"), [(0, 1), (3, 2)])
    grad_own = jnp.concatenate(grad_x, axis=0)
    grad_other = swap_core(grad_own)
    above, below = hidden_near
    hidden = inputs + near_sum(hidden_part[0], up_x(above), down_x(below))

    unit_two, factor_two = normalize(hidden)
    normed_two = (unit_two * gain_two).astype(BF)
    logits = dot_rows(normed_two, router)
    chosen = jnp.sum(
        (routes[:, :, None] == jnp.arange(EXPERTS, dtype=jnp.int32)[None, None, :]).astype(F32),
        axis=1,
    )
    weighted = chosen * jnp.exp(logits)
    gates = weighted / jnp.sum(weighted, axis=-1, keepdims=True)
    packed = jnp.concatenate(
        [normed_two, *pair_of_float(gates), jnp.zeros((rows, 112), BF)], axis=1
    )
    packed = spread_x(after(packed, *grad_x[3:]))
    packed = (*packed, *(swap_core(p) for p in packed))

    scalars = jnp.stack([member, core * 4 + place, (core == half).astype(jnp.uint32)])
    back_own, back_other, mixed, grad_pre, normed_all, w_down = expert_pass(
        scalars.astype(jnp.int32), packed, grad_own, grad_other, blocks, w_shared_out, shared_other
    )
    back_other = swap_core(back_other)
    back_part = [plus(o, s) for o, s in zip(pieces_of(back_own), pieces_of(back_other))]
    normed_all, _, _ = lax.optimization_barrier((normed_all, back_part[3], back_part[4]))
    flat = expert_grads(normed_all, grad_pre, mixed, grad_own, grad_other)
    back_sum, flat_ffn = collect_x(back_part, flat)

    grad_gates = back_sum[:, D : D + 8] + back_sum[:, D + 8 : D + 16]
    grad_logits = (
        gates * (grad_gates - jnp.sum(gates * grad_gates, axis=-1, keepdims=True))
    ).astype(BF)
    grad_normed_two = back_sum[:, :D] + dot(grad_logits, router)
    grad_router = dot_cols(normed_two, jnp.pad(grad_logits, ((0, 0), (0, 120))))
    grad_gain_ffn = jnp.sum(grad_normed_two * unit_two, axis=0, keepdims=True)
    grad_hidden = cotangent.astype(F32) + norm_back(
        grad_normed_two, unit_two, factor_two, gain_two
    )
    grad_hidden_low = grad_hidden.astype(BF)
    hidden_low = spread_x(grad_hidden_low)
    result_part = dot(after(mixed, grad_hidden_low), w_down).astype(BF)
    hidden_low = (after(hidden_low[0], result_part), *hidden_low[1:])

    grad_low, grad_query, grad_kv, to_other = on_chip(
        attend_back_kernel,
        at_block,
        (*hidden_low, query, kv, kv_other, segments, out_mine, out_other, logs),
        (out(512, D), out(512, 384), out(512, 256, dtype=F32), out(512, 256)),
        scratch=[pltpu.VMEM((384, D), BF)],
        flops=2 * 512 * 384 * 6656,
        exps=3 * 512 * 1024,
    )
    from_other = lax.ppermute(to_other, "yhi", [(1, 0)])
    small = grad_router + jnp.pad(grad_gain_ffn.T, ((0, 0), (8, 119)))
    query_sums, outs_sums, column = on_chip(
        early_grads_kernel,
        at_core,
        (grad_query, w_qkv, normed_one, attended, grad_low),
        (out(8, 8, 24, 384), out(2, 8, 4, 24, 384), out(D, 1, dtype=F32)),
        flops=2 * 512 * D * 768,
    )
    keep, give, back_kv = on_chip(
        weight_grads_kernel,
        at_core,
        (
            grad_kv,
            from_other,
            w_qkv,
            normed_one,
            small,
            gain_one.reshape(D, 1),
            column,
            query_sums,
            outs_sums,
        ),
        (out(8, 12, 24, 384), out(8, 12, 24, 384), out(512, 256)),
        flops=2 * 512 * D * 256,
    )

    flat = plus(keep, swap_core(give))
    flat_sent = flat
    result_other = swap_core(after(result_part[512:], flat_sent))
    flat = exchange(flat, "z")
    ffn = lax.psum_scatter(flat_ffn, "z", scatter_dimension=0, tiled=True)[0]
    ffn = after(ffn, flat_sent)
    side = ffn[..., 1792:].reshape(4, 2, 24, 128)
    main = ffn[..., :1792].reshape(2, 4, 24, 1792)
    both = [
        jnp.concatenate([m[..., :896], side[:, 0], m[..., 896:], side[:, 1]], axis=-1)
        for m in (main[0], main[1])
    ]
    keep = jnp.where(half == 0, both[0], both[1])
    away = jnp.where(half == 0, both[1], both[0])
    ffn = plus(keep, lax.ppermute(away, "yhi", [(0, 1), (1, 0)]))
    here = lax.axis_index("ylo")
    keep = jnp.where(here == 0, ffn[..., :1024], ffn[..., 1024:])
    away = jnp.where(here == 0, ffn[..., 1024:], ffn[..., :1024])
    ffn = plus(keep, lax.ppermute(away, "ylo", [(0, 1), (1, 0)]))
    to = [
        lax.dynamic_index_in_dim(ffn[..., :896], (place + k) & 3, 0, False) for k in (0, 1, 3, 2)
    ]
    across = lax.ppermute(to[3], "x", [(i, (i + 2) % 4) for i in range(4)])
    (piece,) = on_chip(
        piece_kernel,
        place.reshape(1).astype(jnp.int32),
        (to[0], up_x(to[1]), down_x(to[2]), across, ffn[..., 896:]),
        (out(4, 24, 1024),),
    )
    whole = lax.all_gather(after(piece, flat, result_other), REP).reshape(8, 2, 2, 4, 24, 1024)
    flat = jnp.sum(flat.astype(F32), axis=0).astype(BF)
    outs = lax.dynamic_update_slice(
        jnp.zeros((8, 2, 24, 384), BF), flat[8:].reshape(2, 2, 24, 384), (2 * key_head, *(jnp.uint32(0),) * 3)
    )
    flat = jnp.concatenate([flat[:8, None], outs], axis=1)
    flat = jnp.concatenate([flat, flat], axis=0)
    result_part = [
        plus(o, s)
        for o, s in zip(pieces_of(result_part[:512]), pieces_of(after(result_other, flat)))
    ]
    back_one = on_chip(
        input_back_kernel,
        at_core,
        (after(grad_query, flat), back_kv, w_qkv),
        part,
        scratch=[pltpu.VMEM((512, 640), BF)],
        flops=2 * 512 * D * 640,
    )
    got = exchange(flat, PLANE).reshape(4, 4, 3, 24, 384)
    got = jnp.sum(got.astype(F32), axis=0)
    mine = jnp.concatenate([got[:, 0], jnp.sum(got[:, 1:], axis=0)], axis=0).astype(BF)
    result = (hidden + collect_x(result_part, gate=got)).astype(BF)
    mine = spread_z(mine, level)
    above, below = after_all(near_pieces(back_one, far_pieces(back_one)), mine)
    back_near = up_x(above), down_x(below)
    sum_query, sum_key, sum_value, sum_router, sum_ffn, sum_attn, sum_out = on_chip(
        settle_kernel,
        at_core,
        (mine, swap_core(mine)),
        (
            out(192, D, dtype=F32),
            out(192, 512, dtype=F32),
            out(192, 512, dtype=F32),
            out(EXPERTS, 192, dtype=F32),
            out(1, 192, dtype=F32),
            out(1, 192, dtype=F32),
            out(192, D, dtype=F32),
        ),
        scratch=[pltpu.VMEM((256, 128), F32)],
    )

    at_half = half.reshape(1).astype(jnp.int32)
    sum_expert_in, sum_shared_in, sum_expert_out, sum_shared_out = settle_experts(
        at_half, after(whole, sum_query, result)
    )

    back_one = near_sum(back_one[0], *after_all(back_near, sum_expert_in))
    unit_own, factor_own = normalize(inputs)
    grad_input = (grad_hidden + norm_back(back_one, unit_own, factor_own, gain_one)).astype(BF)

    return (
        result,
        grad_input,
        sum_attn.reshape(192),
        sum_query,
        sum_key,
        sum_value,
        sum_out,
        sum_ffn.reshape(192),
        sum_router.T,
        sum_shared_in,
        sum_shared_out,
        sum_expert_in,
        sum_expert_out,
    )


def solution(mesh):
    fine = Mesh(mesh.devices.reshape(SIZES), AXES)
    tokens = P((*REP, *FSDP), None)
    first = P(FSDP, None)
    return jax.shard_map(
        shards,
        mesh=fine,
        in_specs=(
            tokens,
            P(REP),
            tokens,
            P(FSDP),
            first,
            first,
            first,
            first,
            P(FSDP),
            first,
            first,
            first,
            P(FSDP, None, None),
            P(None, FSDP, None),
            tokens,
        ),
        out_specs=(
            tokens,
            tokens,
            P(FSDP),
            first,
            first,
            first,
            first,
            P(FSDP),
            first,
            first,
            first,
            P(FSDP, None, None),
            P(None, FSDP, None),
        ),
        check_vma=False,
    )
```

```python
import math

import jax
import jax.numpy as jnp
from jax import lax
from jax.experimental import pallas as pl
from jax.experimental.pallas import tpu as pltpu
from jax.sharding import Mesh, PartitionSpec as P

HEADS = 12
KV_HEADS = 4
HEAD = 128
GROUP = HEADS // KV_HEADS
D = 1536
FE = 512
FS = 1024
EXPERTS = 8
EPS = 1e-05
SCALE = 1.0 / math.sqrt(HEAD)

AXES = ("z", "ylo", "core", "yhi", "x")
SIZES = (8, 2, 2, 2, 4)
REP = ("z", "ylo", "core")
FSDP = ("yhi", "x")
PLANE = ("ylo", "yhi", "x")
KEY_HEAD = (0, 2, 1, 3)
BF = jnp.bfloat16
F32 = jnp.float32


def dot(left, right):
    return jnp.dot(left, right, preferred_element_type=F32)


def dot_rows(left, right):
    return lax.dot_general(left, right, (((1,), (1,)), ((), ())), preferred_element_type=F32)


def dot_cols(left, right):
    return lax.dot_general(left, right, (((0,), (0,)), ((), ())), preferred_element_type=F32)


def exchange(blocks, axes):
    return lax.all_to_all(blocks, axes, 0, 0, tiled=True)


def up_x(rows):
    return lax.ppermute(rows, "x", [(i, (i + 1) % 4) for i in range(4)])


def down_x(rows):
    return lax.ppermute(rows, "x", [(i, (i + 3) % 4) for i in range(4)])


def spread_x(rows):
    cut = rows.shape[0] // 2
    below, above = up_x(rows), down_x(rows)
    return rows, below, above, up_x(below[:cut]), down_x(above[cut:])


def pieces_of(rows):
    return tuple(rows[at : at + size] for at, size in PIECES)


def collect_x(pieces, beside=None, gate=None):
    above, below = near_pieces(pieces, far_pieces(pieces))
    if gate is not None:
        above, below = after_all((above, below), gate)
    if beside is not None:
        above, below, beside = lax.optimization_barrier((above, below, beside))
    total = near_sum(pieces[0], up_x(above), down_x(below))
    return total if beside is None else (total, beside)


def far_pieces(pieces):
    return up_x(pieces[3]), down_x(pieces[4])


def near_pieces(pieces, far):
    _, below, above, *_ = pieces
    cut = far[0].shape[0]
    above = jnp.concatenate([plus(above[:cut], far[0]), above[cut:]], axis=0)
    below = jnp.concatenate([below[:cut], plus(below[cut:], far[1])], axis=0)
    return above, below


def near_sum(own, below, above):
    return own.astype(F32) + below.astype(F32) + above.astype(F32)


def plus(left, right):
    return (left.astype(F32) + right.astype(F32)).astype(BF)


def spread_z(rows, level):
    up = [(i, (i + 1) % 8) for i in range(8)]
    down = [(i, (i + 7) % 8) for i in range(8)]
    cut = rows.shape[0] // 2
    whole = jnp.zeros((8, *rows.shape), rows.dtype)
    rest = (jnp.uint32(0),) * (rows.ndim - 1)

    level = level.astype(jnp.int32)

    def put(whole, block, distance, start=0):
        return lax.dynamic_update_slice(
            whole,
            block[None],
            ((level + distance + 8 & 7).astype(jnp.uint32), jnp.uint32(start), *rest)
        )

    whole = put(whole, rows, 0)
    below = above = rows
    for k in (1, 2, 3):
        below, above = lax.ppermute(below, "z", up), lax.ppermute(above, "z", down)
        below, above = lax.optimization_barrier((below, above))
        whole = put(put(whole, below, -k), above, k)
    whole = put(whole, lax.ppermute(below[:cut], "z", up), 4)
    return put(whole, lax.ppermute(above[cut:], "z", down), 4, cut)


def after(value, *others):
    return lax.optimization_barrier((value, *others))[0]


def after_all(values, *others):
    return lax.optimization_barrier((*values, *others))[: len(values)]


def swap_core(rows):
    return lax.ppermute(rows, "core", [(0, 1), (1, 0)])


def pair_of_float(values):
    high = values.astype(BF)
    return high, (values - high.astype(F32)).astype(BF)


def normalize(values):
    factor = lax.rsqrt(jnp.mean(values * values, axis=-1, keepdims=True) + EPS)
    return values * factor, factor


def norm_back(grad_normed, unit, factor, gain):
    scaled = grad_normed * gain
    inner = jnp.mean(scaled * unit, axis=-1, keepdims=True)
    return factor * (scaled - unit * inner)


def silu_slope(values, sig):
    return sig * (1.0 + values * (1.0 - sig))


def expert_kernel(member, own, below, above, far_up, far_down, own_o, below_o, above_o, far_up_o,
                  far_down_o, grad_own, grad_other, w_in, w_expert, shared_mine, shared_other, back_own,
                  back_other, mixed, grad_pre, normed, w_down, rows):
    step = pl.program_id(0)

    @pl.when(step == 0)
    def _():
        w_down[:FE] = w_expert[...]

        @pl.when(member[2] == 0)
        def _():
            w_down[FE:] = shared_other[...]

        @pl.when(member[2] != 0)
        def _():
            w_down[FE:] = shared_mine[...]

        at = 0
        for piece in (own, below, above, far_up, far_down, own_o, below_o, above_o, far_up_o,
                      far_down_o):
            rows[at : at + piece.shape[0]] = piece[...]
            at += piece.shape[0]

    part = pl.ds(pl.multiple_of(step * 256, 256), 256)
    x = rows[part, :D]
    lane = lax.broadcasted_iota(jnp.int32, (256, 128), 1)
    expert = member[1]
    high, low = lane == expert, lane == expert + 8
    gate = jnp.sum(
        jnp.where(high | low, rows[part, D:].astype(F32), 0.0), axis=1, keepdims=True
    )
    back_down = dot_rows(jnp.where(step < 2, grad_own[...], grad_other[...]), w_down[...])
    pre = dot(x, w_in[...])
    gate_part, up_part = pre[:, :FE], pre[:, FE : 2 * FE]
    shared_gate, shared_up = pre[:, 2 * FE : 2 * FE + 128], pre[:, 2 * FE + 128 :]
    gate_sig = jax.nn.sigmoid(gate_part)
    gate_act = gate_part * gate_sig
    activ = gate_act * up_part
    shared_sig = jax.nn.sigmoid(shared_gate)
    shared_silu = shared_gate * shared_sig
    grad_mixed, grad_shared = back_down[:, :FE], back_down[:, FE:]
    grad_gate = jnp.sum(grad_mixed * activ, axis=1, keepdims=True)
    grad_activ = grad_mixed * gate
    mixed[:, :FE] = (gate * activ).astype(BF)
    mixed[:, FE:] = (shared_silu * shared_up).astype(BF)
    grad_pre[:, :FE] = (grad_activ * up_part * silu_slope(gate_part, gate_sig)).astype(BF)
    grad_pre[:, FE : 2 * FE] = (grad_activ * gate_act).astype(BF)
    grad_pre[:, 2 * FE : 2 * FE + 128] = (
        grad_shared * shared_up * silu_slope(shared_gate, shared_sig)
    ).astype(BF)
    grad_pre[:, 2 * FE + 128 :] = (grad_shared * shared_silu).astype(BF)
    normed[...] = x
    back = dot_rows(grad_pre[...], w_in[...]).astype(BF)
    top = grad_gate.astype(BF).astype(F32)
    tail = jnp.where(high, top, jnp.where(low, grad_gate - top, 0.0)).astype(BF)

    @pl.when(step < 2)
    def _():
        back_own[:, :D], back_own[:, D:] = back, tail

    @pl.when(step >= 2)
    def _():
        back_other[:, :D], back_other[:, D:] = back, tail


def lower_chunk(n):
    return pl.BlockSpec((256, n), lambda i, *_: (jnp.minimum(i, 1), 0))


def upper_chunk(n):
    return pl.BlockSpec((256, n), lambda i, *_: (jnp.maximum(i - 2, 0), 0))


def expert_pass(scalars, pieces, grad_own, grad_other, *weights):
    whole = lambda a: pl.BlockSpec(a.shape, lambda i, *_, n=a.ndim: (0,) * n)
    chunk = lambda n: pl.BlockSpec((256, n), lambda i, *_: (i, 0))
    shape = lambda n, rows=1024: jax.ShapeDtypeStruct((rows, n), BF)
    return pl.pallas_call(
        expert_kernel,
        out_shape=(shape(1664, 512), shape(1664, 512), shape(640), shape(1280), shape(D), shape(D, 640)),
        grid_spec=pltpu.PrefetchScalarGridSpec(
            num_scalar_prefetch=1,
            grid=(4,),
            in_specs=[
                *(whole(p) for p in pieces),
                lower_chunk(D),
                upper_chunk(D),
                *(whole(w) for w in weights),
            ],
            out_specs=(
                lower_chunk(1664),
                upper_chunk(1664),
                chunk(640),
                chunk(1280),
                chunk(D),
                pl.BlockSpec((640, D), lambda i, *_: (0, 0)),
            ),
            scratch_shapes=[
                pltpu.VMEM((1024, 1664), BF),
            ],
        ),
        compiler_params=pltpu.CompilerParams(vmem_limit_bytes=56 << 20),
        cost_estimate=pl.CostEstimate(
            flops=2 * 1024 * D * 3200, bytes_accessed=30 << 20, transcendentals=1024 * 640
        ),
    )(scalars, *pieces, grad_own, grad_other, *weights)


def expert_grad_kernel(normed, grad_pre, mixed, shared, own, other, own_cols, other_cols, out):
    into = dot_cols(normed[...], grad_pre[...])
    down = dot_cols(mixed[:512], own[...]) + dot_cols(mixed[512:], other[...])
    side = dot_cols(shared[:512], own_cols[...]) + dot_cols(shared[512:], other_cols[...])
    for b in range(2):
        for z in range(8):
            at = b * 64 + z * 8
            folded = jnp.concatenate(
                [down[at : at + 8, k * 512 : (k + 1) * 512] for k in range(3)], axis=0
            )
            mine = jnp.concatenate(
                [side[z * 16 + b * 8 : z * 16 + b * 8 + 8, k * 128 : (k + 1) * 128] for k in range(3)],
                axis=0,
            )
            out[z, b] = jnp.concatenate(
                [
                    into[b * 192 + z * 24 : b * 192 + z * 24 + 24],
                    folded,
                    mine,
                ],
                axis=1,
            ).astype(BF)


def expert_grads(normed, grad_pre, mixed, grad_own, grad_other):
    return pl.pallas_call(
        expert_grad_kernel,
        out_shape=jax.ShapeDtypeStruct((8, 8, 24, 1920), BF),
        grid=(4,),
        in_specs=[
            pl.BlockSpec((1024, 384), lambda j: (0, j)),
            pl.BlockSpec((1024, 1280), lambda j: (0, 0)),
            pl.BlockSpec((1024, 128), lambda j: (0, j)),
            pl.BlockSpec((1024, 128), lambda j: (0, 4)),
            pl.BlockSpec((512, D), lambda j: (0, 0)),
            pl.BlockSpec((512, D), lambda j: (0, 0)),
            pl.BlockSpec((512, 384), lambda j: (0, j)),
            pl.BlockSpec((512, 384), lambda j: (0, j)),
        ],
        out_specs=pl.BlockSpec((8, 2, 24, 1920), lambda j: (0, j, 0, 0)),
        compiler_params=pltpu.CompilerParams(vmem_limit_bytes=56 << 20),
        cost_estimate=pl.CostEstimate(
            flops=2 * 1024 * D * 1920, bytes_accessed=22 << 20, transcendentals=0
        ),
    )(normed, grad_pre, mixed, mixed, grad_own, grad_other, grad_own, grad_other)


def full(a):
    return pl.BlockSpec(a.shape, lambda *_, n=len(a.shape): (0,) * n)


def on_chip(kernel, scalars, args, outs, scratch=(), flops=0, exps=0):
    size = sum(math.prod(a.shape) * a.dtype.itemsize for a in (*args, *outs))
    return pl.pallas_call(
        kernel,
        out_shape=tuple(outs),
        grid_spec=pltpu.PrefetchScalarGridSpec(
            num_scalar_prefetch=1,
            grid=(1,),
            in_specs=[full(a) for a in args],
            out_specs=tuple(full(a) for a in outs),
            scratch_shapes=list(scratch),
        ),
        compiler_params=pltpu.CompilerParams(vmem_limit_bytes=56 << 20),
        cost_estimate=pl.CostEstimate(flops=flops, bytes_accessed=size, transcendentals=exps),
    )(scalars, *args)


def out(*shape, dtype=BF):
    return jax.ShapeDtypeStruct(shape, dtype)


PIECES = ((0, 128), (128, 128), (256, 128), (384, 64), (448, 64))


def turn_kernel(member, blocks, w_in, w_down):
    for b in range(8):
        flip = (b >> 2) ^ (member[0] >> 2)
        first = flip * 4 + ((b - member[0]) & 3)
        second = (1 - flip) * 4 + ((b - member[0] - 2) & 3)
        w_in[b * 192 : (b + 1) * 192, :896] = blocks[first, :, :896]
        w_in[b * 192 : (b + 1) * 192, 896:] = blocks[second, :, 896:1280]
        for k in range(3):
            w_down[b * 64 : (b + 1) * 64, k * 512 : (k + 1) * 512] = blocks[
                second, k * 64 : (k + 1) * 64, 1280:
            ]


def plus_kernel(core, left, right, total):
    total[...] = plus(left[...], right[...])


def pack_kernel(core, query, key, value, small, slots):
    rows = pl.ds(pl.multiple_of(core[0] * 96, 32), 96)
    for k, head in enumerate(KEY_HEAD):
        for slot in (k, k + 4):
            slots[slot, :96, :384] = query[rows, head * 384 : (head + 1) * 384]
            slots[slot, :96, 384:512] = key[rows, head * 128 : (head + 1) * 128]
            slots[slot, :96, 512:] = value[rows, head * 128 : (head + 1) * 128]
            slots[slot, 96:] = small[...]


def keys_kernel(core, own, below, above, far_up, far_down, gain, got, other, normed, kv, weight):
    for b in range(8):
        first = pl.multiple_of(b * 192 + core[0] * 96, 32)
        second = pl.multiple_of(b * 192 + (1 - core[0]) * 96, 32)
        weight[pl.ds(first, 96)] = got[b, :96]
        weight[pl.ds(second, 96)] = other[b, :96]
    for (at, size), piece in zip(PIECES, (own, below, above, far_up, far_down)):
        unit, _ = normalize(piece[...].astype(F32))
        normed[at : at + size] = (unit * gain[...]).astype(BF)
    kv[...] = dot(normed[...], weight[:, GROUP * HEAD :]).astype(BF)


def query_kernel(core, normed, weight, kv, query):
    query[...] = dot(normed[...], weight[:, : GROUP * HEAD]).astype(BF)


def mask_of(scalars, segments):
    def place_of(i):
        shift = jnp.where(i < 384, scalars[4] - 256, scalars[5] - 384)
        return i + jnp.where(i < 128, scalars[2], jnp.where(i < 256, scalars[3] - 128, shift))

    query_at = place_of(lax.broadcasted_iota(jnp.int32, (512, 1), 0))
    lane = lax.broadcasted_iota(jnp.int32, (1, 512), 1)
    own_at = place_of(lane)
    other_at = jnp.where(scalars[1] == 1, own_at - 512, 1 << 20)
    key_at = jnp.concatenate([own_at, other_at], axis=1)
    key_seg = segments[...]
    query_seg = jnp.broadcast_to(key_seg[:, :512], (8, 512)).T[:, :1]
    return (query_at == key_at) | (
        (key_at < query_at) & (query_seg == key_seg) & (key_seg != 0.0)
    )


def attend_kernel(core, query, kv, kv_other, segments, attended, logs):
    allowed = mask_of(core, segments)
    keys = jnp.concatenate([kv[:, :HEAD], kv_other[:, :HEAD]], axis=0)
    values = jnp.concatenate([kv[:, HEAD:], kv_other[:, HEAD:]], axis=0)
    lane = lax.broadcasted_iota(jnp.int32, (512, 128), 1)
    kept = jnp.zeros((512, 128), F32)
    for g in range(GROUP):
        scores = dot_rows(query[:, g * HEAD : (g + 1) * HEAD], keys) * SCALE
        scores = jnp.where(allowed, scores, -1e30)
        top = jnp.max(scores, axis=1, keepdims=True)
        expo = jnp.exp(scores - top)
        total = jnp.sum(expo, axis=1, keepdims=True)
        kept = jnp.where(lane == g, top + jnp.log(total), kept)
        attended[:, g * HEAD : (g + 1) * HEAD] = dot((expo / total).astype(BF), values).astype(BF)
    logs[...] = kept


def output_kernel(core, attended, mine, other, own, below, above, far_up, far_down, weight):
    for c in range(2):
        @pl.when(core[0] == c)
        def _():
            weight[c * 192 : (c + 1) * 192] = mine[...]
            weight[(1 - c) * 192 : (2 - c) * 192] = other[...]
    whole = dot(attended[...], weight[...]).astype(BF)
    for (at, size), piece in zip(PIECES, (own, below, above, far_up, far_down)):
        piece[...] = whole[at : at + size]


def attend_back_kernel(core, own, below, above, far_up, far_down, query, kv, kv_other, segments,
                       mine, other, logs, grad, grad_query, grad_own, grad_other, weight):
    for c in range(2):
        @pl.when(core[0] == c)
        def _():
            weight[c * 192 : (c + 1) * 192] = mine[...]
            weight[(1 - c) * 192 : (2 - c) * 192] = other[...]
    for (at, size), piece in zip(PIECES, (own, below, above, far_up, far_down)):
        grad[at : at + size] = piece[...]
    grad_att = dot_rows(grad[...], weight[...]).astype(BF)
    allowed = mask_of(core, segments)
    keys = jnp.concatenate([kv[:, :HEAD], kv_other[:, :HEAD]], axis=0)
    values = jnp.concatenate([kv[:, HEAD:], kv_other[:, HEAD:]], axis=0)
    grad_keys = jnp.zeros((1024, HEAD), F32)
    grad_values = jnp.zeros((1024, HEAD), F32)
    for g in range(GROUP):
        queries = query[:, g * HEAD : (g + 1) * HEAD]
        heads = grad_att[:, g * HEAD : (g + 1) * HEAD]
        scores = jnp.where(allowed, dot_rows(queries, keys) * SCALE, -1e30)
        probs = jnp.exp(scores - logs[:, g : g + 1])
        grad_probs = dot_rows(heads, values)
        inner = jnp.sum(probs * grad_probs, axis=1, keepdims=True)
        grad_scores = (probs * (grad_probs - inner)).astype(BF)
        grad_query[:, g * HEAD : (g + 1) * HEAD] = (dot(grad_scores, keys) * SCALE).astype(BF)
        grad_keys += dot_cols(grad_scores, queries)
        grad_values += dot_cols(probs.astype(BF), heads)
    grad_keys = grad_keys * SCALE
    grad_own[:, :HEAD] = grad_keys[:512]
    grad_own[:, HEAD:] = grad_values[:512]
    grad_other[:, :HEAD] = grad_keys[512:].astype(BF)
    grad_other[:, HEAD:] = grad_values[512:].astype(BF)


def early_grads_kernel(core, grad_query, weight, normed, attended, grad, small, gain, query, outs, side):
    into = dot_cols(normed[...], grad_query[...])
    column = jnp.sum(into * weight[:, : GROUP * HEAD].astype(F32), axis=1, keepdims=True)
    lane = lax.broadcasted_iota(jnp.int32, (D, 128), 1)
    turned = 1.0 / gain[...]
    side[...] = jnp.where(lane == 9, column * turned, jnp.where(lane == 10, turned, small[...]))
    sums = dot_cols(attended[...], grad[...])
    for z in range(8):
        for b in range(8):
            query[z, b] = into[b * 192 + z * 24 : b * 192 + z * 24 + 24].astype(BF)
        for c in range(2):
            for j in range(2):
                for k in range(2):
                    outs[c, z, j * 2 + k] = sums[
                        j * 192 + z * 24 : j * 192 + z * 24 + 24,
                        c * 768 + k * 384 : c * 768 + (k + 1) * 384,
                    ].astype(BF)


def weight_grads_kernel(core, grad_kv, from_other, weight, normed, sides, query, outs, keep, give,
                        back_kv):
    back_kv[...] = (grad_kv[...] + from_other[...].astype(F32)).astype(BF)
    into = dot_cols(normed[...], back_kv[...])
    late = jnp.sum(into * weight[:, GROUP * HEAD :].astype(F32), axis=1, keepdims=True)
    lane = lax.broadcasted_iota(jnp.int32, (D, 128), 1)
    side = sides[...]
    side = jnp.where(lane == 9, side + late * side[:, 10:11], jnp.where(lane == 10, 0.0, side))

    def put(first, second):
        first[:, :8] = query[...]
        first[:, 8:] = outs[0]
        second[:, 8:] = outs[1]
        for z in range(8):
            for b in range(8):
                rows = slice(b * 192 + z * 24, b * 192 + z * 24 + 24)
                second[z, b] = jnp.concatenate([into[rows], side[rows]], axis=1).astype(BF)

    @pl.when(core[0] == 0)
    def _():
        put(keep, give)

    @pl.when(core[0] == 1)
    def _():
        put(give, keep)


def input_back_kernel(core, query, kv, weight, own, below, above, far_up, far_down, both):
    both[:, : GROUP * HEAD] = query[...]
    both[:, GROUP * HEAD :] = kv[...]
    back = dot_rows(both[...], weight[...]).astype(BF)
    for (at, size), piece in zip(PIECES, (own, below, above, far_up, far_down)):
        piece[...] = back[at : at + size]


def settle_experts_kernel(half, whole, expert_in, shared_in, expert_out, shared_out):
    low = [whole[0, 0, e // 4, e % 4, :, :896].astype(F32) for e in range(8)]
    high = [whole[0, 1, e // 4, e % 4, :, :896].astype(F32) for e in range(8)]
    expert_in[:, :, :896] = jnp.transpose(jnp.stack(low), (1, 0, 2))
    expert_in[:, :, 896:] = jnp.transpose(jnp.stack([h[:, :128] for h in high]), (1, 0, 2))
    for e in range(8):
        shared_in[:, e * 128 : (e + 1) * 128] = high[e][:, 128:256]
        shared_in[:, FS + e * 128 : FS + (e + 1) * 128] = high[e][:, 256:384]
        for k in range(3):
            expert_out[e, :, k * 512 : (k + 1) * 512] = high[e][k * 8 : (k + 1) * 8, 384:]
    for y in range(2):
        for j in range(4):
            side = whole[0, y, half[0], j, :, 896:].astype(F32)
            for k in range(3):
                lanes = j * 384 + k * 128
                shared_out[y * 8 : (y + 1) * 8, lanes : lanes + 128] = side[k * 8 : (k + 1) * 8]


def settle_experts(half, whole):
    f32 = lambda *s: jax.ShapeDtypeStruct(s, F32)
    return pl.pallas_call(
        settle_experts_kernel,
        out_shape=(f32(192, EXPERTS, 1024), f32(192, 2 * FS), f32(8, 64, D), f32(128, D)),
        grid_spec=pltpu.PrefetchScalarGridSpec(
            num_scalar_prefetch=1,
            grid=(8,),
            in_specs=[pl.BlockSpec((1, 2, 2, 4, 24, 1024), lambda z, *_: (z,) + (0,) * 5)],
            out_specs=(
                pl.BlockSpec((24, EXPERTS, 1024), lambda z, *_: (z, 0, 0)),
                pl.BlockSpec((24, 2 * FS), lambda z, *_: (z, 0)),
                pl.BlockSpec((8, 8, D), lambda z, *_: (0, z, 0)),
                pl.BlockSpec((16, D), lambda z, *_: (z, 0)),
            ),
        ),
        compiler_params=pltpu.CompilerParams(vmem_limit_bytes=56 << 20),
        cost_estimate=pl.CostEstimate(flops=0, bytes_accessed=19 << 20, transcendentals=0),
    )(half, whole)


def piece_kernel(place, same, below, above, across, side, piece):
    for ref, distance in ((same, 0), (below, 3), (above, 1), (across, 2)):
        piece[lax.rem(place[0] + distance, 4), :, :896] = ref[...]
    piece[:, :, 896:] = side[...]


def settle_kernel(core, mine, other, query, key, value, router, ffn, attn, outs, small):
    small[192:] = jnp.zeros((64, 128), F32)

    def put(first, second):
        for z in range(8):
            rows = slice(z * 24, (z + 1) * 24)
            sums = jnp.zeros((24, 128), F32)
            for k, head in enumerate(KEY_HEAD):
                query[rows, head * 384 : (head + 1) * 384] = first[z, k].astype(F32)
                key[rows, head * 128 : (head + 1) * 128] = second[z, k, :, :128].astype(F32)
                value[rows, head * 128 : (head + 1) * 128] = second[z, k, :, 128:256].astype(F32)
                sums += second[z, k, :, 256:].astype(F32)
            small[rows] = sums
            for k in range(2):
                outs[rows, k * 384 : (k + 1) * 384] = first[z, 4 + k].astype(F32)
                outs[rows, (2 + k) * 384 : (3 + k) * 384] = second[z, 4 + k].astype(F32)

    @pl.when(core[0] == 0)
    def _():
        put(mine, other)

    @pl.when(core[0] == 1)
    def _():
        put(other, mine)

    turned = small[...].T
    router[...] = turned[:8, :192]
    ffn[...] = turned[8:9, :192]
    attn[...] = turned[9:10, :192]


def shards(
    tokens,
    segment_ids,
    routes,
    gain_attn,
    w_query,
    w_key,
    w_value,
    w_out,
    gain_ffn,
    w_router,
    w_shared_in,
    w_shared_out,
    w_expert_in,
    w_expert_out,
    cotangent,
):
    level, core, half, place = (
        lax.axis_index(a).astype(jnp.uint32) for a in ("z", "core", "yhi", "x")
    )
    rows = tokens.shape[0]
    zero = jnp.uint32(0)

    member = half * 4 + place
    key_head = jnp.where((place == 1) | (place == 2), 3 - place, place)

    tokens_x = spread_x(tokens)
    at_core = core.reshape(1).astype(jnp.int32)
    small = jnp.concatenate([gain_attn[None], gain_ffn[None], w_router.T], axis=0)
    small = jnp.pad(small, ((0, 6), (0, 448)))
    (slots,) = on_chip(
        pack_kernel, at_core, (w_query, w_key, w_value, small), (out(8, 112, 640),)
    )
    got = exchange(slots, FSDP)
    small = got[:, 96:106, :192].transpose(1, 0, 2).reshape(10, D)
    gain_one = small[:1].astype(F32)
    gain_two = small[1:2].astype(F32)
    router = small[2:]

    w_out_late, *_ = lax.optimization_barrier((w_out, *tokens_x[1:3]))
    out_mine = lax.ppermute(
        w_out_late,
        ("core", "yhi", "x"),
        [(s * 8 + b, (b % 2) * 8 + s * 4 + KEY_HEAD[b // 2]) for s in range(2) for b in range(8)],
    )

    qkv_other = swap_core(after(got, *tokens_x[3:]))
    turn, flip = level & 3, level >> 2
    first, second = core * 4 + ((place - turn) & 3), core * 4 + ((place - turn - 2) & 3)
    halves = (
        lax.dynamic_slice(w_expert_in, (zero, first, zero), (192, 1, 896)).reshape(192, 896),
        jnp.concatenate(
            [
                lax.dynamic_slice(w_expert_in, (zero, second, zero + 896), (192, 1, 128)).reshape(
                    192, 128
                ),
                lax.dynamic_slice(w_shared_in, (zero, second * 128), (192, 128)),
                lax.dynamic_slice(w_shared_in, (zero, second * 128 + FS), (192, 128)),
                lax.dynamic_slice(w_expert_out, (second, zero, zero), (1, 64, D))
                .reshape(64, 3, 512)
                .transpose(1, 0, 2)
                .reshape(192, 512),
            ],
            axis=1,
        ),
    )
    halves = after_all(halves, slots)
    halves = [
        lax.ppermute(
            part,
            ("z", *FSDP),
            [
                (z * 8 + h * 4 + x, z * 8 + (h ^ (z >> 2) ^ k) * 4 + ((x - z - 2 * k) & 3))
                for z in range(8)
                for h in range(2)
                for x in range(4)
            ],
        )
        for k, part in enumerate(halves)
    ]
    block = after(jnp.concatenate(halves, axis=1), got, *tokens_x[3:])
    blocks = lax.all_gather(block, "z")
    inputs = tokens.astype(F32)
    normed_one, kv, w_qkv = on_chip(
        keys_kernel,
        at_core,
        (*tokens_x, gain_one, got, qkv_other),
        (out(512, D), out(512, 256), out(D, 640)),
        flops=2 * 512 * D * 256,
    )
    kv_other = lax.ppermute(kv, "yhi", [(0, 1)])
    (query,) = on_chip(
        query_kernel, at_core, (normed_one, w_qkv, kv), (out(512, 384),), flops=2 * 512 * D * 384
    )
    grad_late = after(cotangent, kv)
    grad_below, grad_above = up_x(grad_late), down_x(grad_late)
    out_other = swap_core(after(out_mine, kv_other, query))
    starts = [((place + k) & 3) * 128 for k in (0, 3, 1, 2)]
    segments = [lax.dynamic_slice_in_dim(segment_ids, half * 512 + s, 128) for s in starts]
    segments += [lax.dynamic_slice_in_dim(segment_ids, s, 128) for s in starts]
    segments = jnp.concatenate(segments)[None].astype(F32)
    at_block = jnp.stack([core, half, *starts]).astype(jnp.int32)
    part = [out(size, D) for _, size in PIECES]
    attended, logs = on_chip(
        attend_kernel,
        at_block,
        (query, kv, kv_other, segments),
        (out(512, 384), out(512, 128, dtype=F32)),
        flops=2 * 512 * 384 * 2048,
        exps=3 * 512 * 1024,
    )
    hidden_part = on_chip(
        output_kernel,
        at_core,
        (attended, out_mine, out_other),
        part,
        scratch=[pltpu.VMEM((384, D), BF)],
        flops=2 * 512 * 384 * D,
    )
    far_up, far_down = after_all((grad_below[:64], grad_above[64:]), hidden_part[0])
    hidden_near = near_pieces(hidden_part, far_pieces(hidden_part))
    grad_x = (cotangent, grad_below, grad_above, up_x(far_up), down_x(far_down))
    shared_other = lax.ppermute(after(w_shared_out, attended), ("core", "yhi"), [(0, 1), (3, 2)])
    grad_own = jnp.concatenate(grad_x, axis=0)
    grad_other = swap_core(grad_own)
    above, below = hidden_near
    hidden = inputs + near_sum(hidden_part[0], up_x(above), down_x(below))

    unit_two, factor_two = normalize(hidden)
    normed_two = (unit_two * gain_two).astype(BF)
    logits = dot_rows(normed_two, router)
    chosen = jnp.sum(
        (routes[:, :, None] == jnp.arange(EXPERTS, dtype=jnp.int32)[None, None, :]).astype(F32),
        axis=1,
    )
    weighted = chosen * jnp.exp(logits)
    gates = weighted / jnp.sum(weighted, axis=-1, keepdims=True)
    packed = jnp.concatenate(
        [normed_two, *pair_of_float(gates), jnp.zeros((rows, 112), BF)], axis=1
    )
    scalars = jnp.stack([member, core * 4 + place, (core == half).astype(jnp.uint32)])
    scalars = scalars.astype(jnp.int32)
    packed = after(packed, *grad_x[3:])
    w_in, w_expert = on_chip(
        turn_kernel, scalars, (after(blocks, packed),), (out(D, 2 * FE + 256), out(FE, D))
    )
    below, above, w_in = lax.optimization_barrier((up_x(packed), down_x(packed), w_in))
    packed = (packed, below, above, up_x(below[:64]), down_x(above[64:]))
    packed = (*packed, *(swap_core(p) for p in packed))

    back_own, back_other, mixed, grad_pre, normed_all, w_down = expert_pass(
        scalars, packed, grad_own, grad_other, w_in, w_expert, w_shared_out, shared_other
    )
    back_other = swap_core(back_other)
    back_part = [plus(o, s) for o, s in zip(pieces_of(back_own), pieces_of(back_other))]
    normed_all, _, _ = lax.optimization_barrier((normed_all, back_part[3], back_part[4]))
    flat = expert_grads(normed_all, grad_pre, mixed, grad_own, grad_other)
    back_sum, flat_ffn = collect_x(back_part, flat)

    grad_gates = back_sum[:, D : D + 8] + back_sum[:, D + 8 : D + 16]
    grad_logits = (
        gates * (grad_gates - jnp.sum(gates * grad_gates, axis=-1, keepdims=True))
    ).astype(BF)
    grad_normed_two = back_sum[:, :D] + dot(grad_logits, router)
    grad_router = dot_cols(normed_two, jnp.pad(grad_logits, ((0, 0), (0, 120))))
    grad_gain_ffn = jnp.sum(grad_normed_two * unit_two, axis=0, keepdims=True)
    grad_hidden = cotangent.astype(F32) + norm_back(
        grad_normed_two, unit_two, factor_two, gain_two
    )
    grad_hidden_low = grad_hidden.astype(BF)
    hidden_low = spread_x(grad_hidden_low)
    result_part = dot(after(mixed, grad_hidden_low), w_down).astype(BF)
    hidden_low = (after(hidden_low[0], result_part), *hidden_low[1:])

    grad_low, grad_query, grad_kv, to_other = on_chip(
        attend_back_kernel,
        at_block,
        (*hidden_low, query, kv, kv_other, segments, out_mine, out_other, logs),
        (out(512, D), out(512, 384), out(512, 256, dtype=F32), out(512, 256)),
        scratch=[pltpu.VMEM((384, D), BF)],
        flops=2 * 512 * 384 * 6656,
        exps=3 * 512 * 1024,
    )
    from_other = lax.ppermute(to_other, "yhi", [(1, 0)])
    small = grad_router + jnp.pad(grad_gain_ffn.T, ((0, 0), (8, 119)))
    query_sums, outs_sums, sides = on_chip(
        early_grads_kernel,
        at_core,
        (grad_query, w_qkv, normed_one, attended, grad_low, small, gain_one.reshape(D, 1)),
        (out(8, 8, 24, 384), out(2, 8, 4, 24, 384), out(D, 128, dtype=F32)),
        flops=2 * 512 * D * 768,
    )
    keep, give, back_kv = on_chip(
        weight_grads_kernel,
        at_core,
        (
            grad_kv,
            from_other,
            w_qkv,
            normed_one,
            sides,
            query_sums,
            outs_sums,
        ),
        (out(8, 12, 24, 384), out(8, 12, 24, 384), out(512, 256)),
        flops=2 * 512 * D * 256,
    )

    (flat,) = on_chip(
        plus_kernel, at_core, (keep, swap_core(give)), (out(8, 12, 24, 384),)
    )
    flat_sent = flat
    result_other = swap_core(after(result_part[512:], flat_sent))
    flat = exchange(flat, "z")
    ffn = lax.psum_scatter(flat_ffn, "z", scatter_dimension=0, tiled=True)[0]
    ffn = after(ffn, flat_sent)
    side = ffn[..., 1792:].reshape(4, 2, 24, 128)
    main = ffn[..., :1792].reshape(2, 4, 24, 1792)
    both = [
        jnp.concatenate([m[..., :896], side[:, 0], m[..., 896:], side[:, 1]], axis=-1)
        for m in (main[0], main[1])
    ]
    keep = jnp.where(half == 0, both[0], both[1])
    away = jnp.where(half == 0, both[1], both[0])
    ffn = plus(keep, lax.ppermute(away, "yhi", [(0, 1), (1, 0)]))
    here = lax.axis_index("ylo")
    keep = jnp.where(here == 0, ffn[..., :1024], ffn[..., 1024:])
    away = jnp.where(here == 0, ffn[..., 1024:], ffn[..., :1024])
    ffn = plus(keep, lax.ppermute(away, "ylo", [(0, 1), (1, 0)]))
    to = [
        lax.dynamic_index_in_dim(ffn[..., :896], (place + k) & 3, 0, False) for k in (0, 1, 3, 2)
    ]
    across = lax.ppermute(to[3], "x", [(i, (i + 2) % 4) for i in range(4)])
    (piece,) = on_chip(
        piece_kernel,
        place.reshape(1).astype(jnp.int32),
        (to[0], up_x(to[1]), down_x(to[2]), across, ffn[..., 896:]),
        (out(4, 24, 1024),),
    )
    whole = lax.all_gather(after(piece, flat, result_other), REP).reshape(8, 2, 2, 4, 24, 1024)
    flat = jnp.sum(flat.astype(F32), axis=0).astype(BF)
    outs = lax.dynamic_update_slice(
        jnp.zeros((8, 2, 24, 384), BF), flat[8:].reshape(2, 2, 24, 384), (2 * key_head, *(jnp.uint32(0),) * 3)
    )
    flat = jnp.concatenate([flat[:8, None], outs], axis=1)
    flat = jnp.concatenate([flat, flat], axis=0)
    result_part = [
        plus(o, s)
        for o, s in zip(pieces_of(result_part[:512]), pieces_of(after(result_other, flat)))
    ]
    back_one = on_chip(
        input_back_kernel,
        at_core,
        (after(grad_query, flat), back_kv, w_qkv),
        part,
        scratch=[pltpu.VMEM((512, 640), BF)],
        flops=2 * 512 * D * 640,
    )
    got = exchange(flat, PLANE).reshape(4, 4, 3, 24, 384)
    got = jnp.sum(got.astype(F32), axis=0)
    mine = jnp.concatenate([got[:, 0], jnp.sum(got[:, 1:], axis=0)], axis=0).astype(BF)
    result = (hidden + collect_x(result_part, gate=got)).astype(BF)
    mine = spread_z(mine, level)
    above, below = after_all(near_pieces(back_one, far_pieces(back_one)), mine)
    back_near = up_x(above), down_x(below)
    sum_query, sum_key, sum_value, sum_router, sum_ffn, sum_attn, sum_out = on_chip(
        settle_kernel,
        at_core,
        (mine, swap_core(mine)),
        (
            out(192, D, dtype=F32),
            out(192, 512, dtype=F32),
            out(192, 512, dtype=F32),
            out(EXPERTS, 192, dtype=F32),
            out(1, 192, dtype=F32),
            out(1, 192, dtype=F32),
            out(192, D, dtype=F32),
        ),
        scratch=[pltpu.VMEM((256, 128), F32)],
    )

    at_half = half.reshape(1).astype(jnp.int32)
    sum_expert_in, sum_shared_in, sum_expert_out, sum_shared_out = settle_experts(
        at_half, after(whole, sum_query, result)
    )

    back_one = near_sum(back_one[0], *after_all(back_near, sum_expert_in))
    unit_own, factor_own = normalize(inputs)
    grad_input = (grad_hidden + norm_back(back_one, unit_own, factor_own, gain_one)).astype(BF)

    return (
        result,
        grad_input,
        sum_attn.reshape(192),
        sum_query,
        sum_key,
        sum_value,
        sum_out,
        sum_ffn.reshape(192),
        sum_router.T,
        sum_shared_in,
        sum_shared_out,
        sum_expert_in,
        sum_expert_out,
    )


def solution(mesh):
    fine = Mesh(mesh.devices.reshape(SIZES), AXES)
    tokens = P((*REP, *FSDP), None)
    first = P(FSDP, None)
    return jax.shard_map(
        shards,
        mesh=fine,
        in_specs=(
            tokens,
            P(REP),
            tokens,
            P(FSDP),
            first,
            first,
            first,
            first,
            P(FSDP),
            first,
            first,
            first,
            P(FSDP, None, None),
            P(None, FSDP, None),
            tokens,
        ),
        out_specs=(
            tokens,
            tokens,
            P(FSDP),
            first,
            first,
            first,
            first,
            P(FSDP),
            first,
            first,
            first,
            P(FSDP, None, None),
            P(None, FSDP, None),
        ),
        check_vma=False,
    )
```

```python
import math

import jax
import jax.numpy as jnp
from jax import lax
from jax.experimental import pallas as pl
from jax.experimental.pallas import tpu as pltpu
from jax.sharding import Mesh, PartitionSpec as P

HEADS = 12
KV_HEADS = 4
HEAD = 128
GROUP = HEADS // KV_HEADS
D = 1536
FE = 512
FS = 1024
EXPERTS = 8
EPS = 1e-05
SCALE = 1.0 / math.sqrt(HEAD)

AXES = ("z", "ylo", "core", "yhi", "x")
SIZES = (8, 2, 2, 2, 4)
REP = ("z", "ylo", "core")
FSDP = ("yhi", "x")
PLANE = ("ylo", "yhi", "x")
KEY_HEAD = (0, 2, 1, 3)
BF = jnp.bfloat16
F32 = jnp.float32


def dot(left, right):
    return jnp.dot(left, right, preferred_element_type=F32)


def dot_rows(left, right):
    return lax.dot_general(left, right, (((1,), (1,)), ((), ())), preferred_element_type=F32)


def dot_cols(left, right):
    return lax.dot_general(left, right, (((0,), (0,)), ((), ())), preferred_element_type=F32)


def exchange(blocks, axes):
    return lax.all_to_all(blocks, axes, 0, 0, tiled=True)


def up_x(rows):
    return lax.ppermute(rows, "x", [(i, (i + 1) % 4) for i in range(4)])


def down_x(rows):
    return lax.ppermute(rows, "x", [(i, (i + 3) % 4) for i in range(4)])


def spread_x(rows):
    cut = rows.shape[0] // 2
    below, above = up_x(rows), down_x(rows)
    return rows, below, above, up_x(below[:cut]), down_x(above[cut:])


def pieces_of(rows):
    return tuple(rows[at : at + size] for at, size in PIECES)


def collect_x(pieces, beside=None, gate=None):
    above, below = near_pieces(pieces, far_pieces(pieces))
    if gate is not None:
        above, below = after_all((above, below), gate)
    if beside is not None:
        above, below, beside = lax.optimization_barrier((above, below, beside))
    total = near_sum(pieces[0], up_x(above), down_x(below))
    return total if beside is None else (total, beside)


def far_pieces(pieces):
    return up_x(pieces[3]), down_x(pieces[4])


def near_pieces(pieces, far):
    _, below, above, *_ = pieces
    cut = far[0].shape[0]
    above = jnp.concatenate([plus(above[:cut], far[0]), above[cut:]], axis=0)
    below = jnp.concatenate([below[:cut], plus(below[cut:], far[1])], axis=0)
    return above, below


def near_sum(own, below, above):
    return own.astype(F32) + below.astype(F32) + above.astype(F32)


def plus(left, right):
    return (left.astype(F32) + right.astype(F32)).astype(BF)


def spread_z(rows, level):
    up = [(i, (i + 1) % 8) for i in range(8)]
    down = [(i, (i + 7) % 8) for i in range(8)]
    cut = rows.shape[0] // 2
    whole = jnp.zeros((8, *rows.shape), rows.dtype)
    rest = (jnp.uint32(0),) * (rows.ndim - 1)

    level = level.astype(jnp.int32)

    def put(whole, block, distance, start=0):
        return lax.dynamic_update_slice(
            whole,
            block[None],
            ((level + distance + 8 & 7).astype(jnp.uint32), jnp.uint32(start), *rest)
        )

    whole = put(whole, rows, 0)
    below = above = rows
    for k in (1, 2, 3):
        below, above = lax.ppermute(below, "z", up), lax.ppermute(above, "z", down)
        below, above = lax.optimization_barrier((below, above))
        whole = put(put(whole, below, -k), above, k)
    whole = put(whole, lax.ppermute(below[:cut], "z", up), 4)
    return put(whole, lax.ppermute(above[cut:], "z", down), 4, cut)


def after(value, *others):
    return lax.optimization_barrier((value, *others))[0]


def after_all(values, *others):
    return lax.optimization_barrier((*values, *others))[: len(values)]


def swap_core(rows):
    return lax.ppermute(rows, "core", [(0, 1), (1, 0)])


def pair_of_float(values):
    high = values.astype(BF)
    return high, (values - high.astype(F32)).astype(BF)


def normalize(values):
    factor = lax.rsqrt(jnp.mean(values * values, axis=-1, keepdims=True) + EPS)
    return values * factor, factor


def norm_back(grad_normed, unit, factor, gain):
    scaled = grad_normed * gain
    inner = jnp.mean(scaled * unit, axis=-1, keepdims=True)
    return factor * (scaled - unit * inner)


def silu_slope(values, sig):
    return sig * (1.0 + values * (1.0 - sig))


def expert_kernel(member, own, below, above, far_up, far_down, own_o, below_o, above_o, far_up_o,
                  far_down_o, grad_own, grad_other, blocks, shared_mine, shared_other, back_own, back_other, mixed, grad_pre, normed, w_down,
                  w_in, rows):
    step = pl.program_id(0)

    @pl.when(step == 0)
    def _():
        for b in range(8):
            flip = (b >> 2) ^ (member[0] >> 2)
            first = flip * 4 + ((b - member[0]) & 3)
            second = (1 - flip) * 4 + ((b - member[0] - 2) & 3)
            w_in[b * 192 : (b + 1) * 192, :896] = blocks[first, :, :896]
            w_in[b * 192 : (b + 1) * 192, 896:] = blocks[second, :, 896:1280]
            for k in range(3):
                w_down[b * 64 : (b + 1) * 64, k * 512 : (k + 1) * 512] = blocks[
                    second, k * 64 : (k + 1) * 64, 1280:
                ]

        @pl.when(member[2] == 0)
        def _():
            w_down[FE:] = shared_other[...]

        @pl.when(member[2] != 0)
        def _():
            w_down[FE:] = shared_mine[...]

        at = 0
        for piece in (own, below, above, far_up, far_down, own_o, below_o, above_o, far_up_o,
                      far_down_o):
            rows[at : at + piece.shape[0]] = piece[...]
            at += piece.shape[0]

    part = pl.ds(pl.multiple_of(step * 256, 256), 256)
    x = rows[part, :D]
    lane = lax.broadcasted_iota(jnp.int32, (256, 128), 1)
    expert = member[1]
    high, low = lane == expert, lane == expert + 8
    gate = jnp.sum(
        jnp.where(high | low, rows[part, D:].astype(F32), 0.0), axis=1, keepdims=True
    )
    back_down = dot_rows(jnp.where(step < 2, grad_own[...], grad_other[...]), w_down[...])
    pre = dot(x, w_in[...])
    gate_part, up_part = pre[:, :FE], pre[:, FE : 2 * FE]
    shared_gate, shared_up = pre[:, 2 * FE : 2 * FE + 128], pre[:, 2 * FE + 128 :]
    gate_sig = jax.nn.sigmoid(gate_part)
    gate_act = gate_part * gate_sig
    activ = gate_act * up_part
    shared_sig = jax.nn.sigmoid(shared_gate)
    shared_silu = shared_gate * shared_sig
    grad_mixed, grad_shared = back_down[:, :FE], back_down[:, FE:]
    grad_gate = jnp.sum(grad_mixed * activ, axis=1, keepdims=True)
    grad_activ = grad_mixed * gate
    mixed[:, :FE] = (gate * activ).astype(BF)
    mixed[:, FE:] = (shared_silu * shared_up).astype(BF)
    grad_pre[:, :FE] = (grad_activ * up_part * silu_slope(gate_part, gate_sig)).astype(BF)
    grad_pre[:, FE : 2 * FE] = (grad_activ * gate_act).astype(BF)
    grad_pre[:, 2 * FE : 2 * FE + 128] = (
        grad_shared * shared_up * silu_slope(shared_gate, shared_sig)
    ).astype(BF)
    grad_pre[:, 2 * FE + 128 :] = (grad_shared * shared_silu).astype(BF)
    normed[...] = x
    back = dot_rows(grad_pre[...], w_in[...]).astype(BF)
    top = grad_gate.astype(BF).astype(F32)
    tail = jnp.where(high, top, jnp.where(low, grad_gate - top, 0.0)).astype(BF)

    @pl.when(step < 2)
    def _():
        back_own[:, :D], back_own[:, D:] = back, tail

    @pl.when(step >= 2)
    def _():
        back_other[:, :D], back_other[:, D:] = back, tail


def lower_chunk(n):
    return pl.BlockSpec((256, n), lambda i, *_: (jnp.minimum(i, 1), 0))


def upper_chunk(n):
    return pl.BlockSpec((256, n), lambda i, *_: (jnp.maximum(i - 2, 0), 0))


def expert_pass(scalars, pieces, grad_own, grad_other, blocks, shared_mine, shared_other):
    whole = lambda a: pl.BlockSpec(a.shape, lambda i, *_, n=a.ndim: (0,) * n)
    chunk = lambda n: pl.BlockSpec((256, n), lambda i, *_: (i, 0))
    shape = lambda n, rows=1024: jax.ShapeDtypeStruct((rows, n), BF)
    return pl.pallas_call(
        expert_kernel,
        out_shape=(shape(1664, 512), shape(1664, 512), shape(640), shape(1280), shape(D), shape(D, 640)),
        grid_spec=pltpu.PrefetchScalarGridSpec(
            num_scalar_prefetch=1,
            grid=(4,),
            in_specs=[
                *(whole(p) for p in pieces),
                lower_chunk(D),
                upper_chunk(D),
                whole(blocks),
                whole(shared_mine),
                whole(shared_other),
            ],
            out_specs=(
                lower_chunk(1664),
                upper_chunk(1664),
                chunk(640),
                chunk(1280),
                chunk(D),
                pl.BlockSpec((640, D), lambda i, *_: (0, 0)),
            ),
            scratch_shapes=[
                pltpu.VMEM((D, 1280), BF),
                pltpu.VMEM((1024, 1664), BF),
            ],
        ),
        compiler_params=pltpu.CompilerParams(vmem_limit_bytes=56 << 20),
        cost_estimate=pl.CostEstimate(
            flops=2 * 1024 * D * 3200, bytes_accessed=30 << 20, transcendentals=1024 * 640
        ),
    )(scalars, *pieces, grad_own, grad_other, blocks, shared_mine, shared_other)


def expert_grad_kernel(normed, grad_pre, mixed, shared, own, other, own_cols, other_cols, out):
    into = dot_cols(normed[...], grad_pre[...])
    down = dot_cols(mixed[:512], own[...]) + dot_cols(mixed[512:], other[...])
    side = dot_cols(shared[:512], own_cols[...]) + dot_cols(shared[512:], other_cols[...])
    for b in range(2):
        for z in range(8):
            at = b * 64 + z * 8
            folded = jnp.concatenate(
                [down[at : at + 8, k * 512 : (k + 1) * 512] for k in range(3)], axis=0
            )
            mine = jnp.concatenate(
                [side[z * 16 + b * 8 : z * 16 + b * 8 + 8, k * 128 : (k + 1) * 128] for k in range(3)],
                axis=0,
            )
            out[z, b] = jnp.concatenate(
                [
                    into[b * 192 + z * 24 : b * 192 + z * 24 + 24],
                    folded,
                    mine,
                ],
                axis=1,
            ).astype(BF)


def expert_grads(normed, grad_pre, mixed, grad_own, grad_other):
    return pl.pallas_call(
        expert_grad_kernel,
        out_shape=jax.ShapeDtypeStruct((8, 8, 24, 1920), BF),
        grid=(4,),
        in_specs=[
            pl.BlockSpec((1024, 384), lambda j: (0, j)),
            pl.BlockSpec((1024, 1280), lambda j: (0, 0)),
            pl.BlockSpec((1024, 128), lambda j: (0, j)),
            pl.BlockSpec((1024, 128), lambda j: (0, 4)),
            pl.BlockSpec((512, D), lambda j: (0, 0)),
            pl.BlockSpec((512, D), lambda j: (0, 0)),
            pl.BlockSpec((512, 384), lambda j: (0, j)),
            pl.BlockSpec((512, 384), lambda j: (0, j)),
        ],
        out_specs=pl.BlockSpec((8, 2, 24, 1920), lambda j: (0, j, 0, 0)),
        compiler_params=pltpu.CompilerParams(vmem_limit_bytes=56 << 20),
        cost_estimate=pl.CostEstimate(
            flops=2 * 1024 * D * 1920, bytes_accessed=22 << 20, transcendentals=0
        ),
    )(normed, grad_pre, mixed, mixed, grad_own, grad_other, grad_own, grad_other)


def full(a):
    return pl.BlockSpec(a.shape, lambda *_, n=len(a.shape): (0,) * n)


def on_chip(kernel, scalars, args, outs, scratch=(), flops=0, exps=0):
    size = sum(math.prod(a.shape) * a.dtype.itemsize for a in (*args, *outs))
    return pl.pallas_call(
        kernel,
        out_shape=tuple(outs),
        grid_spec=pltpu.PrefetchScalarGridSpec(
            num_scalar_prefetch=1,
            grid=(1,),
            in_specs=[full(a) for a in args],
            out_specs=tuple(full(a) for a in outs),
            scratch_shapes=list(scratch),
        ),
        compiler_params=pltpu.CompilerParams(vmem_limit_bytes=56 << 20),
        cost_estimate=pl.CostEstimate(flops=flops, bytes_accessed=size, transcendentals=exps),
    )(scalars, *args)


def out(*shape, dtype=BF):
    return jax.ShapeDtypeStruct(shape, dtype)


PIECES = ((0, 128), (128, 128), (256, 128), (384, 64), (448, 64))


def pack_kernel(core, query, key, value, small, slots):
    rows = pl.ds(pl.multiple_of(core[0] * 96, 32), 96)
    for k, head in enumerate(KEY_HEAD):
        for slot in (k, k + 4):
            slots[slot, :96, :384] = query[rows, head * 384 : (head + 1) * 384]
            slots[slot, :96, 384:512] = key[rows, head * 128 : (head + 1) * 128]
            slots[slot, :96, 512:] = value[rows, head * 128 : (head + 1) * 128]
            slots[slot, 96:] = small[...]


def keys_kernel(core, own, below, above, far_up, far_down, gain, got, other, normed, kv, weight):
    for b in range(8):
        first = pl.multiple_of(b * 192 + core[0] * 96, 32)
        second = pl.multiple_of(b * 192 + (1 - core[0]) * 96, 32)
        weight[pl.ds(first, 96)] = got[b, :96]
        weight[pl.ds(second, 96)] = other[b, :96]
    for (at, size), piece in zip(PIECES, (own, below, above, far_up, far_down)):
        unit, _ = normalize(piece[...].astype(F32))
        normed[at : at + size] = (unit * gain[...]).astype(BF)
    kv[...] = dot(normed[...], weight[:, GROUP * HEAD :]).astype(BF)


def query_kernel(core, normed, weight, kv, query):
    query[...] = dot(normed[...], weight[:, : GROUP * HEAD]).astype(BF)


def mask_of(scalars, segments):
    def place_of(i):
        shift = jnp.where(i < 384, scalars[4] - 256, scalars[5] - 384)
        return i + jnp.where(i < 128, scalars[2], jnp.where(i < 256, scalars[3] - 128, shift))

    query_at = place_of(lax.broadcasted_iota(jnp.int32, (512, 1), 0))
    lane = lax.broadcasted_iota(jnp.int32, (1, 512), 1)
    own_at = place_of(lane)
    other_at = jnp.where(scalars[1] == 1, own_at - 512, 1 << 20)
    key_at = jnp.concatenate([own_at, other_at], axis=1)
    key_seg = segments[...]
    query_seg = jnp.broadcast_to(key_seg[:, :512], (8, 512)).T[:, :1]
    return (query_at == key_at) | (
        (key_at < query_at) & (query_seg == key_seg) & (key_seg != 0.0)
    )


def attend_kernel(core, query, kv, kv_other, segments, attended, logs):
    allowed = mask_of(core, segments)
    keys = jnp.concatenate([kv[:, :HEAD], kv_other[:, :HEAD]], axis=0)
    values = jnp.concatenate([kv[:, HEAD:], kv_other[:, HEAD:]], axis=0)
    lane = lax.broadcasted_iota(jnp.int32, (512, 128), 1)
    kept = jnp.zeros((512, 128), F32)
    for g in range(GROUP):
        scores = dot_rows(query[:, g * HEAD : (g + 1) * HEAD], keys) * SCALE
        scores = jnp.where(allowed, scores, -1e30)
        top = jnp.max(scores, axis=1, keepdims=True)
        expo = jnp.exp(scores - top)
        total = jnp.sum(expo, axis=1, keepdims=True)
        kept = jnp.where(lane == g, top + jnp.log(total), kept)
        attended[:, g * HEAD : (g + 1) * HEAD] = dot((expo / total).astype(BF), values).astype(BF)
    logs[...] = kept


def output_kernel(core, attended, mine, other, own, below, above, far_up, far_down, weight):
    for c in range(2):
        @pl.when(core[0] == c)
        def _():
            weight[c * 192 : (c + 1) * 192] = mine[...]
            weight[(1 - c) * 192 : (2 - c) * 192] = other[...]
    whole = dot(attended[...], weight[...]).astype(BF)
    for (at, size), piece in zip(PIECES, (own, below, above, far_up, far_down)):
        piece[...] = whole[at : at + size]


def attend_back_kernel(core, own, below, above, far_up, far_down, query, kv, kv_other, segments,
                       mine, other, logs, grad, grad_query, grad_own, grad_other, weight):
    for c in range(2):
        @pl.when(core[0] == c)
        def _():
            weight[c * 192 : (c + 1) * 192] = mine[...]
            weight[(1 - c) * 192 : (2 - c) * 192] = other[...]
    for (at, size), piece in zip(PIECES, (own, below, above, far_up, far_down)):
        grad[at : at + size] = piece[...]
    grad_att = dot_rows(grad[...], weight[...]).astype(BF)
    allowed = mask_of(core, segments)
    keys = jnp.concatenate([kv[:, :HEAD], kv_other[:, :HEAD]], axis=0)
    values = jnp.concatenate([kv[:, HEAD:], kv_other[:, HEAD:]], axis=0)
    grad_keys = jnp.zeros((1024, HEAD), F32)
    grad_values = jnp.zeros((1024, HEAD), F32)
    for g in range(GROUP):
        queries = query[:, g * HEAD : (g + 1) * HEAD]
        heads = grad_att[:, g * HEAD : (g + 1) * HEAD]
        scores = jnp.where(allowed, dot_rows(queries, keys) * SCALE, -1e30)
        probs = jnp.exp(scores - logs[:, g : g + 1])
        grad_probs = dot_rows(heads, values)
        inner = jnp.sum(probs * grad_probs, axis=1, keepdims=True)
        grad_scores = (probs * (grad_probs - inner)).astype(BF)
        grad_query[:, g * HEAD : (g + 1) * HEAD] = (dot(grad_scores, keys) * SCALE).astype(BF)
        grad_keys += dot_cols(grad_scores, queries)
        grad_values += dot_cols(probs.astype(BF), heads)
    grad_keys = grad_keys * SCALE
    grad_own[:, :HEAD] = grad_keys[:512]
    grad_own[:, HEAD:] = grad_values[:512]
    grad_other[:, :HEAD] = grad_keys[512:].astype(BF)
    grad_other[:, HEAD:] = grad_values[512:].astype(BF)


def early_grads_kernel(core, grad_query, weight, normed, attended, grad, query, outs, column):
    into = dot_cols(normed[...], grad_query[...])
    column[...] = jnp.sum(into * weight[:, : GROUP * HEAD].astype(F32), axis=1, keepdims=True)
    sums = dot_cols(attended[...], grad[...])
    for z in range(8):
        for b in range(8):
            query[z, b] = into[b * 192 + z * 24 : b * 192 + z * 24 + 24].astype(BF)
        for c in range(2):
            for j in range(2):
                for k in range(2):
                    outs[c, z, j * 2 + k] = sums[
                        j * 192 + z * 24 : j * 192 + z * 24 + 24,
                        c * 768 + k * 384 : c * 768 + (k + 1) * 384,
                    ].astype(BF)


def weight_grads_kernel(core, grad_kv, from_other, weight, normed, small, gain, column, query, outs,
                        keep, give, back_kv):
    back_kv[...] = (grad_kv[...] + from_other[...].astype(F32)).astype(BF)
    into = dot_cols(normed[...], back_kv[...])
    late = jnp.sum(into * weight[:, GROUP * HEAD :].astype(F32), axis=1, keepdims=True)
    lane = lax.broadcasted_iota(jnp.int32, (D, 128), 1)
    side = jnp.where(lane == 9, (column[...] + late) / gain[...], small[...])

    def put(first, second):
        first[:, :8] = query[...]
        first[:, 8:] = outs[0]
        second[:, 8:] = outs[1]
        for z in range(8):
            for b in range(8):
                rows = slice(b * 192 + z * 24, b * 192 + z * 24 + 24)
                second[z, b] = jnp.concatenate([into[rows], side[rows]], axis=1).astype(BF)

    @pl.when(core[0] == 0)
    def _():
        put(keep, give)

    @pl.when(core[0] == 1)
    def _():
        put(give, keep)


def input_back_kernel(core, query, kv, weight, own, below, above, far_up, far_down, both):
    both[:, : GROUP * HEAD] = query[...]
    both[:, GROUP * HEAD :] = kv[...]
    back = dot_rows(both[...], weight[...]).astype(BF)
    for (at, size), piece in zip(PIECES, (own, below, above, far_up, far_down)):
        piece[...] = back[at : at + size]


def settle_experts_kernel(half, whole, expert_in, shared_in, expert_out, shared_out):
    low = [whole[0, 0, e // 4, e % 4, :, :896].astype(F32) for e in range(8)]
    high = [whole[0, 1, e // 4, e % 4, :, :896].astype(F32) for e in range(8)]
    expert_in[:, :, :896] = jnp.transpose(jnp.stack(low), (1, 0, 2))
    expert_in[:, :, 896:] = jnp.transpose(jnp.stack([h[:, :128] for h in high]), (1, 0, 2))
    for e in range(8):
        shared_in[:, e * 128 : (e + 1) * 128] = high[e][:, 128:256]
        shared_in[:, FS + e * 128 : FS + (e + 1) * 128] = high[e][:, 256:384]
        for k in range(3):
            expert_out[e, :, k * 512 : (k + 1) * 512] = high[e][k * 8 : (k + 1) * 8, 384:]
    for y in range(2):
        for j in range(4):
            side = whole[0, y, half[0], j, :, 896:].astype(F32)
            for k in range(3):
                lanes = j * 384 + k * 128
                shared_out[y * 8 : (y + 1) * 8, lanes : lanes + 128] = side[k * 8 : (k + 1) * 8]


def settle_experts(half, whole):
    f32 = lambda *s: jax.ShapeDtypeStruct(s, F32)
    return pl.pallas_call(
        settle_experts_kernel,
        out_shape=(f32(192, EXPERTS, 1024), f32(192, 2 * FS), f32(8, 64, D), f32(128, D)),
        grid_spec=pltpu.PrefetchScalarGridSpec(
            num_scalar_prefetch=1,
            grid=(8,),
            in_specs=[pl.BlockSpec((1, 2, 2, 4, 24, 1024), lambda z, *_: (z,) + (0,) * 5)],
            out_specs=(
                pl.BlockSpec((24, EXPERTS, 1024), lambda z, *_: (z, 0, 0)),
                pl.BlockSpec((24, 2 * FS), lambda z, *_: (z, 0)),
                pl.BlockSpec((8, 8, D), lambda z, *_: (0, z, 0)),
                pl.BlockSpec((16, D), lambda z, *_: (z, 0)),
            ),
        ),
        compiler_params=pltpu.CompilerParams(vmem_limit_bytes=56 << 20),
        cost_estimate=pl.CostEstimate(flops=0, bytes_accessed=19 << 20, transcendentals=0),
    )(half, whole)


def piece_kernel(place, same, below, above, across, side, piece):
    for ref, distance in ((same, 0), (below, 3), (above, 1), (across, 2)):
        piece[lax.rem(place[0] + distance, 4), :, :896] = ref[...]
    piece[:, :, 896:] = side[...]


def settle_kernel(core, mine, other, query, key, value, router, ffn, attn, outs, small):
    small[192:] = jnp.zeros((64, 128), F32)

    def put(first, second):
        for z in range(8):
            rows = slice(z * 24, (z + 1) * 24)
            sums = jnp.zeros((24, 128), F32)
            for k, head in enumerate(KEY_HEAD):
                query[rows, head * 384 : (head + 1) * 384] = first[z, k].astype(F32)
                key[rows, head * 128 : (head + 1) * 128] = second[z, k, :, :128].astype(F32)
                value[rows, head * 128 : (head + 1) * 128] = second[z, k, :, 128:256].astype(F32)
                sums += second[z, k, :, 256:].astype(F32)
            small[rows] = sums
            for k in range(2):
                outs[rows, k * 384 : (k + 1) * 384] = first[z, 4 + k].astype(F32)
                outs[rows, (2 + k) * 384 : (3 + k) * 384] = second[z, 4 + k].astype(F32)

    @pl.when(core[0] == 0)
    def _():
        put(mine, other)

    @pl.when(core[0] == 1)
    def _():
        put(other, mine)

    turned = small[...].T
    router[...] = turned[:8, :192]
    ffn[...] = turned[8:9, :192]
    attn[...] = turned[9:10, :192]


def shards(
    tokens,
    segment_ids,
    routes,
    gain_attn,
    w_query,
    w_key,
    w_value,
    w_out,
    gain_ffn,
    w_router,
    w_shared_in,
    w_shared_out,
    w_expert_in,
    w_expert_out,
    cotangent,
):
    level, core, half, place = (
        lax.axis_index(a).astype(jnp.uint32) for a in ("z", "core", "yhi", "x")
    )
    rows = tokens.shape[0]
    zero = jnp.uint32(0)

    member = half * 4 + place
    key_head = jnp.where((place == 1) | (place == 2), 3 - place, place)

    tokens_x = spread_x(tokens)
    at_core = core.reshape(1).astype(jnp.int32)
    small = jnp.concatenate([gain_attn[None], gain_ffn[None], w_router.T], axis=0)
    small = jnp.pad(small, ((0, 6), (0, 448)))
    (slots,) = on_chip(
        pack_kernel, at_core, (w_query, w_key, w_value, small), (out(8, 112, 640),)
    )
    got = exchange(slots, FSDP)
    small = got[:, 96:106, :192].transpose(1, 0, 2).reshape(10, D)
    gain_one = small[:1].astype(F32)
    gain_two = small[1:2].astype(F32)
    router = small[2:]

    w_out_late, *_ = lax.optimization_barrier((w_out, *tokens_x[1:3]))
    out_mine = lax.ppermute(
        w_out_late,
        ("core", "yhi", "x"),
        [(s * 8 + b, (b % 2) * 8 + s * 4 + KEY_HEAD[b // 2]) for s in range(2) for b in range(8)],
    )

    qkv_other = swap_core(after(got, *tokens_x[3:]))
    turn, flip = level & 3, level >> 2
    first, second = core * 4 + ((place - turn) & 3), core * 4 + ((place - turn - 2) & 3)
    halves = (
        lax.dynamic_slice(w_expert_in, (zero, first, zero), (192, 1, 896)).reshape(192, 896),
        jnp.concatenate(
            [
                lax.dynamic_slice(w_expert_in, (zero, second, zero + 896), (192, 1, 128)).reshape(
                    192, 128
                ),
                lax.dynamic_slice(w_shared_in, (zero, second * 128), (192, 128)),
                lax.dynamic_slice(w_shared_in, (zero, second * 128 + FS), (192, 128)),
                lax.dynamic_slice(w_expert_out, (second, zero, zero), (1, 64, D))
                .reshape(64, 3, 512)
                .transpose(1, 0, 2)
                .reshape(192, 512),
            ],
            axis=1,
        ),
    )
    halves = after_all(halves, slots)
    halves = [
        lax.ppermute(
            part,
            ("z", *FSDP),
            [
                (z * 8 + h * 4 + x, z * 8 + (h ^ (z >> 2) ^ k) * 4 + ((x - z - 2 * k) & 3))
                for z in range(8)
                for h in range(2)
                for x in range(4)
            ],
        )
        for k, part in enumerate(halves)
    ]
    block = after(jnp.concatenate(halves, axis=1), got, *tokens_x[3:])
    blocks = lax.all_gather(block, "z")
    inputs = tokens.astype(F32)
    normed_one, kv, w_qkv = on_chip(
        keys_kernel,
        at_core,
        (*tokens_x, gain_one, got, qkv_other),
        (out(512, D), out(512, 256), out(D, 640)),
        flops=2 * 512 * D * 256,
    )
    kv_other = lax.ppermute(kv, "yhi", [(0, 1)])
    (query,) = on_chip(
        query_kernel, at_core, (normed_one, w_qkv, kv), (out(512, 384),), flops=2 * 512 * D * 384
    )
    grad_late = after(cotangent, kv)
    grad_below, grad_above = up_x(grad_late), down_x(grad_late)
    out_other = swap_core(after(out_mine, kv_other, query))
    starts = [((place + k) & 3) * 128 for k in (0, 3, 1, 2)]
    segments = [lax.dynamic_slice_in_dim(segment_ids, half * 512 + s, 128) for s in starts]
    segments += [lax.dynamic_slice_in_dim(segment_ids, s, 128) for s in starts]
    segments = jnp.concatenate(segments)[None].astype(F32)
    at_block = jnp.stack([core, half, *starts]).astype(jnp.int32)
    part = [out(size, D) for _, size in PIECES]
    attended, logs = on_chip(
        attend_kernel,
        at_block,
        (query, kv, kv_other, segments),
        (out(512, 384), out(512, 128, dtype=F32)),
        flops=2 * 512 * 384 * 2048,
        exps=3 * 512 * 1024,
    )
    hidden_part = on_chip(
        output_kernel,
        at_core,
        (attended, out_mine, out_other),
        part,
        scratch=[pltpu.VMEM((384, D), BF)],
        flops=2 * 512 * 384 * D,
    )
    far_up, far_down = after_all((grad_below[:64], grad_above[64:]), hidden_part[0])
    hidden_near = near_pieces(hidden_part, far_pieces(hidden_part))
    grad_x = (cotangent, grad_below, grad_above, up_x(far_up), down_x(far_down))
    shared_other = lax.ppermute(after(w_shared_out, attended), ("core", "yhi"), [(0, 1), (3, 2)])
    grad_own = jnp.concatenate(grad_x, axis=0)
    grad_other = swap_core(grad_own)
    above, below = hidden_near
    hidden = inputs + near_sum(hidden_part[0], up_x(above), down_x(below))

    unit_two, factor_two = normalize(hidden)
    normed_two = (unit_two * gain_two).astype(BF)
    logits = dot_rows(normed_two, router)
    chosen = jnp.sum(
        (routes[:, :, None] == jnp.arange(EXPERTS, dtype=jnp.int32)[None, None, :]).astype(F32),
        axis=1,
    )
    weighted = chosen * jnp.exp(logits)
    gates = weighted / jnp.sum(weighted, axis=-1, keepdims=True)
    packed = jnp.concatenate(
        [normed_two, *pair_of_float(gates), jnp.zeros((rows, 112), BF)], axis=1
    )
    packed = spread_x(after(packed, *grad_x[3:]))
    packed = (*packed, *(swap_core(p) for p in packed))

    scalars = jnp.stack([member, core * 4 + place, (core == half).astype(jnp.uint32)])
    back_own, back_other, mixed, grad_pre, normed_all, w_down = expert_pass(
        scalars.astype(jnp.int32), packed, grad_own, grad_other, blocks, w_shared_out, shared_other
    )
    back_other = swap_core(back_other)
    back_part = [plus(o, s) for o, s in zip(pieces_of(back_own), pieces_of(back_other))]
    normed_all, _, _ = lax.optimization_barrier((normed_all, back_part[3], back_part[4]))
    flat = expert_grads(normed_all, grad_pre, mixed, grad_own, grad_other)
    back_sum, flat_ffn = collect_x(back_part, flat)

    grad_gates = back_sum[:, D : D + 8] + back_sum[:, D + 8 : D + 16]
    grad_logits = (
        gates * (grad_gates - jnp.sum(gates * grad_gates, axis=-1, keepdims=True))
    ).astype(BF)
    grad_normed_two = back_sum[:, :D] + dot(grad_logits, router)
    grad_router = dot_cols(normed_two, jnp.pad(grad_logits, ((0, 0), (0, 120))))
    grad_gain_ffn = jnp.sum(grad_normed_two * unit_two, axis=0, keepdims=True)
    grad_hidden = cotangent.astype(F32) + norm_back(
        grad_normed_two, unit_two, factor_two, gain_two
    )
    grad_hidden_low = grad_hidden.astype(BF)
    hidden_low = spread_x(grad_hidden_low)
    result_part = dot(after(mixed, grad_hidden_low), w_down).astype(BF)
    hidden_low = (after(hidden_low[0], result_part), *hidden_low[1:])

    grad_low, grad_query, grad_kv, to_other = on_chip(
        attend_back_kernel,
        at_block,
        (*hidden_low, query, kv, kv_other, segments, out_mine, out_other, logs),
        (out(512, D), out(512, 384), out(512, 256, dtype=F32), out(512, 256)),
        scratch=[pltpu.VMEM((384, D), BF)],
        flops=2 * 512 * 384 * 6656,
        exps=3 * 512 * 1024,
    )
    from_other = lax.ppermute(to_other, "yhi", [(1, 0)])
    small = grad_router + jnp.pad(grad_gain_ffn.T, ((0, 0), (8, 119)))
    query_sums, outs_sums, column = on_chip(
        early_grads_kernel,
        at_core,
        (grad_query, w_qkv, normed_one, attended, grad_low),
        (out(8, 8, 24, 384), out(2, 8, 4, 24, 384), out(D, 1, dtype=F32)),
        flops=2 * 512 * D * 768,
    )
    keep, give, back_kv = on_chip(
        weight_grads_kernel,
        at_core,
        (
            grad_kv,
            from_other,
            w_qkv,
            normed_one,
            small,
            gain_one.reshape(D, 1),
            column,
            query_sums,
            outs_sums,
        ),
        (out(8, 12, 24, 384), out(8, 12, 24, 384), out(512, 256)),
        flops=2 * 512 * D * 256,
    )

    flat = plus(keep, swap_core(give))
    flat_sent = flat
    result_other = swap_core(after(result_part[512:], flat_sent))
    flat = exchange(flat, "z")
    ffn = lax.psum_scatter(flat_ffn, "z", scatter_dimension=0, tiled=True)[0]
    ffn = after(ffn, flat_sent)
    side = ffn[..., 1792:].reshape(4, 2, 24, 128)
    main = ffn[..., :1792].reshape(2, 4, 24, 1792)
    both = [
        jnp.concatenate([m[..., :896], side[:, 0], m[..., 896:], side[:, 1]], axis=-1)
        for m in (main[0], main[1])
    ]
    keep = jnp.where(half == 0, both[0], both[1])
    away = jnp.where(half == 0, both[1], both[0])
    came = lax.ppermute(away, "yhi", [(0, 1), (1, 0)])
    back_one = on_chip(
        input_back_kernel,
        at_core,
        (after(grad_query, flat_sent), back_kv, w_qkv),
        part,
        scratch=[pltpu.VMEM((512, 640), BF)],
        flops=2 * 512 * D * 640,
    )
    ffn = plus(after(keep, back_one[0]), came)
    here = lax.axis_index("ylo")
    keep = jnp.where(here == 0, ffn[..., :1024], ffn[..., 1024:])
    away = jnp.where(here == 0, ffn[..., 1024:], ffn[..., :1024])
    ffn = plus(keep, lax.ppermute(away, "ylo", [(0, 1), (1, 0)]))
    to = [
        lax.dynamic_index_in_dim(ffn[..., :896], (place + k) & 3, 0, False) for k in (0, 1, 3, 2)
    ]
    across = lax.ppermute(to[3], "x", [(i, (i + 2) % 4) for i in range(4)])
    (piece,) = on_chip(
        piece_kernel,
        place.reshape(1).astype(jnp.int32),
        (to[0], up_x(to[1]), down_x(to[2]), across, ffn[..., 896:]),
        (out(4, 24, 1024),),
    )
    whole = lax.all_gather(after(piece, flat, result_other), REP).reshape(8, 2, 2, 4, 24, 1024)
    flat = jnp.sum(flat.astype(F32), axis=0).astype(BF)
    outs = lax.dynamic_update_slice(
        jnp.zeros((8, 2, 24, 384), BF), flat[8:].reshape(2, 2, 24, 384), (2 * key_head, *(jnp.uint32(0),) * 3)
    )
    flat = jnp.concatenate([flat[:8, None], outs], axis=1)
    flat = jnp.concatenate([flat, flat], axis=0)
    back_one = (*back_one[:3], *after_all(back_one[3:], flat))
    result_part = [
        plus(o, s)
        for o, s in zip(pieces_of(result_part[:512]), pieces_of(after(result_other, flat)))
    ]
    got = exchange(flat, PLANE).reshape(4, 4, 3, 24, 384)
    got = jnp.sum(got.astype(F32), axis=0)
    mine = jnp.concatenate([got[:, 0], jnp.sum(got[:, 1:], axis=0)], axis=0).astype(BF)
    result = (hidden + collect_x(result_part, gate=got)).astype(BF)
    mine = spread_z(mine, level)
    above, below = after_all(near_pieces(back_one, far_pieces(back_one)), mine)
    back_near = up_x(above), down_x(below)
    sum_query, sum_key, sum_value, sum_router, sum_ffn, sum_attn, sum_out = on_chip(
        settle_kernel,
        at_core,
        (mine, swap_core(mine)),
        (
            out(192, D, dtype=F32),
            out(192, 512, dtype=F32),
            out(192, 512, dtype=F32),
            out(EXPERTS, 192, dtype=F32),
            out(1, 192, dtype=F32),
            out(1, 192, dtype=F32),
            out(192, D, dtype=F32),
        ),
        scratch=[pltpu.VMEM((256, 128), F32)],
    )

    at_half = half.reshape(1).astype(jnp.int32)
    sum_expert_in, sum_shared_in, sum_expert_out, sum_shared_out = settle_experts(
        at_half, after(whole, sum_query, result)
    )

    back_one = near_sum(back_one[0], *after_all(back_near, sum_expert_in))
    unit_own, factor_own = normalize(inputs)
    grad_input = (grad_hidden + norm_back(back_one, unit_own, factor_own, gain_one)).astype(BF)

    return (
        result,
        grad_input,
        sum_attn.reshape(192),
        sum_query,
        sum_key,
        sum_value,
        sum_out,
        sum_ffn.reshape(192),
        sum_router.T,
        sum_shared_in,
        sum_shared_out,
        sum_expert_in,
        sum_expert_out,
    )


def solution(mesh):
    fine = Mesh(mesh.devices.reshape(SIZES), AXES)
    tokens = P((*REP, *FSDP), None)
    first = P(FSDP, None)
    return jax.shard_map(
        shards,
        mesh=fine,
        in_specs=(
            tokens,
            P(REP),
            tokens,
            P(FSDP),
            first,
            first,
            first,
            first,
            P(FSDP),
            first,
            first,
            first,
            P(FSDP, None, None),
            P(None, FSDP, None),
            tokens,
        ),
        out_specs=(
            tokens,
            tokens,
            P(FSDP),
            first,
            first,
            first,
            first,
            P(FSDP),
            first,
            first,
            first,
            P(FSDP, None, None),
            P(None, FSDP, None),
        ),
        check_vma=False,
    )
```
